256 devices in a mesh: group: 4 (over y), dom: 64 (over z, x, core).
Axes of the slice: x: 4, y: 4, z: 8, core: 2. Of those that a mesh axis runs over, the one named last changes fastest.
Arguments:
- feats: bfloat16 [65536, 512], P(('group', 'dom')), may hold values from -6 to 6
- neigh: bfloat16 [65536, 512], P(('group', 'dom')), may hold values from -6 to 6
- pre_act: bfloat16 [65536, 512], P(('group', 'dom')), may hold values from -6 to 6
- cotan: bfloat16 [65536, 512], P(('group', 'dom')), may hold values from -6 to 6
- w_self: bfloat16 [512, 512], replicated, may hold values from -0.25 to 0.25
- w_neigh: bfloat16 [512, 512], replicated, may hold values from -0.25 to 0.25
- send_list: int32 [4, 64, 64], P('group', 'dom'), may hold values from 0 to 1
- send_live: int32 [4, 64, 64], P('group', 'dom'), may hold values 0 or 1
- cross_list: int32 [4, 64, 4, 2], P('group', 'dom'), may hold values from 0 to 1
- cross_live: int32 [4, 64, 4, 2], P('group', 'dom'), may hold values 0 or 1
- home_tiles: bfloat16 [4, 64, 16, 128, 128], P('group', 'dom'), may hold values from 0 to 0.039794922
- home_target: int32 [4, 64, 16], P('group', 'dom'), may hold values from 0 to 1
- home_source: int32 [4, 64, 16], P('group', 'dom'), may hold values from 0 to 73
- far_tiles: bfloat16 [4, 64, 16, 128, 128], P('group', 'dom'), may hold values from 0 to 0.039794922
- far_target: int32 [4, 64, 16], P('group', 'dom'), may hold values from 2 to 73
- far_source: int32 [4, 64, 16], P('group', 'dom'), may hold values from 0 to 73
- far_count: int32 [4, 64], P('group', 'dom'), may hold values from 1 to 16, as said below
Outputs:
- grad_input: bfloat16 [65536, 512], P(('group', 'dom'))
- grad_wself: float32 [512, 512], replicated
- grad_wneigh: float32 [512, 512], replicated
- grad_bias: float32 [512], replicated
The draws below stay inside these ranges and needn't reach their ends.
Inputs may be any that keep to these rules, and one draw needn't show every extreme that they name: `far_count`: some partition uses all 16 far tiles.
All inputs are finite; a program needn't handle non-finite values. No bound on the sum of `send_live` or of `cross_live` on one device may be relied on, other than what follows from the above.
Results may differ from the reference program's by a relative error of at most 0.0045.
Values may be sent and summed in bfloat16 or wider, within the bound.
No kernel may reach another device: no remote copies, remote signals or barrier semaphores. Data moves between devices by JAX's collectives and lax.ppermute only.
A program may use at most 128 MiB of HBM per device.

```python
import jax
import jax.numpy as jnp
from jax import lax

D = 512
BLOCK = 128
NB = 2
XG = 2
NH = 16
NF = 16
SPACE = 74
ROWS_ALL = 65536
N_GROUP = 4
N_DOM = 64


def draw_far_count(key, part):
    key = jax.random.fold_in(key, 7)
    key_counts, key_pick = jax.random.split(key)
    counts = jax.random.randint(key_counts, (N_GROUP * N_DOM,), 1, NF + 1)
    chosen = jax.random.randint(key_pick, (), 0, N_GROUP * N_DOM)
    places = jnp.arange(N_GROUP * N_DOM)
    counts = jnp.where(places == chosen, NF, counts)
    return counts.reshape(N_GROUP, N_DOM).astype(jnp.int32)


def touch_ends(drawn, key, low, top_value):
    longest = drawn.shape.index(max(drawn.shape))
    spots = []
    for shift in (0, 1):
        where = [jax.random.randint(jax.random.fold_in(key, axis), (), 0, length) for axis, length in enumerate(drawn.shape)]
        where[longest] = (where[longest] + shift) % drawn.shape[longest]
        spots.append(tuple(where))
    return drawn.at[spots[0]].set(low).at[spots[1]].set(top_value)


def levels(key, extent, shards, low, high):
    factor_of = 1.0
    for dim, shards_of in shards:
        draws = jax.random.uniform(jax.random.fold_in(jax.random.fold_in(key, 6), dim), (shards_of,), jnp.float32, low / len(shards), high / len(shards))
        factor_of = factor_of * jnp.repeat(jnp.exp(draws), extent[dim] // shards_of).reshape((-1,) + (1,) * (len(extent) - 1 - dim))
    return factor_of


def scatter_about(own_key, shape, scale, reach, cuts=(), held_as=jnp.bfloat16):
    values = scale * jax.random.normal(own_key, shape, jnp.float32)
    if cuts:
        values = values * levels(own_key, shape, cuts, -0.22, 0.18)
    return jnp.clip(values, -reach, reach).astype(held_as)


def setup_inputs(seed: int = 0) -> dict:
    keys = jax.random.split(jax.random.key(seed), 18)
    feats = scatter_about(keys[0], (ROWS_ALL, D), 1.0, 6.0, ((0, 256),))
    neigh = scatter_about(keys[1], (ROWS_ALL, D), 1.0, 6.0, ((0, 256),))
    pre_act = scatter_about(keys[2], (ROWS_ALL, D), 1.0, 6.0, ((0, 256),))
    cotan = scatter_about(keys[3], (ROWS_ALL, D), 1.0, 6.0, ((0, 256),))
    w_self = scatter_about(keys[4], (D, D), D ** -0.5, 0.25)
    w_neigh = scatter_about(keys[5], (D, D), D ** -0.5, 0.25)
    send_list = touch_ends(jax.random.randint(keys[6], (N_GROUP, N_DOM, N_DOM), 0, NB), jax.random.fold_in(keys[6], 1), 0, NB - 1).astype(jnp.int32)
    send_live = touch_ends((jax.random.randint(keys[7], (N_GROUP, N_DOM, N_DOM), 0, 8) < 7).astype(jnp.int32), jax.random.fold_in(keys[7], 1), 0, 1)
    cross_list = touch_ends(jax.random.randint(keys[8], (N_GROUP, N_DOM, N_GROUP, XG), 0, NB), jax.random.fold_in(keys[8], 1), 0, NB - 1).astype(jnp.int32)
    cross_live = touch_ends((jax.random.randint(keys[9], (N_GROUP, N_DOM, N_GROUP, XG), 0, 2) < 1).astype(jnp.int32), jax.random.fold_in(keys[9], 1), 0, 1)
    home_tiles = jnp.clip(0.039794922 * jax.random.uniform(keys[10], (N_GROUP, N_DOM, NH, BLOCK, BLOCK), jnp.float32) ** levels(keys[10], (N_GROUP, N_DOM, NH, BLOCK, BLOCK), ((0, 4), (1, 64)), -0.2, 0.2), 0.0, 0.039794922).astype(jnp.bfloat16)
    home_target = touch_ends(jax.random.randint(keys[11], (N_GROUP, N_DOM, NH), 0, NB), jax.random.fold_in(keys[11], 1), 0, NB - 1).astype(jnp.int32)
    home_source = touch_ends(jax.random.randint(keys[12], (N_GROUP, N_DOM, NH), 0, SPACE), jax.random.fold_in(keys[12], 1), 0, SPACE - 1).astype(jnp.int32)
    far_tiles = jnp.clip(0.039794922 * jax.random.uniform(keys[13], (N_GROUP, N_DOM, NF, BLOCK, BLOCK), jnp.float32) ** levels(keys[13], (N_GROUP, N_DOM, NF, BLOCK, BLOCK), ((0, 4), (1, 64)), -0.2, 0.2), 0.0, 0.039794922).astype(jnp.bfloat16)
    far_target = touch_ends(jax.random.randint(keys[14], (N_GROUP, N_DOM, NF), NB, SPACE), jax.random.fold_in(keys[14], 1), NB, SPACE - 1).astype(jnp.int32)
    far_source = touch_ends(jax.random.randint(keys[15], (N_GROUP, N_DOM, NF), 0, SPACE), jax.random.fold_in(keys[15], 1), 0, SPACE - 1).astype(jnp.int32)
    far_count = draw_far_count(jax.random.fold_in(keys[17], 71), 0)
    return {"feats": feats, "neigh": neigh, "pre_act": pre_act, "cotan": cotan, "w_self": w_self, "w_neigh": w_neigh, "send_list": send_list, "send_live": send_live, "cross_list": cross_list, "cross_live": cross_live, "home_tiles": home_tiles, "home_target": home_target, "home_source": home_source, "far_tiles": far_tiles, "far_target": far_target, "far_source": far_source, "far_count": far_count}


def tile_terms(tiles, targets, sources, block_space, keep):
    picked = block_space[targets].astype(jnp.float32)
    contrib = jnp.einsum('tij,tid->tjd', tiles.astype(jnp.float32), picked) * keep[:, None, None]
    empty = jnp.zeros((SPACE, BLOCK, D), jnp.float32)
    return empty.at[sources].add(contrib)


def reference(feats, neigh, pre_act, cotan, w_self, w_neigh, send_list, send_live, cross_list, cross_live, home_tiles, home_target, home_source, far_tiles, far_target, far_source, far_count):
    grad_pre = jnp.where(pre_act > 0, cotan, jnp.zeros_like(cotan))
    grad_wself = jnp.dot(feats.T, grad_pre, preferred_element_type=jnp.float32)
    grad_wneigh = jnp.dot(neigh.T, grad_pre, preferred_element_type=jnp.float32)
    grad_bias = jnp.sum(grad_pre.astype(jnp.float32), axis=0)
    self_grad = jnp.dot(grad_pre, w_self.T, preferred_element_type=jnp.float32)
    agg_grad = jnp.dot(grad_pre, w_neigh.T, preferred_element_type=jnp.float32).astype(jnp.bfloat16)
    agg_grad = agg_grad.reshape(N_GROUP, N_DOM, NB, BLOCK, D)
    dom_index = jnp.arange(N_DOM, dtype=jnp.int32)
    group_index = jnp.arange(N_GROUP, dtype=jnp.int32)[:, None]
    far_index = jnp.arange(NF, dtype=jnp.int32)

    def device_step(accum, device):
        group_at = device // N_DOM
        dom_at = device % N_DOM
        dom_keep = send_live[group_at, :, dom_at].astype(jnp.bfloat16)[:, None, None]
        dom_slots = agg_grad[group_at, dom_index, send_list[group_at, :, dom_at]] * dom_keep
        cross_rows = cross_list[:, dom_at, group_at, :]
        cross_keep = cross_live[:, dom_at, group_at, :].astype(jnp.bfloat16)[:, :, None, None]
        cross_slots = (agg_grad[group_index, dom_at, cross_rows] * cross_keep).reshape(N_GROUP * XG, BLOCK, D)
        master_blocks = agg_grad[group_at, dom_at]
        block_space = jnp.concatenate([master_blocks, dom_slots, cross_slots], axis=0)
        home_keep = jnp.ones((NH,), jnp.float32)
        partials = tile_terms(home_tiles[group_at, dom_at], home_target[group_at, dom_at], home_source[group_at, dom_at], block_space, home_keep)
        far_keep = (far_index < far_count[group_at, dom_at]).astype(jnp.float32)
        partials = partials + tile_terms(far_tiles[group_at, dom_at], far_target[group_at, dom_at], far_source[group_at, dom_at], block_space, far_keep)
        accum = accum.at[group_at, dom_at].add(partials[:NB])
        rounded = lax.optimization_barrier(partials[NB:].astype(jnp.bfloat16)).astype(jnp.float32)
        dom_back = rounded[:N_DOM] * dom_keep.astype(jnp.float32)
        accum = accum.at[group_at, dom_index, send_list[group_at, :, dom_at]].add(dom_back)
        cross_back = rounded[N_DOM:].reshape(N_GROUP, XG, BLOCK, D) * cross_keep.astype(jnp.float32)
        accum = accum.at[group_index, dom_at, cross_rows].add(cross_back)
        return accum, None

    start = self_grad.reshape(N_GROUP, N_DOM, NB, BLOCK, D)
    devices = jnp.arange(N_GROUP * N_DOM, dtype=jnp.int32)
    accum, unused = lax.scan(device_step, start, devices)
    grad_input = accum.reshape(ROWS_ALL, D).astype(jnp.bfloat16)
    return grad_input, grad_wself, grad_wneigh, grad_bias
```

```python
import functools

import jax
import jax.numpy as jnp
from jax import lax
from jax.experimental import pallas as pl
from jax.experimental.pallas import tpu as pltpu
from jax.sharding import Mesh
from jax.sharding import PartitionSpec as P

AXES = ("group", "z", "x", "core")
DOM = ("z", "x", "core")
NY, NZ, NX = 4, 8, 4
BLK, HALF = 128, 256
NT = 16
bf16, f32, i32 = jnp.bfloat16, jnp.float32, jnp.int32

SEND, CROSS, HT, HS, FT, FS, FC, ROW = 0, 64, 72, 88, 104, 120, 136, 144
OFF_B, OFF_Y, NP = 64, 128, 140

A_PARTS = ((0, 16), (16, 16), (32, 8), (40, 8), (48, 16))
B_PARTS = tuple(
    (OFF_B + s, n) for s, n in ((0, 8), (8, 8), (16, 8), (24, 8), (32, 4), (36, 4), (40, 8), (48, 8), (56, 8))
)
Y_PARTS = tuple((OFF_Y + 4 * d, 4) for d in range(3))
PARTS = A_PARTS + B_PARTS + Y_PARTS


def rot(n, k):
    return [(i, (i + k) % n) for i in range(n)]


def shift(value, axis, k):
    n = {"group": NY, "z": NZ, "x": NX, "core": 2}[axis]
    return lax.ppermute(value, axis, rot(n, k))


def place_of(tab, r, source):
    base = r * ROW
    core, z, x, y = (tab[2 * ROW + j] for j in range(4))
    q = jnp.clip(source - 2, 0, 63)
    v = jnp.clip(source - 66, 0, 7)
    code = jnp.where(source < 66, tab[base + SEND + q], tab[base + CROSS + v])
    k = code & 1
    same = (q & 1) ^ core
    dz = ((q >> 3) - z) & 7
    dx = (((q >> 1) & 3) - x) & 3
    dom = jnp.where(same == 0, (dx * 8 + dz) * 2 + k, OFF_B + (dz * 4 + dx) * 2 + k)
    dy = ((v >> 1) - y) & 3
    own = jnp.where(r == 0, 0, OFF_B)
    cross = jnp.where(dy == 0, own + k, OFF_Y + (dy - 1) * 4 + r * 2 + k)
    place = jnp.where(source < 2, own + source, jnp.where(source < 66, dom, cross))
    return place, jnp.logical_or(source < 2, code >= 2)


def tile_product(tile, block):
    return lax.dot_general(tile, block, (((0,), (0,)), ((), ())), preferred_element_type=f32)


def home_kernel(tab, tiles_own, tiles_sib, agg_own, agg_sib, out):
    @pl.loop(0, NP)
    def _(b):
        out[b] = jnp.zeros((BLK, HALF), bf16)

    for r, (tiles, agg) in enumerate(((tiles_own, agg_own), (tiles_sib, agg_sib))):

        @pl.loop(0, NT)
        def _(t, r=r, tiles=tiles, agg=agg):
            place, live = place_of(tab, r, tab[r * ROW + HS + t])

            @pl.when(live)
            def _():
                term = tile_product(tiles[t], agg[tab[r * ROW + HT + t]])
                out[place] = (out[place].astype(f32) + term).astype(bf16)


def far_slot(tab, r, t):
    base = r * ROW
    u = tab[base + FT + t]
    q = jnp.clip(u - 2, 0, 63)
    v = jnp.clip(u - 66, 0, 7)
    is_dom = u < 66
    code = jnp.where(is_dom, tab[base + SEND + q], tab[base + CROSS + v])
    k = code & 1
    core, y = tab[2 * ROW], tab[2 * ROW + 3]
    dom = (q >> 1) * 4 + ((q & 1) ^ core) * 2 + k
    cross = ((y - (v >> 1)) & 3) * 4 + r * 2 + k
    place, source_live = place_of(tab, r, tab[base + FS + t])
    live = jnp.logical_and(jnp.logical_and(t < tab[base + FC], code >= 2), source_live)
    return live, is_dom, dom, cross, place


def far_kernel(tab, tiles_own, tiles_sib, base_acc, gathered, crossed, *rest):
    outs, (acc, blocks, sems, acc_sem, out_sems) = rest[: len(PARTS)], rest[len(PARTS) :]
    load = pltpu.make_async_copy(base_acc, acc, acc_sem)
    load.start()
    for r in range(2):

        @pl.loop(0, NT)
        def _(t, r=r):
            live, is_dom, dom, cross, _ = far_slot(tab, r, t)
            slot = r * NT + t

            @pl.when(jnp.logical_and(live, is_dom))
            def _():
                pltpu.make_async_copy(gathered.at[dom], blocks.at[slot], sems.at[slot]).start()

            @pl.when(jnp.logical_and(live, jnp.logical_not(is_dom)))
            def _():
                pltpu.make_async_copy(crossed.at[cross], blocks.at[slot], sems.at[slot]).start()

    load.wait()
    for r, tiles in enumerate((tiles_own, tiles_sib)):

        @pl.loop(0, NT)
        def _(t, r=r, tiles=tiles):
            live, _, _, _, place = far_slot(tab, r, t)
            slot = r * NT + t

            @pl.when(live)
            def _():
                pltpu.make_async_copy(crossed.at[0], blocks.at[slot], sems.at[slot]).wait()
                term = tile_product(tiles[t], blocks[slot])
                acc[place] = (acc[place].astype(f32) + term).astype(bf16)

    copies = [
        pltpu.make_async_copy(acc.at[pl.ds(s, n)], out, out_sems.at[j])
        for j, ((s, n), out) in enumerate(zip(PARTS, outs))
    ]
    for copy in copies:
        copy.start()
    for copy in copies:
        copy.wait()


VMEM = pl.BlockSpec(memory_space=pltpu.VMEM)
SMEM = pl.BlockSpec(memory_space=pltpu.SMEM)
ANY = pl.BlockSpec(memory_space=pl.ANY)


def home_partials(tab, tiles_own, tiles_sib, agg_own, agg_sib):
    return pl.pallas_call(
        home_kernel,
        out_shape=jax.ShapeDtypeStruct((NP, BLK, HALF), bf16),
        in_specs=[SMEM, VMEM, VMEM, VMEM, VMEM],
        out_specs=VMEM,
        compiler_params=pltpu.CompilerParams(vmem_limit_bytes=24 * 2**20),
    )(tab, tiles_own, tiles_sib, agg_own, agg_sib)


def far_partials(tab, tiles_own, tiles_sib, base_acc, gathered, crossed):
    return pl.pallas_call(
        far_kernel,
        out_shape=[jax.ShapeDtypeStruct((n, BLK, HALF), bf16) for _, n in PARTS],
        in_specs=[SMEM, VMEM, VMEM, ANY, ANY, ANY],
        out_specs=[ANY] * len(PARTS),
        scratch_shapes=[
            pltpu.VMEM((NP, BLK, HALF), bf16),
            pltpu.VMEM((2 * NT, BLK, HALF), bf16),
            pltpu.SemaphoreType.DMA((2 * NT,)),
            pltpu.SemaphoreType.DMA,
            pltpu.SemaphoreType.DMA((len(PARTS),)),
        ],
        compiler_params=pltpu.CompilerParams(vmem_limit_bytes=24 * 2**20),
    )(tab, tiles_own, tiles_sib, base_acc, gathered, crossed)


def add(*terms):
    total = terms[0].astype(f32)
    for term in terms[1:]:
        total = total + term.astype(f32)
    return total


def return_a(a0, a1, a2h, a2t, a3):
    first_p, first_m = shift(a2h, "x", 1), shift(a2t, "x", -1)
    s1 = jnp.concatenate([add(a1[:8], first_p).astype(bf16), a1[8:]])
    s3 = jnp.concatenate([a3[:8], add(a3[8:], first_m).astype(bf16)])
    t1, t3 = shift(s1, "x", 1), shift(s3, "x", -1)

    def part(dz):
        rows = slice(2 * dz, 2 * dz + 2)
        return add(a0[rows], t1[rows], t3[rows])

    far = part(4).astype(bf16)
    up, down = shift(far[:1], "z", 1), shift(far[1:], "z", -1)
    near = part(3), part(5)
    up = jnp.concatenate([near[0][:1] + up, near[0][1:]]).astype(bf16)
    down = jnp.concatenate([near[1][:1], near[1][1:] + down]).astype(bf16)
    for dz in (2, 1):
        up, down = shift(up, "z", 1), shift(down, "z", -1)
        up, down = add(part(dz), up).astype(bf16), add(part(8 - dz), down).astype(bf16)
    up, down = shift(up, "z", 1), shift(down, "z", -1)
    return add(part(0), up, down)


def return_b(b0, b1, b2, b3, b4h, b4t, b5, b6, b7):
    up, down = shift(b4h, "z", 1), shift(b4t, "z", -1)
    up = jnp.concatenate([add(b3[:4], up).astype(bf16), b3[4:]])
    down = jnp.concatenate([b5[:4], add(b5[4:], down).astype(bf16)])
    for plus, minus in ((b2, b6), (b1, b7)):
        up, down = shift(up, "z", 1), shift(down, "z", -1)
        up, down = add(plus, up).astype(bf16), add(minus, down).astype(bf16)
    up, down = shift(up, "z", 1), shift(down, "z", -1)

    def part(dx):
        rows = slice(2 * dx, 2 * dx + 2)
        return add(b0[rows], up[rows], down[rows])

    far = part(2).astype(bf16)
    right, left = shift(far[:1], "x", 1), shift(far[1:], "x", -1)
    near = part(1), part(3)
    right_sum = jnp.concatenate([near[0][:1] + right, near[0][1:]]).astype(bf16)
    left_sum = jnp.concatenate([near[1][:1], near[1][1:] + left]).astype(bf16)
    right, left = shift(right_sum, "x", 1), shift(left_sum, "x", -1)
    return add(part(0), right, left)


def body(
    feats,
    neigh,
    pre_act,
    cotan,
    w_self,
    w_neigh,
    send_list,
    send_live,
    cross_list,
    cross_live,
    home_tiles,
    home_target,
    home_source,
    far_tiles,
    far_target,
    far_source,
    far_count,
):
    y, z, x, core = (lax.axis_index(name) for name in AXES)
    first = core == 0
    cols = (((1,), (1,)), ((), ()))
    rows = (((0,), (0,)), ((), ()))
    grad_pre = jnp.where(pre_act > 0, cotan, jnp.zeros_like(cotan))

    def halves(value):
        low, high = value[..., :HALF], value[..., HALF:]
        return jnp.where(first, low, high), jnp.where(first, high, low)

    def join(mine, other):
        low, high = jnp.where(first, mine, other), jnp.where(first, other, mine)
        return jnp.concatenate([low, high], axis=-1)

    wn_mine = lax.dynamic_slice_in_dim(w_neigh, core * HALF, HALF)
    wn_other = lax.dynamic_slice_in_dim(w_neigh, (1 - core) * HALF, HALF)
    agg_other = lax.dot_general(grad_pre, wn_other, cols, preferred_element_type=f32).astype(bf16)
    agg_sib = shift(agg_other.reshape(2, BLK, HALF), "core", 1)
    agg_own = lax.dot_general(grad_pre, wn_mine, cols, preferred_element_type=f32).astype(bf16)
    agg_own = agg_own.reshape(2, BLK, HALF)
    chunk = jnp.concatenate([agg_own, agg_sib])
    gathered = lax.all_gather(chunk, ("z", "x"), axis=0, tiled=True)

    send_code = (send_live[0, 0] * 2 + send_list[0, 0]).astype(i32)
    send_code = lax.all_to_all(send_code, DOM, 0, 0, tiled=True)
    cross_code = (cross_live[0, 0] * 2 + cross_list[0, 0]).astype(i32)
    cross_code = lax.all_to_all(cross_code, "group", 0, 0, tiled=True).reshape(-1)
    table = jnp.concatenate(
        [
            send_code,
            cross_code,
            home_target[0, 0],
            home_source[0, 0],
            far_target[0, 0],
            far_source[0, 0],
            far_count[0],
            jnp.zeros((ROW - FC - 1,), i32),
        ]
    )
    place = jnp.stack([core, z, x, y]).astype(i32)
    table = jnp.concatenate([table, shift(table, "core", 1), place])
    home_own, far_own = home_tiles[0, 0], far_tiles[0, 0]
    home_sib, far_sib = shift(home_own, "core", 1), shift(far_own, "core", 1)
    crossed = jnp.concatenate([chunk] + [shift(chunk, "group", dy) for dy in (1, 2, 3)])

    gp_mine, gp_other = halves(grad_pre)

    def weight_part(gp):
        sums = jnp.concatenate(
            [lax.dot_general(v, gp, rows, preferred_element_type=f32) for v in (feats, neigh)]
        )
        bias = jnp.sum(gp.astype(f32), axis=0).reshape(2, BLK)
        return jnp.concatenate([sums, jnp.pad(bias, ((0, 1022), (0, 0)))], axis=1)

    weights = weight_part(gp_mine) + shift(weight_part(gp_other), "core", 1)
    weights = weights.reshape(NY, 256, 384)

    def for_group(dy):
        return lax.dynamic_index_in_dim(weights, (y + dy) % NY, 0, keepdims=False)

    weights = sum((shift(for_group(dy), "group", dy) for dy in (1, 2, 3)), for_group(0))
    weights = lax.all_to_all(weights.reshape(32, 8, 384), ("z", "x"), 0, 0, tiled=True)
    weights = jnp.sum(weights, axis=0)
    weights = lax.all_gather(weights, ("z", "x"), axis=0, tiled=True)
    weights = lax.all_gather(weights, "group", axis=0, tiled=True)
    weights_sib = shift(weights, "core", 1)
    sums = join(weights[:, :HALF], weights_sib[:, :HALF])
    bias = join(weights[:2, HALF:].reshape(-1), weights_sib[:2, HALF:].reshape(-1))

    self_grad = lax.dot_general(grad_pre, w_self, cols, preferred_element_type=f32)
    acc = home_partials(table, home_own, home_sib, agg_own, agg_sib)
    parts = far_partials(table, far_own, far_sib, acc, gathered, crossed)
    na, nb = len(A_PARTS), len(B_PARTS)
    sum_b = return_b(*parts[na : na + nb])
    sum_a = return_a(*parts[:na])
    from_groups = [shift(part, "group", dy + 1) for dy, part in enumerate(parts[na + nb :])]
    sum_b = add(sum_b, *[part[2:] for part in from_groups])
    sum_a = add(sum_a, *[part[:2] for part in from_groups])
    other = shift(sum_b, "core", 1)
    grad_input = self_grad + join(sum_a.reshape(2 * BLK, HALF), other.reshape(2 * BLK, HALF))
    return grad_input.astype(bf16), sums[:512], sums[512:], bias


def solution(mesh):
    fine = Mesh(mesh.devices.reshape(NY, NZ, NX, 2), AXES)
    rows = P(AXES, None)
    part = lambda extra: P("group", DOM, *([None] * extra))
    return jax.shard_map(
        body,
        mesh=fine,
        in_specs=(rows,) * 4
        + (P(), P())
        + (part(1), part(1), part(2), part(2), part(3), part(1), part(1), part(3), part(1), part(1), part(0)),
        out_specs=(rows, P(), P(), P()),
        check_vma=False,
    )
```

```python
import jax
import jax.numpy as jnp
from jax import lax
from jax.experimental import pallas as pl
from jax.experimental.pallas import tpu as pltpu
from jax.sharding import Mesh
from jax.sharding import PartitionSpec as P

AXES = ("group", "z", "x", "core")
DOM = ("z", "x", "core")
NY, NZ, NX = 4, 8, 4
BLK, HALF = 128, 256
NT = 16
SLOTS = 32
bf16, f32, i32 = jnp.bfloat16, jnp.float32, jnp.int32

OTHER = 128
FIELDS = 5
LIST = 1 + FIELDS * 128

FIRST = 40
FIRST_PARTS = ((0, 8), (8, 8), (16, 4), (20, 4), (24, 8), (32, 8))
REST_PARTS = ((0, 16), (16, 16), (32, 16)) + tuple((48 + 8 * j, 8) for j in range(7)) + ((104, 16), (120, 16))
REST = 136
NP = FIRST + REST

VMEM = pl.BlockSpec(memory_space=pltpu.VMEM)
SMEM = pl.BlockSpec(memory_space=pltpu.SMEM)
HBM = pl.BlockSpec(memory_space=pltpu.HBM)


def shift(value, axis, k):
    n = {"group": NY, "z": NZ, "x": NX, "core": 2}[axis]
    return lax.ppermute(value, axis, [(i, (i + k) % n) for i in range(n)])


def own_kernel(meta, send, cross, home_target, home_source, far_target, far_source, count, out):
    core, z, x, y = (meta[j] for j in range(4))
    own = (z * NX + x) * 4 + core * 2

    def code_of(slot):
        q = jnp.clip(slot - 2, 0, 63)
        v = jnp.clip(slot - 66, 0, 7)
        in_dom = slot < 66
        word = jnp.where(in_dom, send[q], cross[v])
        k = word & 1
        group = v >> 1
        other = jnp.where(group == y, own + k, OTHER + group * 2 + k)
        code = jnp.where(in_dom, q * 2 + k, other)
        return jnp.where(word >= 2, code, -1)

    def place_of(slot):
        return jnp.where(slot < 2, own + slot, code_of(slot))

    @pl.loop(0, NT)
    def _(t):
        place = place_of(far_source[t])
        live = jnp.logical_and(t < count[0], place >= 0)
        out[t] = jnp.where(live, code_of(far_target[t]), -1)
        out[NT + t] = place
        out[2 * NT + t] = home_target[t]
        out[3 * NT + t] = place_of(home_source[t])


def accumulator(meta, place, r, dx):
    core, z, x, y = (meta[j] for j in range(4))
    k = place & 1
    to_z = ((place >> 4) - z) & 7
    to_x = (((place >> 2) & 3) - x) & 3
    same = ((place >> 1) & 1) == core
    a = jnp.where(to_x == 2, 0, FIRST + 16 * jnp.minimum(to_x, 2)) + to_z * 2
    b = jnp.where(to_z == 4, 16, FIRST + 48 + 8 * jnp.where(to_z > 4, to_z - 1, to_z)) + to_x * 2
    dy = (((place - OTHER) >> 1) - y) & 3
    c = jnp.where(dy == 2, 24, jnp.where(dy == 1, FIRST + 104, FIRST + 120)) + r * 8 + dx * 2
    return jnp.where(place >= OTHER, c, jnp.where(same, a, b)) + k


def row_kernel(meta, *refs):
    rows, lists = refs[:NX], refs[NX:]
    core, z, x, y = (meta[j] for j in range(4))
    for out in lists:
        out[0] = 0
    for dx in range(NX):
        for r in range(2):

            @pl.loop(0, NT)
            def _(t, dx=dx, r=r):
                code = rows[dx][r * 2 * NT + t]
                in_column = jnp.where(code >= OTHER, dx == 0, ((code >> 2) & 3) == x)

                @pl.when(jnp.logical_and(code >= 0, in_column))
                def _():
                    k = code & 1
                    dz = ((code >> 4) - z) & 7
                    rr = ((code >> 1) & 1) ^ core
                    far = dz == 4
                    block_ref = jnp.where(far, 4 + rr, jnp.where(dz > 4, dz + 1, dz))
                    block = jnp.where(far, k, rr * 2 + k)
                    crossed = code >= OTHER
                    away = (y - ((code - OTHER) >> 1)) & 3
                    block_ref = jnp.where(crossed, 9, block_ref)
                    block = jnp.where(crossed, away * 4 + r * 2 + k, block)
                    if dx == 2:
                        tile_ref, tile = jnp.where(t < 8, 6 + r, 8 + r), t & 7
                    else:
                        tile_ref, tile = (0, 2, None, 4)[dx] + r, t
                    place = accumulator(meta, rows[dx][r * 2 * NT + NT + t], r, dx)

                    def append(out, place):
                        n = out[0]
                        out[0] = n + 1
                        for j, value in enumerate((tile_ref, tile, block_ref, block, place)):
                            out[1 + 128 * j + n] = value

                    @pl.when(place < FIRST)
                    def _():
                        append(lists[0], place)

                    @pl.when(place >= FIRST)
                    def _():
                        append(lists[1], place - FIRST)


def tile_product(tile, block):
    return lax.dot_general(tile, block, (((0,), (0,)), ((), ())), preferred_element_type=f32)


def home_kernel(meta, tab_own, tab_sib, tiles_own, tiles_sib, agg, out_first, out_rest, acc, sems):
    @pl.loop(0, NP)
    def _(b):
        acc[b] = jnp.zeros((BLK, HALF), bf16)

    for r, (tab, tiles) in enumerate(((tab_own, tiles_own), (tab_sib, tiles_sib))):

        @pl.loop(0, NT)
        def _(t, r=r, tab=tab, tiles=tiles):
            code = tab[3 * NT + t]

            @pl.when(code >= 0)
            def _():
                place = accumulator(meta, code, r, 0)
                term = tile_product(tiles[t], agg[2 * r + tab[2 * NT + t]])
                acc[place] = (acc[place].astype(f32) + term).astype(bf16)

    copies = [
        pltpu.make_async_copy(acc.at[pl.ds(0, FIRST)], out_first, sems.at[0]),
        pltpu.make_async_copy(acc.at[pl.ds(FIRST, REST)], out_rest, sems.at[1]),
    ]
    for copy in copies:
        copy.start()
    for copy in copies:
        copy.wait()


def far_kernel(parts, todo, base, *refs):
    tile_refs, block_refs, outs = refs[:10], refs[10:20], refs[20 : 20 + len(parts)]
    acc, tiles, blocks, tile_sems, block_sems, load_sem, out_sems = refs[20 + len(parts) :]
    load = pltpu.make_async_copy(base, acc, load_sem)
    load.start()
    n = todo[0]

    def held(c):
        return jnp.clip(n - c * SLOTS, 0, SLOTS)

    def start(c):
        def one(j, _):
            i = c * SLOTS + j
            which, tile = todo[1 + i], todo[1 + 128 + i]
            for s, ref in enumerate(tile_refs):

                @pl.when(which == s)
                def _(ref=ref):
                    pltpu.make_async_copy(ref.at[tile], tiles.at[j], tile_sems.at[j]).start()

            which_block, block = todo[1 + 256 + i], todo[1 + 384 + i]
            for s, ref in enumerate(block_refs):

                @pl.when(which_block == s)
                def _(ref=ref):
                    pltpu.make_async_copy(ref.at[block], blocks.at[j], block_sems.at[j]).start()

            return 0

        lax.fori_loop(0, held(c), one, 0)

    def finish(c):
        def one(j, _):
            place = todo[1 + 512 + c * SLOTS + j]
            pltpu.make_async_copy(tile_refs[0].at[0], tiles.at[j], tile_sems.at[j]).wait()
            pltpu.make_async_copy(block_refs[0].at[0], blocks.at[j], block_sems.at[j]).wait()
            term = tile_product(tiles[j], blocks[j])
            acc[place] = (acc[place].astype(f32) + term).astype(bf16)
            return 0

        lax.fori_loop(0, held(c), one, 0)

    start(0)
    load.wait()

    def step(c, _):
        finish(c)
        start(c + 1)
        return 0

    lax.fori_loop(0, (n + SLOTS - 1) // SLOTS, step, 0)
    copies = [
        pltpu.make_async_copy(acc.at[pl.ds(s, m)], out, out_sems.at[j])
        for j, ((s, m), out) in enumerate(zip(parts, outs))
    ]
    for copy in copies:
        copy.start()
    for copy in copies:
        copy.wait()


def blocks_of(n):
    return jax.ShapeDtypeStruct((n, BLK, HALF), bf16)


def far_partials(parts, size, todo, base, tile_refs, block_refs):
    return pl.pallas_call(
        lambda *refs: far_kernel(parts, *refs),
        out_shape=[blocks_of(m) for _, m in parts],
        in_specs=[SMEM] + [HBM] * 21,
        out_specs=[HBM] * len(parts),
        scratch_shapes=[
            pltpu.VMEM((size, BLK, HALF), bf16),
            pltpu.VMEM((SLOTS, BLK, BLK), bf16),
            pltpu.VMEM((SLOTS, BLK, HALF), bf16),
            pltpu.SemaphoreType.DMA((SLOTS,)),
            pltpu.SemaphoreType.DMA((SLOTS,)),
            pltpu.SemaphoreType.DMA,
            pltpu.SemaphoreType.DMA((len(parts),)),
        ],
        compiler_params=pltpu.CompilerParams(vmem_limit_bytes=20 * 2**20),
    )(todo, base, *tile_refs, *block_refs)


def home_partials(meta, tab_own, tab_sib, tiles_own, tiles_sib, agg):
    return pl.pallas_call(
        home_kernel,
        out_shape=[blocks_of(FIRST), blocks_of(REST)],
        in_specs=[SMEM] * 3 + [VMEM] * 3,
        out_specs=[HBM, HBM],
        scratch_shapes=[pltpu.VMEM((NP, BLK, HALF), bf16), pltpu.SemaphoreType.DMA((2,))],
        compiler_params=pltpu.CompilerParams(vmem_limit_bytes=20 * 2**20),
    )(meta, tab_own, tab_sib, tiles_own, tiles_sib, agg)


def scalars(kernel, sizes, *args):
    return pl.pallas_call(
        kernel,
        out_shape=[jax.ShapeDtypeStruct((n,), i32) for n in sizes],
        in_specs=[SMEM] * len(args),
        out_specs=[SMEM] * len(sizes),
    )(*args)


def add(*terms):
    total = terms[0].astype(f32)
    for term in terms[1:]:
        total = total + term.astype(f32)
    return total


def add_head(value, head):
    n = head.shape[0]
    return jnp.concatenate([add(value[:n], head).astype(bf16), value[n:].astype(bf16)])


def add_tail(value, tail):
    n = value.shape[0] - tail.shape[0]
    return jnp.concatenate([value[:n].astype(bf16), add(value[n:], tail).astype(bf16)])


def return_sums(first, rest):
    a2h, a2t, b4h, b4t, y2h, y2t = first
    a0, a1, a3, b0, b1, b2, b3, b5, b6, b7, y1, y3 = rest
    ax_p, ax_m = shift(a2h, "x", 1), shift(a2t, "x", -1)
    up, down = shift(b4h, "z", 1), shift(b4t, "z", -1)
    y_p, y_m = shift(y2h, "group", 1), shift(y2t, "group", -1)

    ax_p, ax_m = shift(add_head(a1, ax_p), "x", 1), shift(add_tail(a3, ax_m), "x", -1)
    up, down = shift(add_head(b3, up), "z", 1), shift(add_tail(b5, down), "z", -1)
    y_p, y_m = shift(add_head(y1, y_p), "group", 1), shift(add_tail(y3, y_m), "group", -1)
    for plus, minus in ((b2, b6), (b1, b7)):
        up, down = add(plus, up).astype(bf16), add(minus, down).astype(bf16)
        up, down = shift(up, "z", 1), shift(down, "z", -1)

    def part_a(dz):
        rows = slice(2 * dz, 2 * dz + 2)
        return add(a0[rows], ax_p[rows], ax_m[rows])

    def part_b(dx):
        rows = slice(2 * dx, 2 * dx + 2)
        cross = slice(8 + 2 * dx, 10 + 2 * dx)
        sums = add(b0[rows], up[rows], down[rows], y_p[cross], y_m[cross])
        return jnp.concatenate([sums, add(y_p[rows], y_m[rows])])

    far = part_a(4).astype(bf16)
    az_p, az_m = shift(far[:1], "z", 1), shift(far[1:], "z", -1)
    az_p, az_m = add_head(part_a(3), az_p), add_tail(part_a(5), az_m)
    az_p, az_m = shift(az_p, "z", 1), shift(az_m, "z", -1)
    az_p, az_m = add(part_a(2), az_p).astype(bf16), add(part_a(6), az_m).astype(bf16)
    far = part_b(2).astype(bf16)
    az_p, az_m, far = lax.optimization_barrier((az_p, az_m, far))
    bx_p, bx_m = shift(far[:2], "x", 1), shift(far[2:], "x", -1)
    az_p, az_m = shift(az_p, "z", 1), shift(az_m, "z", -1)
    bx_p, bx_m = add_head(part_b(1), bx_p), add_tail(part_b(3), bx_m)
    az_p, az_m = add(part_a(1), az_p).astype(bf16), add(part_a(7), az_m).astype(bf16)
    az_p, az_m, bx_p, bx_m = lax.optimization_barrier((az_p, az_m, bx_p, bx_m))
    bx_p, bx_m = shift(bx_p, "x", 1), shift(bx_m, "x", -1)
    az_p, az_m = shift(az_p, "z", 1), shift(az_m, "z", -1)
    sum_b = add(part_b(0), bx_p, bx_m)
    return add(part_a(0), az_p, az_m, sum_b[2:]), sum_b[:2]


def body(
    feats,
    neigh,
    pre_act,
    cotan,
    w_self,
    w_neigh,
    send_list,
    send_live,
    cross_list,
    cross_live,
    home_tiles,
    home_target,
    home_source,
    far_tiles,
    far_target,
    far_source,
    far_count,
):
    y, z, x, core = (lax.axis_index(name) for name in AXES)
    meta = jnp.stack([core, z, x, y]).astype(i32)
    first_core = core == 0
    cols = (((1,), (1,)), ((), ()))
    rows = (((0,), (0,)), ((), ()))
    grad_pre = jnp.where(pre_act > 0, cotan, jnp.zeros_like(cotan))

    def halves(value):
        low, high = value[..., :HALF], value[..., HALF:]
        return jnp.where(first_core, low, high), jnp.where(first_core, high, low)

    def join(mine, other):
        low, high = jnp.where(first_core, mine, other), jnp.where(first_core, other, mine)
        return jnp.concatenate([low, high], axis=-1)

    wn_mine = lax.dynamic_slice_in_dim(w_neigh, core * HALF, HALF)
    wn_other = lax.dynamic_slice_in_dim(w_neigh, (1 - core) * HALF, HALF)
    agg_other = lax.dot_general(grad_pre, wn_other, cols, preferred_element_type=f32).astype(bf16)
    agg_sib = shift(agg_other.reshape(2, BLK, HALF), "core", 1)
    agg_own = lax.dot_general(grad_pre, wn_mine, cols, preferred_element_type=f32).astype(bf16)
    chunk = jnp.concatenate([agg_own.reshape(2, BLK, HALF), agg_sib])

    far_own = far_tiles[0, 0]
    up1, dn1 = shift(chunk, "z", 1), shift(chunk, "z", -1)
    tiles3, tiles1 = shift(far_own, "x", 1), shift(far_own, "x", -1)
    up2, dn2 = shift(up1, "z", 1), shift(dn1, "z", -1)
    tiles2h, tiles2t = shift(tiles3[:8], "x", 1), shift(tiles1[8:], "x", -1)
    up3, dn3 = shift(up2, "z", 1), shift(dn2, "z", -1)
    up4, dn4 = shift(up3[:2], "z", 1), shift(dn3[2:], "z", -1)
    tile_refs = []
    for tiles in (far_own, tiles1, tiles3, tiles2h, tiles2t):
        tile_refs += [tiles, shift(tiles, "core", 1)]
    crossed = jnp.concatenate([chunk] + [shift(chunk, "group", dy) for dy in (1, 2, 3)])
    block_refs = [chunk, dn1, dn2, dn3, up4, dn4, up3, up2, up1, crossed]

    send_word = (send_live[0, 0] * 2 + send_list[0, 0]).astype(i32)
    send_word = lax.all_to_all(send_word, DOM, 0, 0, tiled=True)
    cross_word = (cross_live[0, 0] * 2 + cross_list[0, 0]).astype(i32)
    cross_word = lax.all_to_all(cross_word, "group", 0, 0, tiled=True).reshape(-1)
    (tab_own,) = scalars(
        own_kernel,
        (4 * NT,),
        meta,
        send_word,
        cross_word,
        home_target[0, 0],
        home_source[0, 0],
        far_target[0, 0],
        far_source[0, 0],
        far_count[0],
    )
    tab_sib = shift(tab_own, "core", 1)
    row = jnp.concatenate([tab_own[: 2 * NT], tab_sib[: 2 * NT]])
    todo_first, todo_rest = scalars(
        row_kernel, (LIST, LIST), meta, row, shift(row, "x", -1), shift(row, "x", 2), shift(row, "x", 1)
    )
    home_own = home_tiles[0, 0]
    base_first, base_rest = home_partials(meta, tab_own, tab_sib, home_own, shift(home_own, "core", 1), chunk)

    gp_mine, gp_other = halves(grad_pre)

    def weight_part(gp):
        sums = jnp.concatenate(
            [lax.dot_general(v, gp, rows, preferred_element_type=f32) for v in (feats, neigh)]
        )
        bias = jnp.sum(gp.astype(f32), axis=0).reshape(2, BLK)
        return jnp.concatenate([sums, jnp.pad(bias, ((0, 1022), (0, 0)))], axis=1)

    weights = weight_part(gp_mine) + shift(weight_part(gp_other), "core", 1)
    weights = weights.reshape(NY, 256, 384)

    def for_group(dy):
        return lax.dynamic_index_in_dim(weights, (y + dy) % NY, 0, keepdims=False)

    weights = sum((shift(for_group(dy), "group", dy) for dy in (1, 2, 3)), for_group(0))
    weights = lax.psum_scatter(weights, "z", scatter_dimension=0, tiled=True)
    weights = sum((shift(weights, "x", dx) for dx in (1, 2, 3)), weights)
    weights = lax.all_gather(weights, ("group", "z"), axis=0, tiled=True)
    weights_sib = shift(weights, "core", 1)
    sums = join(weights[:, :HALF], weights_sib[:, :HALF])
    bias = join(weights[:2, HALF:].reshape(-1), weights_sib[:2, HALF:].reshape(-1))

    self_grad = lax.dot_general(grad_pre, w_self, cols, preferred_element_type=f32)
    first = far_partials(FIRST_PARTS, FIRST, todo_first, base_first, tile_refs, block_refs)
    rest = far_partials(REST_PARTS, REST, todo_rest, base_rest, tile_refs, block_refs)
    sum_a, sum_b = return_sums(first, rest)
    other = shift(sum_b, "core", 1)
    grad_input = self_grad + join(sum_a.reshape(2 * BLK, HALF), other.reshape(2 * BLK, HALF))
    return grad_input.astype(bf16), sums[:512], sums[512:], bias


def solution(mesh):
    fine = Mesh(mesh.devices.reshape(NY, NZ, NX, 2), AXES)
    rows = P(AXES, None)
    part = lambda extra: P("group", DOM, *([None] * extra))
    return jax.shard_map(
        body,
        mesh=fine,
        in_specs=(rows,) * 4
        + (P(), P())
        + (part(1), part(1), part(2), part(2), part(3), part(1), part(1), part(3), part(1), part(1), part(0)),
        out_specs=(rows, P(), P(), P()),
        check_vma=False,
    )
```

```python
import jax
import jax.numpy as jnp
from jax import lax
from jax.experimental import pallas as pl
from jax.experimental.pallas import tpu as pltpu
from jax.sharding import Mesh
from jax.sharding import PartitionSpec as P

AXES = ("group", "z", "x", "core")
DOM = ("z", "x", "core")
NY, NZ, NX = 4, 8, 4
BLK, HALF = 128, 256
NT = 16
SLOTS = 32
bf16, f32, i32 = jnp.bfloat16, jnp.float32, jnp.int32

SEND, CROSS, HT, HS, FT, FS, FC, INTS = 0, 64, 72, 88, 104, 120, 136, 256
HEAD = 16
FIELDS, ENTRIES = 5, 160
LIST = 1 + FIELDS * ENTRIES
PICKED = 1 + 128

FIRST = 40
FIRST_PARTS = ((0, 8), (8, 8), (16, 4), (20, 4), (24, 8), (32, 8))
REST_PARTS = ((0, 16), (16, 16), (32, 16)) + tuple((48 + 8 * j, 8) for j in range(7)) + ((104, 16), (120, 16))
REST = 136
NP = FIRST + REST

VMEM = pl.BlockSpec(memory_space=pltpu.VMEM)
SMEM = pl.BlockSpec(memory_space=pltpu.SMEM)
HBM = pl.BlockSpec(memory_space=pltpu.HBM)


def shift(value, axis, k):
    n = {"group": NY, "z": NZ, "x": NX, "core": 2}[axis]
    return lax.ppermute(value, axis, [(i, (i + k) % n) for i in range(n)])


def pick_kernel(meta, row, out):
    x = meta[2]
    out[0] = 0
    for dx in range(NX):
        for r in range(2):
            base = (dx * 2 + r) * INTS

            @pl.loop(0, jnp.minimum(row[base + FC], NT))
            def _(t, dx=dx, r=r, base=base):
                slot = row[base + FT + t]
                column = ((slot - 2) >> 1) & 3
                here = jnp.where(slot < 66, column == x, dx == 0)

                @pl.when(here)
                def _():
                    n = out[0]
                    out[0] = n + 1
                    out[1 + n] = (dx * 2 + r) * NT + t


def list_kernel(meta, row, picked, words, cross, first, rest):
    core, z, x, y = (meta[j] for j in range(4))
    first[0] = 0
    rest[0] = 0

    def master(slot, dx, r):
        in_dom = slot < 66
        q = jnp.clip(slot - 2, 0, 63)
        dz = ((q >> 3) - z) & 7
        to_x = (((q >> 1) & 3) - x) & 3
        same = ((q & 1) ^ core)
        me = z * 8 + ((x + dx) & 3) * 2 + (core ^ r)
        v = jnp.clip(slot - 66, 0, 7)
        dy = ((v >> 1) - y) & 3
        word = jnp.where(
            in_dom,
            words[(dz * 8 + to_x * 2 + same) * 64 + me],
            cross[((4 - dy) & 3) * 256 + (dx * 2 + r) * 8 + y * 2 + (v & 1)],
        )
        k = word & 1
        dz = jnp.where(in_dom, dz, 0)
        to_x = jnp.where(in_dom, to_x, dx)
        same = jnp.where(in_dom, same, r)
        dy = jnp.where(in_dom, 0, dy)
        return word >= 2, dy, dz, to_x, same, k

    def accumulator(slot, dx, r):
        live, dy, dz, to_x, same, k = master(slot, dx, r)
        own = slot < 2
        live = jnp.logical_or(own, live)
        dy, dz = jnp.where(own, 0, dy), jnp.where(own, 0, dz)
        to_x, same = jnp.where(own, dx, to_x), jnp.where(own, r, same)
        k = jnp.where(own, slot, k)
        a = jnp.where(to_x == 2, 0, FIRST + 16 * jnp.minimum(to_x, 2)) + dz * 2
        b = jnp.where(dz == 4, 16, FIRST + 48 + 8 * jnp.where(dz > 4, dz - 1, dz)) + to_x * 2
        c = jnp.where(dy == 2, 24, jnp.where(dy == 1, FIRST + 104, FIRST + 120)) + r * 8 + dx * 2
        return live, jnp.where(dy > 0, c, jnp.where(same == 0, a, b)) + k

    def append(tile_ref, tile, block_ref, start, place):
        def into(out, place):
            n = out[0]
            out[0] = n + 1
            for j, value in enumerate((tile_ref, tile, block_ref, start, place)):
                out[1 + ENTRIES * j + n] = value

        @pl.when(place < FIRST)
        def _():
            into(first, place)

        @pl.when(place >= FIRST)
        def _():
            into(rest, place - FIRST)

    @pl.loop(0, 2 * NT)
    def _(i):
        r, t = i >> 4, i & 15
        live, place = accumulator(row[r * INTS + HS + t], 0, r)

        @pl.when(live)
        def _():
            append(10 + r, t, 0, HEAD + BLK * (2 * r + row[r * INTS + HT + t]), place)

    @pl.loop(0, picked[0])
    def _(i):
        which = picked[1 + i]
        dx, r, t = which >> 5, (which >> 4) & 1, which & 15
        base = (which >> 4) * INTS
        target_live, dy, dz, _, same, k = master(row[base + FT + t], dx, r)
        source_live, place = accumulator(row[base + FS + t], dx, r)

        @pl.when(jnp.logical_and(target_live, source_live))
        def _():
            far = dz == 4
            block_ref = jnp.where(far, 4 + same, jnp.where(dz > 4, dz + 1, dz))
            block_ref = jnp.where(dy > 0, 12 - dy, block_ref)
            j = jnp.where(far, k, 2 * same + k)
            start = jnp.where(jnp.logical_and(far, same == 1), 0, HEAD) + BLK * j
            half = dx == 2
            tile_ref = jnp.where(half, jnp.where(t < 8, 6, 8), jnp.where(dx == 3, 4, 2 * dx)) + r
            append(tile_ref, jnp.where(half, t & 7, t), block_ref, start, place)


bar = lax.optimization_barrier


def tile_product(tile, block):
    return lax.dot_general(tile, block, (((0,), (0,)), ((), ())), preferred_element_type=f32)


def tile_kernel(parts, todo, *refs):
    tile_refs, block_refs, outs = refs[:12], refs[12:24], refs[24 : 24 + len(parts)]
    acc, tiles, blocks, tile_sems, block_sems, out_sems = refs[24 + len(parts) :]
    n = todo[0]

    def held(c):
        return jnp.clip(n - c * SLOTS, 0, SLOTS)

    def start(c):
        def one(j, _):
            i = c * SLOTS + j
            which, tile = todo[1 + i], todo[1 + ENTRIES + i]
            for s, ref in enumerate(tile_refs):

                @pl.when(which == s)
                def _(ref=ref):
                    pltpu.make_async_copy(ref.at[tile], tiles.at[j], tile_sems.at[j]).start()

            which_block = todo[1 + 2 * ENTRIES + i]
            at = pl.multiple_of(todo[1 + 3 * ENTRIES + i], 16)
            for s, ref in enumerate(block_refs):

                @pl.when(which_block == s)
                def _(ref=ref):
                    copy = pltpu.make_async_copy(ref.at[pl.ds(at, BLK)], blocks.at[j], block_sems.at[j])
                    copy.start()

            return 0

        lax.fori_loop(0, held(c), one, 0)

    def finish(c):
        def one(j, _):
            place = todo[1 + 4 * ENTRIES + c * SLOTS + j]
            pltpu.make_async_copy(tile_refs[0].at[0], tiles.at[j], tile_sems.at[j]).wait()
            pltpu.make_async_copy(block_refs[0].at[pl.ds(0, BLK)], blocks.at[j], block_sems.at[j]).wait()
            term = tile_product(tiles[j], blocks[j])
            acc[place] = (acc[place].astype(f32) + term).astype(bf16)
            return 0

        lax.fori_loop(0, held(c), one, 0)

    start(0)

    @pl.loop(0, acc.shape[0])
    def _(b):
        acc[b] = jnp.zeros((BLK, HALF), bf16)

    def step(c, _):
        finish(c)
        start(c + 1)
        return 0

    lax.fori_loop(0, (n + SLOTS - 1) // SLOTS, step, 0)
    copies = [
        pltpu.make_async_copy(acc.at[pl.ds(s, m)], out, out_sems.at[j])
        for j, ((s, m), out) in enumerate(zip(parts, outs))
    ]
    for copy in copies:
        copy.start()
    for copy in copies:
        copy.wait()


def tile_sums(parts, size, todo, tile_refs, block_refs):
    return pl.pallas_call(
        lambda *refs: tile_kernel(parts, *refs),
        out_shape=[jax.ShapeDtypeStruct((m, BLK, HALF), bf16) for _, m in parts],
        in_specs=[SMEM] + [HBM] * 24,
        out_specs=[HBM] * len(parts),
        scratch_shapes=[
            pltpu.VMEM((size, BLK, HALF), bf16),
            pltpu.VMEM((SLOTS, BLK, BLK), bf16),
            pltpu.VMEM((SLOTS, BLK, HALF), bf16),
            pltpu.SemaphoreType.DMA((SLOTS,)),
            pltpu.SemaphoreType.DMA((SLOTS,)),
            pltpu.SemaphoreType.DMA((len(parts),)),
        ],
        compiler_params=pltpu.CompilerParams(vmem_limit_bytes=20 * 2**20),
    )(todo, *tile_refs, *block_refs)


def weight_kernel(meta, feats, neigh, grad_pre, mine, other):
    core, y = meta[0], meta[3]
    low, high = grad_pre[:, :HALF], grad_pre[:, HALF:]
    for out, from_low in ((mine, core == 0), (other, core == 1)):
        part = jnp.where(from_low, low, high)
        bias = jnp.sum(part.astype(f32), axis=0, keepdims=True)
        for g in range(NY):
            source = feats if g < 2 else neigh
            cols = source[:, (g % 2) * HALF : (g % 2 + 1) * HALF]
            dy = (g - y) & 3
            out[dy, :, :HALF] = tile_product(cols, part)
            out[dy, :, HALF:] = jnp.zeros((HALF, BLK), f32)
            if g == 0:
                out[dy, 0:1, HALF:] = bias[:, :BLK]
                out[dy, 1:2, HALF:] = bias[:, BLK:]


def weight_terms(meta, feats, neigh, grad_pre):
    return pl.pallas_call(
        weight_kernel,
        out_shape=[jax.ShapeDtypeStruct((NY, HALF, HALF + BLK), f32)] * 2,
        in_specs=[SMEM] + [VMEM] * 3,
        out_specs=[VMEM] * 2,
        compiler_params=pltpu.CompilerParams(vmem_limit_bytes=16 * 2**20),
    )(meta, feats, neigh, grad_pre)


def scalars(kernel, sizes, *args):
    return pl.pallas_call(
        kernel,
        out_shape=[jax.ShapeDtypeStruct((n,), i32) for n in sizes],
        in_specs=[SMEM] * len(args),
        out_specs=[SMEM] * len(sizes),
    )(*args)


def add(*terms):
    total = terms[0].astype(f32)
    for term in terms[1:]:
        total = total + term.astype(f32)
    return total


def add_head(value, head):
    n = head.shape[0]
    return jnp.concatenate([add(value[:n], head).astype(bf16), value[n:].astype(bf16)])


def add_tail(value, tail):
    n = value.shape[0] - tail.shape[0]
    return jnp.concatenate([value[:n].astype(bf16), add(value[n:], tail).astype(bf16)])


def return_sums(first, rest_of):
    a2h, a2t, b4h, b4t, y2h, y2t = first
    up, down = shift(b4h, "z", 1), shift(b4t, "z", -1)
    ax_p, ax_m = shift(a2h, "x", 1), shift(a2t, "x", -1)
    y_p, y_m = shift(y2h, "group", 1), shift(y2t, "group", -1)
    (up, down), rest = rest_of((up, down))
    a0, a1, a3, b0, b1, b2, b3, b5, b6, b7, y1, y3 = rest

    up, down, ax_p, ax_m, y_p, y_m = bar((up, down, ax_p, ax_m, y_p, y_m))
    ax_p, ax_m = shift(add_head(a1, ax_p), "x", 1), shift(add_tail(a3, ax_m), "x", -1)
    up, down = shift(add_head(b3, up), "z", 1), shift(add_tail(b5, down), "z", -1)
    y_p, y_m = shift(add_head(y1, y_p), "group", 1), shift(add_tail(y3, y_m), "group", -1)
    up, down = add(b2, up).astype(bf16), add(b6, down).astype(bf16)
    up, down = shift(up, "z", 1), shift(down, "z", -1)

    def part_a(dz):
        rows = slice(2 * dz, 2 * dz + 2)
        return add(a0[rows], ax_p[rows], ax_m[rows])

    def part_b(dx):
        rows = slice(2 * dx, 2 * dx + 2)
        cross = slice(8 + 2 * dx, 10 + 2 * dx)
        sums = add(b0[rows], up[rows], down[rows], y_p[cross], y_m[cross])
        return jnp.concatenate([sums, add(y_p[rows], y_m[rows])])

    up, down, ax_p, ax_m, y_p, y_m = bar((up, down, ax_p, ax_m, y_p, y_m))
    far = part_a(4).astype(bf16)
    az_p, az_m = shift(far[:1], "z", 1), shift(far[1:], "z", -1)
    up, down = add(b1, up).astype(bf16), add(b7, down).astype(bf16)
    up, down = shift(up, "z", 1), shift(down, "z", -1)
    az_p, az_m = add_head(part_a(3), az_p), add_tail(part_a(5), az_m)
    az_p, az_m = shift(az_p, "z", 1), shift(az_m, "z", -1)
    az_p, az_m = add(part_a(2), az_p).astype(bf16), add(part_a(6), az_m).astype(bf16)
    far = part_b(2).astype(bf16)
    az_p, az_m, far = bar((az_p, az_m, far))
    bx_p, bx_m = shift(far[:2], "x", 1), shift(far[2:], "x", -1)
    az_p, az_m = shift(az_p, "z", 1), shift(az_m, "z", -1)
    bx_p, bx_m = add_head(part_b(1), bx_p), add_tail(part_b(3), bx_m)
    az_p, az_m = add(part_a(1), az_p).astype(bf16), add(part_a(7), az_m).astype(bf16)
    az_p, az_m, bx_p, bx_m = bar((az_p, az_m, bx_p, bx_m))
    bx_p, bx_m = shift(bx_p, "x", 1), shift(bx_m, "x", -1)
    az_p, az_m = shift(az_p, "z", 1), shift(az_m, "z", -1)
    sum_b = add(part_b(0), bx_p, bx_m)
    return add(part_a(0), az_p, az_m, sum_b[2:]), sum_b[:2]


def body(
    feats,
    neigh,
    pre_act,
    cotan,
    w_self,
    w_neigh,
    send_list,
    send_live,
    cross_list,
    cross_live,
    home_tiles,
    home_target,
    home_source,
    far_tiles,
    far_target,
    far_source,
    far_count,
):
    y, z, x, core = (lax.axis_index(name) for name in AXES)
    meta = jnp.stack([core, z, x, y]).astype(i32)
    first_core = core == 0
    cols = (((1,), (1,)), ((), ()))
    ints = jnp.concatenate(
        [
            (send_live * 2 + send_list).reshape(-1),
            (cross_live * 2 + cross_list).reshape(-1),
            home_target[0, 0],
            home_source[0, 0],
            far_target[0, 0],
            far_source[0, 0],
            far_count[0],
            jnp.zeros((INTS - FC - 1,), i32),
        ]
    )
    row = jnp.stack([ints, shift(ints, "x", -1), shift(ints, "x", 2), shift(ints, "x", 1)])
    row = jnp.stack([row, shift(row, "core", 1)], axis=1)
    words = row[:, :, :CROSS].reshape(2, HALF).astype(bf16)
    cross_words = jnp.pad(row[:, :, CROSS:HT].reshape(1, BLK // 2).astype(bf16), ((0, 0), (0, HALF - BLK // 2)))
    row = row.reshape(-1)

    grad_pre = jnp.where(pre_act > 0, cotan, jnp.zeros_like(cotan))

    def join(mine, other):
        low, high = jnp.where(first_core, mine, other), jnp.where(first_core, other, mine)
        return jnp.concatenate([low, high], axis=-1)

    wn_mine = lax.dynamic_slice_in_dim(w_neigh, core * HALF, HALF)
    wn_other = lax.dynamic_slice_in_dim(w_neigh, (1 - core) * HALF, HALF)
    agg_other = lax.dot_general(grad_pre, wn_other, cols, preferred_element_type=f32).astype(bf16)
    agg_sib = shift(agg_other, "core", 1)
    agg_own = lax.dot_general(grad_pre, wn_mine, cols, preferred_element_type=f32).astype(bf16)
    head = jnp.concatenate([words, cross_words, jnp.zeros((HEAD - 3, HALF), bf16)])
    chunk = jnp.concatenate([head, agg_own, agg_sib])

    far_own, home_own = far_tiles[0, 0], home_tiles[0, 0]
    chunk, far_own, feats, neigh, grad_pre, home_own = bar((chunk, far_own, feats, neigh, grad_pre, home_own))
    up1, dn1 = shift(chunk, "z", 1), shift(chunk, "z", -1)
    tiles3, tiles1 = shift(far_own, "x", 1), shift(far_own, "x", -1)
    mine, other = weight_terms(meta, feats, neigh, grad_pre)
    weights = mine + shift(other, "core", 1)
    up1, dn1, weights, far_own = bar((up1, dn1, weights, far_own))

    up2, dn2 = shift(up1, "z", 1), shift(dn1, "z", -1)
    weights = sum((shift(weights[dy], "group", dy) for dy in (1, 2, 3)), weights[0])
    far_sib, home_sib = shift(far_own, "core", 1), shift(home_own, "core", 1)
    up2, dn2, weights, tiles1, tiles3, chunk, row = bar((up2, dn2, weights, tiles1, tiles3, chunk, row))

    up3, dn3 = shift(up2, "z", 1), shift(dn2, "z", -1)
    weights = lax.psum_scatter(weights, "z", scatter_dimension=0, tiled=True)
    tiles2h, tiles2t = shift(tiles3[:8], "x", 1), shift(tiles1[8:], "x", -1)
    from_y = [shift(chunk, "group", dy) for dy in (1, 2, 3)]
    (picked,) = scalars(pick_kernel, (PICKED,), meta, row)
    up3, dn3, tiles1, tiles3, picked = bar((up3, dn3, tiles1, tiles3, picked))

    middle = HEAD + 2 * BLK
    up4, dn4 = shift(up3[:middle], "z", 1), shift(dn3[middle:], "z", -1)
    sib1, sib3 = shift(tiles1, "core", 1), shift(tiles3, "core", 1)
    sib2h, sib2t = shift(tiles2h, "core", 1), shift(tiles2t, "core", 1)
    up4, dn4, sib1, sib3, sib2h, sib2t, from_y = bar((up4, dn4, sib1, sib3, sib2h, sib2t, from_y))
    tile_refs = [far_own, far_sib, tiles1, sib1, tiles3, sib3, tiles2h, sib2h, tiles2t, sib2t, home_own, home_sib]
    block_refs = [chunk, dn1, dn2, dn3, up4, dn4, up3, up2, up1] + from_y
    all_words = jnp.concatenate([v[:2] for v in (chunk, dn1, dn2, dn3, up4, up3, up2, up1)])
    all_cross = jnp.concatenate([v[2:3] for v in [chunk] + from_y])
    todo_first, todo_rest = scalars(
        list_kernel,
        (LIST, LIST),
        meta,
        row,
        picked,
        all_words.astype(i32).reshape(-1),
        all_cross.astype(i32).reshape(-1),
    )
    first = tile_sums(FIRST_PARTS, FIRST, todo_first, tile_refs, block_refs)

    late = {}

    def rest_of(arrived):
        arrived, todo, w, gp = bar((arrived, todo_rest, weights, grad_pre))
        late["weights"], late["grad_pre"] = w, gp
        return arrived, tile_sums(REST_PARTS, REST, todo, tile_refs, block_refs)

    sum_a, sum_b = return_sums(first, rest_of)
    weights, grad_pre = late["weights"], late["grad_pre"]
    weights = sum((shift(weights, "x", dx) for dx in (1, 2, 3)), weights)
    weights = jnp.stack([shift(weights, "group", -dy) if dy else weights for dy in range(NY)])
    weights = lax.all_gather(weights, "z", axis=0)
    self_grad = lax.dot_general(grad_pre, w_self, cols, preferred_element_type=f32)

    weights, sum_b, self_grad = bar((weights, sum_b, self_grad))
    other = shift(sum_b, "core", 1)
    weights_sib = shift(weights, "core", 1)

    def rows_of(value):
        return jnp.roll(value, y, axis=1).transpose(1, 0, 2, 3).reshape(4 * HALF, HALF + BLK)

    weights, weights_sib = rows_of(weights), rows_of(weights_sib)
    sums = join(weights[:, :HALF], weights_sib[:, :HALF])
    bias = join(weights[:2, HALF:].reshape(-1), weights_sib[:2, HALF:].reshape(-1))
    grad_input = self_grad + join(sum_a.reshape(2 * BLK, HALF), other.reshape(2 * BLK, HALF))
    return grad_input.astype(bf16), sums[:512], sums[512:], bias


def solution(mesh):
    fine = Mesh(mesh.devices.reshape(NY, NZ, NX, 2), AXES)
    rows = P(AXES, None)
    part = lambda extra: P("group", DOM, *([None] * extra))
    return jax.shard_map(
        body,
        mesh=fine,
        in_specs=(rows,) * 4
        + (P(), P())
        + (part(1), part(1), part(2), part(2), part(3), part(1), part(1), part(3), part(1), part(1), part(0)),
        out_specs=(rows, P(), P(), P()),
        check_vma=False,
    )
```

```python
import jax
import jax.numpy as jnp
from jax import lax
from jax.experimental import pallas as pl
from jax.experimental.pallas import tpu as pltpu
from jax.sharding import Mesh
from jax.sharding import PartitionSpec as P

AXES = ("group", "z", "x", "core")
DOM = ("z", "x", "core")
NY, NZ, NX = 4, 8, 4
BLK, HALF = 128, 256
NT = 16
SLOTS = 32
bf16, f32, i32 = jnp.bfloat16, jnp.float32, jnp.int32

SEND, CROSS, HT, HS, FT, FS, FC, INTS = 0, 64, 72, 88, 104, 120, 136, 256
HEAD = 16
FIELDS, ENTRIES = 5, 160
LIST = 1 + FIELDS * ENTRIES
PICKED = 1 + 128

GROUPS = (
    ((0, 8), (8, 8), (16, 4), (20, 4), (24, 8), (32, 8)),
    ((0, 16), (16, 16), (32, 8), (40, 8), (48, 16), (64, 16)),
    ((0, 16), (16, 8), (24, 8), (32, 8), (40, 8), (48, 8)),
)
STARTS, SIZES = (0, 40, 120), (40, 80, 56)
MIB = 2**20

VMEM = pl.BlockSpec(memory_space=pltpu.VMEM)
SMEM = pl.BlockSpec(memory_space=pltpu.SMEM)
ANY = pl.BlockSpec(memory_space=pl.ANY)
HBM = pl.BlockSpec(memory_space=pltpu.HBM)


def shift(value, axis, k):
    n = {"group": NY, "z": NZ, "x": NX, "core": 2}[axis]
    return lax.ppermute(value, axis, [(i, (i + k) % n) for i in range(n)])


def pick_kernel(meta, row, out):
    x = meta[2]
    out[0] = 0
    for dx in range(NX):
        for r in range(2):
            base = (dx * 2 + r) * INTS

            @pl.loop(0, jnp.minimum(row[base + FC], NT))
            def _(t, dx=dx, r=r, base=base):
                slot = row[base + FT + t]
                column = ((slot - 2) >> 1) & 3
                here = jnp.where(slot < 66, column == x, dx == 0)

                @pl.when(here)
                def _():
                    n = out[0]
                    out[0] = n + 1
                    out[1 + n] = (dx * 2 + r) * NT + t


def list_kernel(meta, row, picked, *refs):
    heads, lists, (low, wide, words, sems) = refs[:11], refs[11:14], refs[14:]
    core, z, x, y = (meta[j] for j in range(4))
    copies = [pltpu.make_async_copy(v.at[pl.ds(0, HEAD)], low.at[j], sems.at[j]) for j, v in enumerate(heads)]
    for copy in copies:
        copy.start()
    for copy in copies:
        copy.wait()
    wide[...] = low[...].astype(f32).astype(i32)
    copy = pltpu.make_async_copy(wide.at[:, pl.ds(0, 8)], words, sems.at[0])
    copy.start()
    copy.wait()
    for out in lists:
        out[0] = 0

    def master(slot, dx, r):
        in_dom = slot < 66
        q = jnp.clip(slot - 2, 0, 63)
        dz = ((q >> 3) - z) & 7
        to_x = (((q >> 1) & 3) - x) & 3
        same = ((q & 1) ^ core)
        me = z * 8 + ((x + dx) & 3) * 2 + (core ^ r)
        v = jnp.clip(slot - 66, 0, 7)
        dy = ((v >> 1) - y) & 3
        word = jnp.where(
            in_dom,
            words[dz, to_x >> 1, ((to_x & 1) * 2 + same) * 64 + me],
            words[jnp.where(dy == 0, 0, 11 - dy), 2, (dx * 2 + r) * 8 + y * 2 + (v & 1)],
        )
        k = word & 1
        dz = jnp.where(in_dom, dz, 0)
        to_x = jnp.where(in_dom, to_x, dx)
        same = jnp.where(in_dom, same, r)
        dy = jnp.where(in_dom, 0, dy)
        return word >= 2, dy, dz, to_x, same, k

    def accumulator(slot, dx, r):
        live, dy, dz, to_x, same, k = master(slot, dx, r)
        own = slot < 2
        live = jnp.logical_or(own, live)
        dy, dz = jnp.where(own, 0, dy), jnp.where(own, 0, dz)
        to_x, same = jnp.where(own, dx, to_x), jnp.where(own, r, same)
        k = jnp.where(own, slot, k)
        a = jnp.where(to_x == 0, 120, jnp.where(to_x == 2, 0, 32 + 8 * to_x)) + dz * 2
        middle = jnp.where(dz == 4, 16, 72 + 4 * (dz - 3))
        outer = jnp.where(dz < 3, 136 + 8 * dz, 112 + 8 * dz)
        b = jnp.where((dz - 4) * (dz - 4) < 2, middle, outer) + to_x * 2
        c = jnp.where(dy == 2, 24, jnp.where(dy == 1, 88, 104)) + r * 8 + dx * 2
        return live, jnp.where(dy > 0, c, jnp.where(same == 0, a, b)) + k

    def append(tile_ref, tile, block_ref, start, place):
        def into(out, place):
            n = out[0]
            out[0] = n + 1
            for j, value in enumerate((tile_ref, tile, block_ref, start, place)):
                out[1 + ENTRIES * j + n] = value

        for out, begin, size in zip(lists, STARTS, SIZES):

            @pl.when(jnp.logical_and(place >= begin, place < begin + size))
            def _(out=out, begin=begin):
                into(out, place - begin)

    @pl.loop(0, 2 * NT)
    def _(i):
        r, t = i >> 4, i & 15
        live, place = accumulator(row[r * INTS + HS + t], 0, r)

        @pl.when(live)
        def _():
            append(5 + r, t, 0, HEAD + BLK * (2 * r + row[r * INTS + HT + t]), place)

    @pl.loop(0, picked[0])
    def _(i):
        which = picked[1 + i]
        dx, r, t = which >> 5, (which >> 4) & 1, which & 15
        base = (which >> 4) * INTS
        target_live, dy, dz, _, same, k = master(row[base + FT + t], dx, r)
        source_live, place = accumulator(row[base + FS + t], dx, r)

        @pl.when(jnp.logical_and(target_live, source_live))
        def _():
            far = dz == 4
            block_ref = jnp.where(far, 4 + same, jnp.where(dz > 4, dz + 1, dz))
            block_ref = jnp.where(dy > 0, 12 - dy, block_ref)
            j = jnp.where(far, k, 2 * same + k)
            start = jnp.where(jnp.logical_and(far, same == 1), 0, HEAD) + BLK * j
            tile_ref = jnp.where(dx == 2, 3 + r, jnp.where(dx == 3, 2, dx))
            append(tile_ref, jnp.where(dx == 2, t, r * NT + t), block_ref, start, place)


bar = lax.optimization_barrier


def tile_product(tile, block):
    return lax.dot_general(tile, block, (((0,), (0,)), ((), ())), preferred_element_type=f32)


def tile_kernel(parts, todo, *refs):
    tile_refs, block_refs, outs = refs[:7], refs[7:19], refs[19 : 19 + len(parts)]
    acc, tiles, blocks, tile_sems, block_sems, out_sems = refs[19 + len(parts) :]
    n = todo[0]

    def held(c):
        return jnp.clip(n - c * SLOTS, 0, SLOTS)

    def start(c):
        def one(j, _):
            i = c * SLOTS + j
            which, tile = todo[1 + i], todo[1 + ENTRIES + i]
            for s, ref in enumerate(tile_refs):

                @pl.when(which == s)
                def _(ref=ref):
                    pltpu.make_async_copy(ref.at[tile], tiles.at[j], tile_sems.at[j]).start()

            which_block = todo[1 + 2 * ENTRIES + i]
            at = pl.multiple_of(todo[1 + 3 * ENTRIES + i], 16)
            for s, ref in enumerate(block_refs):

                @pl.when(which_block == s)
                def _(ref=ref):
                    copy = pltpu.make_async_copy(ref.at[pl.ds(at, BLK)], blocks.at[j], block_sems.at[j])
                    copy.start()

            return 0

        lax.fori_loop(0, held(c), one, 0)

    def finish(c):
        def one(j, _):
            place = todo[1 + 4 * ENTRIES + c * SLOTS + j]
            pltpu.make_async_copy(tile_refs[0].at[0], tiles.at[j], tile_sems.at[j]).wait()
            pltpu.make_async_copy(block_refs[0].at[pl.ds(0, BLK)], blocks.at[j], block_sems.at[j]).wait()
            term = tile_product(tiles[j], blocks[j])
            acc[place] = (acc[place].astype(f32) + term).astype(bf16)
            return 0

        lax.fori_loop(0, held(c), one, 0)

    start(0)

    @pl.loop(0, acc.shape[0])
    def _(b):
        acc[b] = jnp.zeros((BLK, HALF), bf16)

    def step(c, _):
        finish(c)
        start(c + 1)
        return 0

    lax.fori_loop(0, (n + SLOTS - 1) // SLOTS, step, 0)
    copies = [
        pltpu.make_async_copy(acc.at[pl.ds(s, m)], out, out_sems.at[j])
        for j, ((s, m), out) in enumerate(zip(parts, outs))
    ]
    for copy in copies:
        copy.start()
    for copy in copies:
        copy.wait()


def tile_sums(group, todo, tile_refs, block_refs):
    parts, size = GROUPS[group], SIZES[group]
    return pl.pallas_call(
        lambda *refs: tile_kernel(parts, *refs),
        out_shape=[jax.ShapeDtypeStruct((m, BLK, HALF), bf16) for _, m in parts],
        in_specs=[SMEM] + [ANY] * 19,
        out_specs=[HBM] * len(parts),
        scratch_shapes=[
            pltpu.VMEM((size, BLK, HALF), bf16),
            pltpu.VMEM((SLOTS, BLK, BLK), bf16),
            pltpu.VMEM((SLOTS, BLK, HALF), bf16),
            pltpu.SemaphoreType.DMA((SLOTS,)),
            pltpu.SemaphoreType.DMA((SLOTS,)),
            pltpu.SemaphoreType.DMA((len(parts),)),
        ],
        compiler_params=pltpu.CompilerParams(vmem_limit_bytes=10 * MIB),
        cost_estimate=pl.CostEstimate(flops=10**9, bytes_accessed=2 * 10**7, transcendentals=0),
    )(todo, *tile_refs, *block_refs)


def agg_kernel(meta, pre_act, cotan, w_neigh, grad_pre, agg_own, agg_other):
    grad = jnp.where(pre_act[...] > 0, cotan[...], jnp.zeros_like(cotan))
    grad_pre[...] = grad
    for out, half in ((agg_other, 1 - meta[0]), (agg_own, meta[0])):
        weight = w_neigh[pl.ds(pl.multiple_of(half * HALF, HALF), HALF), :]
        product = lax.dot_general(grad, weight, (((1,), (1,)), ((), ())), preferred_element_type=f32)
        out[...] = product.astype(bf16)


def agg_terms(meta, pre_act, cotan, w_neigh):
    half = jax.ShapeDtypeStruct((HALF, HALF), bf16)
    return pl.pallas_call(
        agg_kernel,
        out_shape=[jax.ShapeDtypeStruct(pre_act.shape, bf16), half, half],
        in_specs=[SMEM] + [VMEM] * 3,
        out_specs=[VMEM] * 3,
        compiler_params=pltpu.CompilerParams(vmem_limit_bytes=6 * MIB),
    )(meta, pre_act, cotan, w_neigh)


def join_kernel(head, own, sib, out):
    out[:HEAD] = head[...]
    out[HEAD : HEAD + HALF] = own[...]
    out[HEAD + HALF :] = sib[...]


def join_chunk(head, own, sib):
    return pl.pallas_call(
        join_kernel,
        out_shape=jax.ShapeDtypeStruct((HEAD + 2 * HALF, HALF), bf16),
        in_specs=[VMEM] * 3,
        out_specs=VMEM,
        compiler_params=pltpu.CompilerParams(vmem_limit_bytes=4 * MIB),
    )(head, own, sib)


def weight_kernel(meta, feats, neigh, grad_pre, mine, other):
    core = meta[0]
    low, high = grad_pre[:, :HALF], grad_pre[:, HALF:]
    for out, from_low in ((mine, core == 0), (other, core == 1)):
        part = jnp.where(from_low, low, high)
        bias = jnp.sum(part.astype(f32), axis=0, keepdims=True)
        for g in range(NY):
            source = feats if g < 2 else neigh
            cols = source[:, (g % 2) * HALF : (g % 2 + 1) * HALF]
            out[g, :, :HALF] = tile_product(cols, part)
            out[g, :, HALF:] = jnp.zeros((HALF, BLK), f32)
            if g == 0:
                out[g, 0:1, HALF:] = bias[:, :BLK]
                out[g, 1:2, HALF:] = bias[:, BLK:]


def weight_terms(meta, feats, neigh, grad_pre):
    return pl.pallas_call(
        weight_kernel,
        out_shape=[jax.ShapeDtypeStruct((NY, HALF, HALF + BLK), f32)] * 2,
        in_specs=[SMEM] + [VMEM] * 3,
        out_specs=[VMEM] * 2,
        compiler_params=pltpu.CompilerParams(vmem_limit_bytes=10 * MIB),
    )(meta, feats, neigh, grad_pre)


def scalars(kernel, sizes, *args, tables=(), scratch=()):
    return pl.pallas_call(
        kernel,
        out_shape=[jax.ShapeDtypeStruct((n,), i32) for n in sizes],
        in_specs=[SMEM] * len(args) + [ANY] * len(tables),
        out_specs=[SMEM] * len(sizes),
        scratch_shapes=scratch,
        compiler_params=pltpu.CompilerParams(vmem_limit_bytes=3 * MIB),
    )(*args, *tables)


def add(*terms):
    total = terms[0].astype(f32)
    for term in terms[1:]:
        total = total + term.astype(f32)
    return total


def add_head(value, head):
    n = head.shape[0]
    return jnp.concatenate([add(value[:n], head).astype(bf16), value[n:].astype(bf16)])


def add_tail(value, tail):
    n = value.shape[0] - tail.shape[0]
    return jnp.concatenate([value[:n].astype(bf16), add(value[n:], tail).astype(bf16)])


def return_sums(first, sums_of):
    a2h, a2t, b4h, b4t, y2h, y2t = first
    b4h, b4t, a2h, a2t, (a1, a3, b3, b5, y1, y3) = sums_of(1, (b4h, b4t, a2h, a2t))
    up, down = shift(b4h, "z", 1), shift(b4t, "z", -1)
    ax_p, ax_m = shift(a2h, "x", 1), shift(a2t, "x", -1)
    up, down, y2h, y2t = bar((up, down, y2h, y2t))
    y_p, y_m = shift(y2h, "group", 1), shift(y2t, "group", -1)

    up, down, ax_p, ax_m, a1, a3, b3, b5 = bar((up, down, ax_p, ax_m, a1, a3, b3, b5))
    up, down, ax_p, ax_m, (a0, b0, b1, b2, b6, b7) = sums_of(2, (up, down, ax_p, ax_m))
    ax_p, ax_m = shift(add_head(a1, ax_p), "x", 1), shift(add_tail(a3, ax_m), "x", -1)
    up, down = shift(add_head(b3, up), "z", 1), shift(add_tail(b5, down), "z", -1)
    up, down, y_p, y_m = bar((up, down, y_p, y_m))
    up, down = add(b2, up).astype(bf16), add(b6, down).astype(bf16)
    up, down = shift(up, "z", 1), shift(down, "z", -1)
    y_p = shift(add_head(y1, y_p), "group", 1)
    y_p, y_m = bar((y_p, y_m))
    y_m = shift(add_tail(y3, y_m), "group", -1)

    def part_a(dz):
        rows = slice(2 * dz, 2 * dz + 2)
        return add(a0[rows], ax_p[rows], ax_m[rows])

    def part_b(dx):
        rows = slice(2 * dx, 2 * dx + 2)
        cross = slice(8 + 2 * dx, 10 + 2 * dx)
        sums = add(b0[rows], up[rows], down[rows], y_p[cross], y_m[cross])
        return jnp.concatenate([sums, add(y_p[rows], y_m[rows])])

    up, down, ax_p, ax_m = bar((up, down, ax_p, ax_m))
    far = part_a(4).astype(bf16)
    up, down = add(b1, up).astype(bf16), add(b7, down).astype(bf16)
    az_p, az_m = shift(far[:1], "z", 1), shift(far[1:], "z", -1)
    up, down = shift(up, "z", 1), shift(down, "z", -1)
    az_p, az_m = add_head(part_a(3), az_p), add_tail(part_a(5), az_m)
    az_p, az_m = shift(az_p, "z", 1), shift(az_m, "z", -1)
    az_p, az_m = add(part_a(2), az_p).astype(bf16), add(part_a(6), az_m).astype(bf16)
    far = part_b(2).astype(bf16)
    az_p, az_m, far = bar((az_p, az_m, far))
    bx_p, bx_m = shift(far[:2], "x", 1), shift(far[2:], "x", -1)
    az_p, az_m = shift(az_p, "z", 1), shift(az_m, "z", -1)
    bx_p, bx_m = add_head(part_b(1), bx_p), add_tail(part_b(3), bx_m)
    az_p, az_m = add(part_a(1), az_p).astype(bf16), add(part_a(7), az_m).astype(bf16)
    az_p, az_m, bx_p, bx_m = bar((az_p, az_m, bx_p, bx_m))
    bx_p, bx_m = shift(bx_p, "x", 1), shift(bx_m, "x", -1)
    az_p, az_m = shift(az_p, "z", 1), shift(az_m, "z", -1)
    sum_b = add(part_b(0), bx_p, bx_m)
    return add(part_a(0), az_p, az_m, sum_b[2:]), sum_b[:2]


def body(
    feats,
    neigh,
    pre_act,
    cotan,
    w_self,
    w_neigh,
    send_list,
    send_live,
    cross_list,
    cross_live,
    home_tiles,
    home_target,
    home_source,
    far_tiles,
    far_target,
    far_source,
    far_count,
):
    y, z, x, core = (lax.axis_index(name) for name in AXES)
    meta = jnp.stack([core, z, x, y]).astype(i32)
    first_core = core == 0
    cols = (((1,), (1,)), ((), ()))
    ints = jnp.concatenate(
        [
            (send_live * 2 + send_list).reshape(-1),
            (cross_live * 2 + cross_list).reshape(-1),
            home_target[0, 0],
            home_source[0, 0],
            far_target[0, 0],
            far_source[0, 0],
            far_count[0],
            jnp.zeros((INTS - FC - 1,), i32),
        ]
    )
    row = jnp.stack([ints, shift(ints, "x", -1), shift(ints, "x", 2), shift(ints, "x", 1)])
    row = jnp.stack([row, shift(row, "core", 1)], axis=1)
    words = row[:, :, :CROSS].reshape(2, HALF).astype(bf16)
    cross_words = jnp.pad(row[:, :, CROSS:HT].reshape(1, BLK // 2).astype(bf16), ((0, 0), (0, HALF - BLK // 2)))
    row = row.reshape(-1)

    def join(mine, other):
        low, high = jnp.where(first_core, mine, other), jnp.where(first_core, other, mine)
        return jnp.concatenate([low, high], axis=-1)

    grad_pre, agg_own, agg_other = agg_terms(meta, pre_act, cotan, w_neigh)
    head = jnp.concatenate([words, cross_words, jnp.zeros((HEAD - 3, HALF), bf16)])
    chunk = join_chunk(head, agg_own, shift(agg_other, "core", 1))

    far_own, home_own = far_tiles[0, 0], home_tiles[0, 0]
    mine, other = weight_terms(meta, feats, neigh, grad_pre)

    far_both = jnp.concatenate([far_own, shift(far_own, "core", 1)])
    home_sib = shift(home_own, "core", 1)
    chunk, far_both, home_sib, mine, other = bar((chunk, far_both, home_sib, mine, other))
    up1, dn1 = shift(chunk, "z", 1), shift(chunk, "z", -1)
    tiles3, tiles1 = shift(far_both, "x", 1), shift(far_both, "x", -1)
    other = shift(other, "core", 1)
    up1, dn1, chunk, row, mine, other = bar((up1, dn1, chunk, row, mine, other))
    weights = (mine + other).reshape(4 * HALF, HALF + BLK)
    weights = lax.psum_scatter(weights, "group", scatter_dimension=0, tiled=True)
    weights = lax.psum_scatter(weights, "z", scatter_dimension=0, tiled=True)
    weights = jnp.pad(weights, ((0, 16), (0, 0)))
    weights = lax.all_gather(weights, ("group", "x"), axis=0).reshape(NY, NX, 48, HALF + BLK)
    weights = jnp.sum(weights[:, :, :32], axis=1)
    weights = lax.all_gather(weights, "z", axis=0)
    up2, dn2 = shift(up1, "z", 1), shift(dn1, "z", -1)
    y1 = shift(chunk, "group", 1)
    (picked,) = scalars(pick_kernel, (PICKED,), meta, row)
    up2, dn2, y1, tiles1, tiles3, chunk, picked = bar((up2, dn2, y1, tiles1, tiles3, chunk, picked))
    up3, dn3 = shift(up2, "z", 1), shift(dn2, "z", -1)
    tiles2h, tiles2t = shift(tiles3[:NT], "x", 1), shift(tiles1[NT:], "x", -1)
    y3 = shift(chunk, "group", 3)
    up3, dn3, y3, chunk = bar((up3, dn3, y3, chunk))
    middle = HEAD + 2 * BLK
    up4, dn4 = shift(up3[:middle], "z", 1), shift(dn3[middle:], "z", -1)
    y2 = shift(chunk, "group", 2)
    up4, dn4, tiles2h, tiles2t, y2 = bar((up4, dn4, tiles2h, tiles2t, y2))

    tile_refs = [far_both, tiles1, tiles3, tiles2h, tiles2t, home_own, home_sib]
    block_refs = [chunk, dn1, dn2, dn3, up4, dn4, up3, up2, up1, y1, y2, y3]
    heads = [chunk, dn1, dn2, dn3, up4, up3, up2, up1, y1, y2, y3]
    todo = scalars(
        list_kernel,
        (LIST,) * 3,
        meta,
        row,
        picked,
        tables=heads,
        scratch=[
            pltpu.VMEM((len(heads), HEAD, HALF), bf16),
            pltpu.VMEM((len(heads), HEAD, HALF), i32),
            pltpu.SMEM((len(heads), 8, HALF), i32),
            pltpu.SemaphoreType.DMA((len(heads),)),
        ],
    )

    def sums_of(group, arrived):
        *arrived, now = bar((*arrived, todo[group]))
        return *arrived, tile_sums(group, now, tile_refs, block_refs)

    (first,) = sums_of(0, ())
    sum_a, sum_b = return_sums(first, sums_of)
    self_grad = lax.dot_general(grad_pre, w_self, cols, preferred_element_type=f32)
    weights, sum_b = bar((weights, sum_b))
    other = shift(sum_b, "core", 1)
    weights_sib = shift(weights, "core", 1)

    def rows_of(value):
        return value.transpose(1, 0, 2, 3).reshape(4 * HALF, HALF + BLK)

    weights, weights_sib = rows_of(weights), rows_of(weights_sib)
    sums = join(weights[:, :HALF], weights_sib[:, :HALF])
    bias = join(weights[:2, HALF:].reshape(-1), weights_sib[:2, HALF:].reshape(-1))
    grad_input = self_grad + join(sum_a.reshape(2 * BLK, HALF), other.reshape(2 * BLK, HALF))
    return grad_input.astype(bf16), sums[:512], sums[512:], bias


def solution(mesh):
    fine = Mesh(mesh.devices.reshape(NY, NZ, NX, 2), AXES)
    rows = P(AXES, None)
    part = lambda extra: P("group", DOM, *([None] * extra))
    return jax.shard_map(
        body,
        mesh=fine,
        in_specs=(rows,) * 4
        + (P(), P())
        + (part(1), part(1), part(2), part(2), part(3), part(1), part(1), part(3), part(1), part(1), part(0)),
        out_specs=(rows, P(), P(), P()),
        check_vma=False,
    )
```

```python
import jax
import jax.numpy as jnp
from jax import lax
from jax.experimental import pallas as pl
from jax.experimental.pallas import tpu as pltpu
from jax.sharding import Mesh
from jax.sharding import PartitionSpec as P

AXES = ("group", "z", "x", "core")
DOM = ("z", "x", "core")
NY, NZ, NX = 4, 8, 4
BLK, HALF = 128, 256
NT = 16
SLOTS = 32
bf16, f32, i32 = jnp.bfloat16, jnp.float32, jnp.int32

SEND, CROSS, HT, HS, FT, FS, FC, INTS = 0, 64, 72, 88, 104, 120, 136, 256
HEAD = 16
FIELDS, ENTRIES = 5, 161
LIST = 1 + FIELDS * ENTRIES
PICKED = 1 + 128

GROUPS = (
    ((0, 8), (8, 8), (16, 4), (20, 4), (24, 8), (32, 8)),
    ((0, 16), (16, 16), (32, 8), (40, 8), (48, 16), (64, 16)),
    ((0, 16), (16, 8), (24, 8), (32, 8), (40, 8), (48, 8)),
)
STARTS, SIZES = (0, 40, 120), (40, 80, 56)
MIB = 2**20

VMEM = pl.BlockSpec(memory_space=pltpu.VMEM)
SMEM = pl.BlockSpec(memory_space=pltpu.SMEM)
ANY = pl.BlockSpec(memory_space=pl.ANY)
HBM = pl.BlockSpec(memory_space=pltpu.HBM)


def shift(value, axis, k):
    n = {"group": NY, "z": NZ, "x": NX, "core": 2}[axis]
    return lax.ppermute(value, axis, [(i, (i + k) % n) for i in range(n)])


def pick_kernel(meta, row, out):
    x = meta[2]
    out[0] = 0
    for dx in range(NX):
        for r in range(2):
            base = (dx * 2 + r) * INTS

            @pl.loop(0, jnp.minimum(row[base + FC], NT))
            def _(t, dx=dx, r=r, base=base):
                slot = row[base + FT + t]
                column = ((slot - 2) >> 1) & 3
                here = jnp.where(slot < 66, column == x, dx == 0)

                @pl.when(here)
                def _():
                    n = out[0]
                    out[0] = n + 1
                    out[1 + n] = (dx * 2 + r) * NT + t


def list_kernel(meta, row, picked, *refs):
    heads, (out, low, wide, words, sems) = refs[:11], refs[11:]
    core, z, x, y = (meta[j] for j in range(4))
    copies = [pltpu.make_async_copy(v.at[pl.ds(0, HEAD)], low.at[j], sems.at[j]) for j, v in enumerate(heads)]
    for copy in copies:
        copy.start()
    for copy in copies:
        copy.wait()
    wide[...] = low[...].astype(f32).astype(i32)
    copy = pltpu.make_async_copy(wide.at[:, pl.ds(0, 8)], words, sems.at[0])
    copy.start()
    copy.wait()
    for group in range(3):
        out[group * LIST] = 0

    def master(slot, dx, r):
        in_dom = slot < 66
        q = jnp.clip(slot - 2, 0, 63)
        dz = ((q >> 3) - z) & 7
        to_x = (((q >> 1) & 3) - x) & 3
        same = ((q & 1) ^ core)
        me = z * 8 + ((x + dx) & 3) * 2 + (core ^ r)
        v = jnp.clip(slot - 66, 0, 7)
        dy = ((v >> 1) - y) & 3
        word = jnp.where(
            in_dom,
            words[dz, to_x >> 1, ((to_x & 1) * 2 + same) * 64 + me],
            words[jnp.where(dy == 0, 0, 11 - dy), 2, (dx * 2 + r) * 8 + y * 2 + (v & 1)],
        )
        k = word & 1
        dz = jnp.where(in_dom, dz, 0)
        to_x = jnp.where(in_dom, to_x, dx)
        same = jnp.where(in_dom, same, r)
        dy = jnp.where(in_dom, 0, dy)
        return word >= 2, dy, dz, to_x, same, k

    def accumulator(slot, dx, r):
        live, dy, dz, to_x, same, k = master(slot, dx, r)
        own = slot < 2
        live = jnp.logical_or(own, live)
        dy, dz = jnp.where(own, 0, dy), jnp.where(own, 0, dz)
        to_x, same = jnp.where(own, dx, to_x), jnp.where(own, r, same)
        k = jnp.where(own, slot, k)
        a = jnp.where(to_x == 0, 120, jnp.where(to_x == 2, 0, 32 + 8 * to_x)) + dz * 2
        middle = jnp.where(dz == 4, 16, 72 + 4 * (dz - 3))
        outer = jnp.where(dz < 3, 136 + 8 * dz, 112 + 8 * dz)
        b = jnp.where((dz - 4) * (dz - 4) < 2, middle, outer) + to_x * 2
        c = jnp.where(dy == 2, 24, jnp.where(dy == 1, 88, 104)) + r * 8 + dx * 2
        return live, jnp.where(dy > 0, c, jnp.where(same == 0, a, b)) + k

    def append(live, tile_ref, tile, block_ref, start, place):
        middle, last = place >= STARTS[1], place >= STARTS[2]
        base = jnp.where(last, 2 * LIST, jnp.where(middle, LIST, 0))
        place = place - jnp.where(last, STARTS[2], jnp.where(middle, STARTS[1], 0))
        n = out[base]
        for j, value in enumerate((tile_ref, tile, block_ref, start, place)):
            out[base + 1 + ENTRIES * j + n] = value
        out[base] = n + live.astype(i32)

    @pl.loop(0, 2 * NT, unroll=4)
    def _(i):
        r, t = i >> 4, i & 15
        live, place = accumulator(row[r * INTS + HS + t], 0, r)
        append(live, 5 + r, t, 0, HEAD + BLK * (2 * r + row[r * INTS + HT + t]), place)

    @pl.loop(0, picked[0])
    def _(i):
        which = picked[1 + i]
        dx, r, t = which >> 5, (which >> 4) & 1, which & 15
        base = (which >> 4) * INTS
        target_live, dy, dz, _, same, k = master(row[base + FT + t], dx, r)
        source_live, place = accumulator(row[base + FS + t], dx, r)
        far = dz == 4
        block_ref = jnp.where(far, 4 + same, jnp.where(dz > 4, dz + 1, dz))
        block_ref = jnp.where(dy > 0, 12 - dy, block_ref)
        j = jnp.where(far, k, 2 * same + k)
        start = jnp.where(jnp.logical_and(far, same == 1), 0, HEAD) + BLK * j
        tile_ref = jnp.where(dx == 2, 3 + r, jnp.where(dx == 3, 2, dx))
        live = jnp.logical_and(target_live, source_live)
        append(live, tile_ref, jnp.where(dx == 2, t, r * NT + t), block_ref, start, place)


bar = lax.optimization_barrier


def tile_product(tile, block):
    return lax.dot_general(tile, block, (((0,), (0,)), ((), ())), preferred_element_type=f32)


def tile_kernel(group, todo, *refs):
    parts, base = GROUPS[group], group * LIST
    tile_refs, block_refs, outs = refs[:7], refs[7:19], refs[19 : 19 + len(parts)]
    acc, tiles, blocks, tile_sems, block_sems, out_sems = refs[19 + len(parts) :]
    n = todo[base]

    def held(c):
        return jnp.clip(n - c * SLOTS, 0, SLOTS)

    def choose(which, options, low, act):
        if len(options) == 1:
            act(options[0])
            return
        cut = len(options) // 2

        @pl.when(which < low + cut)
        def _():
            choose(which, options[:cut], low, act)

        @pl.when(which >= low + cut)
        def _():
            choose(which, options[cut:], low + cut, act)

    def start(c):
        def one(j, _):
            i = base + 1 + c * SLOTS + j
            tile = todo[ENTRIES + i]
            at = pl.multiple_of(todo[3 * ENTRIES + i], 16)

            def fetch_tile(ref):
                pltpu.make_async_copy(ref.at[tile], tiles.at[j], tile_sems.at[j]).start()

            def fetch_block(ref):
                pltpu.make_async_copy(ref.at[pl.ds(at, BLK)], blocks.at[j], block_sems.at[j]).start()

            choose(todo[i], tile_refs, 0, fetch_tile)
            choose(todo[2 * ENTRIES + i], block_refs, 0, fetch_block)
            return 0

        lax.fori_loop(0, held(c), one, 0)

    def finish(c):
        def one(j, _):
            place = todo[base + 1 + 4 * ENTRIES + c * SLOTS + j]
            pltpu.make_async_copy(tile_refs[0].at[0], tiles.at[j], tile_sems.at[j]).wait()
            pltpu.make_async_copy(block_refs[0].at[pl.ds(0, BLK)], blocks.at[j], block_sems.at[j]).wait()
            term = tile_product(tiles[j], blocks[j])
            acc[place] = (acc[place].astype(f32) + term).astype(bf16)
            return 0

        lax.fori_loop(0, held(c), one, 0)

    start(0)

    @pl.loop(0, acc.shape[0])
    def _(b):
        acc[b] = jnp.zeros((BLK, HALF), bf16)

    def step(c, _):
        finish(c)
        start(c + 1)
        return 0

    lax.fori_loop(0, (n + SLOTS - 1) // SLOTS, step, 0)
    copies = [
        pltpu.make_async_copy(acc.at[pl.ds(s, m)], out, out_sems.at[j])
        for j, ((s, m), out) in enumerate(zip(parts, outs))
    ]
    for copy in copies:
        copy.start()
    for copy in copies:
        copy.wait()


def tile_sums(group, todo, tile_refs, block_refs):
    parts, size = GROUPS[group], SIZES[group]
    return pl.pallas_call(
        lambda *refs: tile_kernel(group, *refs),
        out_shape=[jax.ShapeDtypeStruct((m, BLK, HALF), bf16) for _, m in parts],
        in_specs=[SMEM] + [ANY] * 19,
        out_specs=[ANY] * len(parts),
        scratch_shapes=[
            pltpu.VMEM((size, BLK, HALF), bf16),
            pltpu.VMEM((SLOTS, BLK, BLK), bf16),
            pltpu.VMEM((SLOTS, BLK, HALF), bf16),
            pltpu.SemaphoreType.DMA((SLOTS,)),
            pltpu.SemaphoreType.DMA((SLOTS,)),
            pltpu.SemaphoreType.DMA((len(parts),)),
        ],
        compiler_params=pltpu.CompilerParams(vmem_limit_bytes=10 * MIB),
        cost_estimate=pl.CostEstimate(flops=10**9, bytes_accessed=2 * 10**7, transcendentals=0),
    )(todo, *tile_refs, *block_refs)


def join_kernel(head, own, sib, out):
    out[:HEAD] = head[...]
    out[HEAD : HEAD + HALF] = own[...]
    out[HEAD + HALF :] = sib[...]


def join_chunk(head, own, sib):
    return pl.pallas_call(
        join_kernel,
        out_shape=jax.ShapeDtypeStruct((HEAD + 2 * HALF, HALF), bf16),
        in_specs=[VMEM] * 3,
        out_specs=VMEM,
        compiler_params=pltpu.CompilerParams(vmem_limit_bytes=4 * MIB),
    )(head, own, sib)


def weight_kernel(meta, grad_pre, feats, neigh, mine, other, source, sums, sems):
    loads = [pltpu.make_async_copy(v, source.at[j], sems.at[j]) for j, v in enumerate((feats, neigh))]
    for load in loads:
        load.start()
    core = meta[0]
    low, high = grad_pre[:, :HALF], grad_pre[:, HALF:]
    for load in loads:
        load.wait()
    stores = []
    for j, (out, from_low) in enumerate(((other, core == 1), (mine, core == 0))):
        part = jnp.where(from_low, low, high)
        bias = jnp.sum(part.astype(f32), axis=0, keepdims=True)
        for g in range(NY):
            cols = source[g // 2, :, (g % 2) * HALF : (g % 2 + 1) * HALF]
            sums[j, g, :, :HALF] = tile_product(cols, part)
            sums[j, g, :, HALF:] = jnp.zeros((HALF, BLK), f32)
            if g == 0:
                sums[j, g, 0:1, HALF:] = bias[:, :BLK]
                sums[j, g, 1:2, HALF:] = bias[:, BLK:]
        stores.append(pltpu.make_async_copy(sums.at[j], out, sems.at[2 + j]))
        stores[-1].start()
    for store in stores:
        store.wait()


def weight_terms(meta, feats, neigh, grad_pre):
    shape = (NY, HALF, HALF + BLK)
    return pl.pallas_call(
        weight_kernel,
        out_shape=[jax.ShapeDtypeStruct(shape, f32)] * 2,
        in_specs=[SMEM, VMEM, HBM, HBM],
        out_specs=[HBM] * 2,
        scratch_shapes=[
            pltpu.VMEM((2, *feats.shape), bf16),
            pltpu.VMEM((2, *shape), f32),
            pltpu.SemaphoreType.DMA((4,)),
        ],
        compiler_params=pltpu.CompilerParams(vmem_limit_bytes=8 * MIB),
    )(meta, grad_pre, feats, neigh)


def agg_kernel(meta, pre_act, cotan, w_neigh, grad_pre, agg_own, agg_other):
    grad = jnp.where(pre_act[...] > 0, cotan[...], jnp.zeros_like(cotan))
    grad_pre[...] = grad
    for out, half in ((agg_other, 1 - meta[0]), (agg_own, meta[0])):
        weight = w_neigh[pl.ds(pl.multiple_of(half * HALF, HALF), HALF), :]
        product = lax.dot_general(grad, weight, (((1,), (1,)), ((), ())), preferred_element_type=f32)
        out[...] = product.astype(bf16)


def agg_terms(meta, pre_act, cotan, w_neigh):
    half = jax.ShapeDtypeStruct((HALF, HALF), bf16)
    return pl.pallas_call(
        agg_kernel,
        out_shape=[jax.ShapeDtypeStruct(pre_act.shape, bf16), half, half],
        in_specs=[SMEM] + [VMEM] * 3,
        out_specs=[VMEM] * 3,
        compiler_params=pltpu.CompilerParams(vmem_limit_bytes=6 * MIB),
    )(meta, pre_act, cotan, w_neigh)


def join_kernel(head, own, sib, out):
    out[:HEAD] = head[...]
    out[HEAD : HEAD + HALF] = own[...]
    out[HEAD + HALF :] = sib[...]


def join_chunk(head, own, sib):
    return pl.pallas_call(
        join_kernel,
        out_shape=jax.ShapeDtypeStruct((HEAD + 2 * HALF, HALF), bf16),
        in_specs=[VMEM] * 3,
        out_specs=VMEM,
        compiler_params=pltpu.CompilerParams(vmem_limit_bytes=4 * MIB),
    )(head, own, sib)


def weight_kernel(meta, feats, neigh, grad_pre, mine, other):
    core = meta[0]
    low, high = grad_pre[:, :HALF], grad_pre[:, HALF:]
    for out, from_low in ((mine, core == 0), (other, core == 1)):
        part = jnp.where(from_low, low, high)
        bias = jnp.sum(part.astype(f32), axis=0, keepdims=True)
        for g in range(NY):
            source = feats if g < 2 else neigh
            cols = source[:, (g % 2) * HALF : (g % 2 + 1) * HALF]
            out[g, :, :HALF] = tile_product(cols, part)
            out[g, :, HALF:] = jnp.zeros((HALF, BLK), f32)
            if g == 0:
                out[g, 0:1, HALF:] = bias[:, :BLK]
                out[g, 1:2, HALF:] = bias[:, BLK:]


def weight_terms(meta, feats, neigh, grad_pre):
    return pl.pallas_call(
        weight_kernel,
        out_shape=[jax.ShapeDtypeStruct((NY, HALF, HALF + BLK), f32)] * 2,
        in_specs=[SMEM] + [VMEM] * 3,
        out_specs=[VMEM] * 2,
        compiler_params=pltpu.CompilerParams(vmem_limit_bytes=10 * MIB),
    )(meta, feats, neigh, grad_pre)


def scalars(kernel, sizes, *args, tables=(), scratch=()):
    return pl.pallas_call(
        kernel,
        out_shape=[jax.ShapeDtypeStruct((n,), i32) for n in sizes],
        in_specs=[SMEM] * len(args) + [ANY] * len(tables),
        out_specs=[SMEM] * len(sizes),
        scratch_shapes=scratch,
        compiler_params=pltpu.CompilerParams(vmem_limit_bytes=3 * MIB),
    )(*args, *tables)


def add(*terms):
    total = terms[0].astype(f32)
    for term in terms[1:]:
        total = total + term.astype(f32)
    return total


def add_head(value, head):
    n = head.shape[0]
    return jnp.concatenate([add(value[:n], head).astype(bf16), value[n:].astype(bf16)])


def add_tail(value, tail):
    n = value.shape[0] - tail.shape[0]
    return jnp.concatenate([value[:n].astype(bf16), add(value[n:], tail).astype(bf16)])


def return_sums(first, sums_of, weights):
    a2h, a2t, b4h, b4t, y2h, y2t = first
    w = next(weights)
    b4h, b4t, a2h, a2t, y2h, y2t, w, (a1, a3, b3, b5, y1, y3) = sums_of(1, (b4h, b4t, a2h, a2t, y2h, y2t, w))
    w = weights.send(w)
    up, down = shift(b4h, "z", 1), shift(b4t, "z", -1)
    ax_p, ax_m = shift(a2h, "x", 1), shift(a2t, "x", -1)
    y_p = shift(y2h, "group", 1)

    up, down, ax_p, ax_m, y_p, y2t, a1, a3, b3, b5 = bar((up, down, ax_p, ax_m, y_p, y2t, a1, a3, b3, b5))
    up, down, ax_p, ax_m, y2t, (a0, b0, b1, b2, b6, b7) = sums_of(2, (up, down, ax_p, ax_m, y2t))
    up, down = shift(add_head(b3, up), "z", 1), shift(add_tail(b5, down), "z", -1)
    ax_p, ax_m = shift(add_head(a1, ax_p), "x", 1), shift(add_tail(a3, ax_m), "x", -1)
    y_m = shift(y2t, "group", -1)

    up, down, y_p, y_m, b2, b6 = bar((up, down, y_p, y_m, b2, b6))
    up, down = add(b2, up).astype(bf16), add(b6, down).astype(bf16)
    up, down = shift(up, "z", 1), shift(down, "z", -1)
    y_p = shift(add_head(y1, y_p), "group", 1)

    def part_a(dz):
        rows = slice(2 * dz, 2 * dz + 2)
        return add(a0[rows], ax_p[rows], ax_m[rows])

    def part_b(dx):
        rows = slice(2 * dx, 2 * dx + 2)
        cross = slice(8 + 2 * dx, 10 + 2 * dx)
        sums = add(b0[rows], up[rows], down[rows], y_p[cross], y_m[cross])
        return jnp.concatenate([sums, add(y_p[rows], y_m[rows])])

    up, down, ax_p, ax_m, y_p, y_m, w = bar((up, down, ax_p, ax_m, y_p, y_m, w))
    w = weights.send(w)
    far = part_a(4).astype(bf16)
    up, down = add(b1, up).astype(bf16), add(b7, down).astype(bf16)
    az_p, az_m = shift(far[:1], "z", 1), shift(far[1:], "z", -1)
    up, down = shift(up, "z", 1), shift(down, "z", -1)
    y_m = shift(add_tail(y3, y_m), "group", -1)
    az_p, az_m = add_head(part_a(3), az_p), add_tail(part_a(5), az_m)
    az_p, az_m = shift(az_p, "z", 1), shift(az_m, "z", -1)
    az_p, az_m = add(part_a(2), az_p).astype(bf16), add(part_a(6), az_m).astype(bf16)
    far = part_b(2).astype(bf16)
    az_p, az_m, far = bar((az_p, az_m, far))
    bx_p, bx_m = shift(far[:2], "x", 1), shift(far[2:], "x", -1)
    az_p, az_m = shift(az_p, "z", 1), shift(az_m, "z", -1)
    bx_p, bx_m = add_head(part_b(1), bx_p), add_tail(part_b(3), bx_m)
    az_p, az_m = add(part_a(1), az_p).astype(bf16), add(part_a(7), az_m).astype(bf16)
    az_p, az_m, bx_p, bx_m = bar((az_p, az_m, bx_p, bx_m))
    bx_p, bx_m = shift(bx_p, "x", 1), shift(bx_m, "x", -1)
    az_p, az_m = shift(az_p, "z", 1), shift(az_m, "z", -1)
    sum_b = add(part_b(0), bx_p, bx_m)
    return add(part_a(0), az_p, az_m, sum_b[2:]), sum_b[:2], w


def body(
    feats,
    neigh,
    pre_act,
    cotan,
    w_self,
    w_neigh,
    send_list,
    send_live,
    cross_list,
    cross_live,
    home_tiles,
    home_target,
    home_source,
    far_tiles,
    far_target,
    far_source,
    far_count,
):
    y, z, x, core = (lax.axis_index(name) for name in AXES)
    meta = jnp.stack([core, z, x, y]).astype(i32)
    first_core = core == 0
    cols = (((1,), (1,)), ((), ()))
    ints = jnp.concatenate(
        [
            (send_live * 2 + send_list).reshape(-1),
            (cross_live * 2 + cross_list).reshape(-1),
            home_target[0, 0],
            home_source[0, 0],
            far_target[0, 0],
            far_source[0, 0],
            far_count[0],
            jnp.zeros((INTS - FC - 1,), i32),
        ]
    )
    row = jnp.stack([ints, shift(ints, "x", -1), shift(ints, "x", 2), shift(ints, "x", 1)])
    row = jnp.stack([row, shift(row, "core", 1)], axis=1)
    words = row[:, :, :CROSS].reshape(2, HALF).astype(bf16)
    cross_words = jnp.pad(row[:, :, CROSS:HT].reshape(1, BLK // 2).astype(bf16), ((0, 0), (0, HALF - BLK // 2)))
    row = row.reshape(-1)

    def join(mine, other):
        low, high = jnp.where(first_core, mine, other), jnp.where(first_core, other, mine)
        return jnp.concatenate([low, high], axis=-1)

    grad_pre = jnp.where(pre_act > 0, cotan, jnp.zeros_like(cotan))
    wn_mine = lax.dynamic_slice_in_dim(w_neigh, core * HALF, HALF)
    wn_other = lax.dynamic_slice_in_dim(w_neigh, (1 - core) * HALF, HALF)
    agg_other = lax.dot_general(grad_pre, wn_other, cols, preferred_element_type=f32).astype(bf16)
    agg_sib = shift(agg_other, "core", 1)
    agg_own = lax.dot_general(grad_pre, wn_mine, cols, preferred_element_type=f32).astype(bf16)
    head = jnp.concatenate([words, cross_words, jnp.zeros((HEAD - 3, HALF), bf16)])
    chunk = join_chunk(head, agg_own, agg_sib)

    far_own, home_own = far_tiles[0, 0], home_tiles[0, 0]
    mine, other = weight_terms(meta, feats, neigh, grad_pre)

    far_both = jnp.concatenate([far_own, shift(far_own, "core", 1)])
    home_sib = shift(home_own, "core", 1)
    chunk, far_both, home_sib, mine, other = bar((chunk, far_both, home_sib, mine, other))
    up1, dn1 = shift(chunk, "z", 1), shift(chunk, "z", -1)
    tiles3, tiles1 = shift(far_both, "x", 1), shift(far_both, "x", -1)
    other = shift(other, "core", 1)
    up1, dn1, chunk, row, mine, other = bar((up1, dn1, chunk, row, mine, other))
    weights = (mine + other).reshape(4 * HALF, HALF + BLK)
    weights = lax.psum_scatter(weights, "group", scatter_dimension=0, tiled=True)
    up2, dn2 = shift(up1, "z", 1), shift(dn1, "z", -1)
    y1 = shift(chunk, "group", 1)
    (picked,) = scalars(pick_kernel, (PICKED,), meta, row)
    up2, dn2, tiles1, tiles3, picked = bar((up2, dn2, tiles1, tiles3, picked))
    up3, dn3 = shift(up2, "z", 1), shift(dn2, "z", -1)
    tiles2h, tiles2t = shift(tiles3[:NT], "x", 1), shift(tiles1[NT:], "x", -1)
    y1, chunk = bar((y1, chunk))
    y3 = shift(chunk, "group", 3)
    up3, dn3, weights = bar((up3, dn3, weights))
    weights = lax.psum_scatter(weights, "z", scatter_dimension=0, tiled=True)
    middle = HEAD + 2 * BLK
    up4, dn4 = shift(up3[:middle], "z", 1), shift(dn3[middle:], "z", -1)
    y3, chunk = bar((y3, chunk))
    y2 = shift(chunk, "group", 2)
    up4, dn4, tiles2h, tiles2t, y2 = bar((up4, dn4, tiles2h, tiles2t, y2))

    def weight_stages(w):
        w = yield w
        w = jnp.pad(w, ((0, 16), (0, 0)))
        w = yield lax.all_gather(w, ("group", "x"), axis=0)
        w = jnp.sum(w.reshape(NY, NX, 48, HALF + BLK)[:, :, :32], axis=1)
        yield lax.all_gather(w, "z", axis=0)

    tile_refs = [far_both, tiles1, tiles3, tiles2h, tiles2t, home_own, home_sib]
    block_refs = [chunk, dn1, dn2, dn3, up4, dn4, up3, up2, up1, y1, y2, y3]
    heads = [chunk, dn1, dn2, dn3, up4, up3, up2, up1, y1, y2, y3]
    (todo,) = scalars(
        list_kernel,
        (3 * LIST,),
        meta,
        row,
        picked,
        tables=heads,
        scratch=[
            pltpu.VMEM((len(heads), HEAD, HALF), bf16),
            pltpu.VMEM((len(heads), HEAD, HALF), i32),
            pltpu.SMEM((len(heads), 8, HALF), i32),
            pltpu.SemaphoreType.DMA((len(heads),)),
        ],
    )

    def sums_of(group, arrived):
        *arrived, now = bar((*arrived, todo))
        return *arrived, tile_sums(group, now, tile_refs, block_refs)

    (first,) = sums_of(0, ())
    sum_a, sum_b, weights = return_sums(first, sums_of, weight_stages(weights))
    self_grad = lax.dot_general(grad_pre, w_self, cols, preferred_element_type=f32)
    weights, sum_b = bar((weights, sum_b))
    other = shift(sum_b, "core", 1)
    weights_sib = shift(weights, "core", 1)

    def rows_of(value):
        return value.transpose(1, 0, 2, 3).reshape(4 * HALF, HALF + BLK)

    weights, weights_sib = rows_of(weights), rows_of(weights_sib)
    sums = join(weights[:, :HALF], weights_sib[:, :HALF])
    bias = join(weights[:2, HALF:].reshape(-1), weights_sib[:2, HALF:].reshape(-1))
    grad_input = self_grad + join(sum_a.reshape(2 * BLK, HALF), other.reshape(2 * BLK, HALF))
    return grad_input.astype(bf16), sums[:512], sums[512:], bias


def solution(mesh):
    fine = Mesh(mesh.devices.reshape(NY, NZ, NX, 2), AXES)
    rows = P(AXES, None)
    part = lambda extra: P("group", DOM, *([None] * extra))
    return jax.shard_map(
        body,
        mesh=fine,
        in_specs=(rows,) * 4
        + (P(), P())
        + (part(1), part(1), part(2), part(2), part(3), part(1), part(1), part(3), part(1), part(1), part(0)),
        out_specs=(rows, P(), P(), P()),
        check_vma=False,
    )
```

```python
import jax
import jax.numpy as jnp
from jax import lax
from jax.experimental import pallas as pl
from jax.experimental.pallas import tpu as pltpu
from jax.sharding import Mesh
from jax.sharding import PartitionSpec as P

AXES = ("group", "z", "x", "core")
DOM = ("z", "x", "core")
NY, NZ, NX = 4, 8, 4
BLK, HALF = 128, 256
NT = 16
SLOTS = 32
bf16, f32, i32 = jnp.bfloat16, jnp.float32, jnp.int32

SEND, CROSS, HT, HS, FT, FS, FC, INTS = 0, 64, 72, 88, 104, 120, 136, 256
HEAD = 16
ENTRIES = 161
LIST = 1 + 2 * ENTRIES
TOTAL = 3 * LIST
HEADS = (0, 1, 2, 3, 4, 6, 7, 8, 9, 10, 11)
PICKED = 1 + 128

GROUPS = (
    ((0, 8), (8, 8), (16, 4), (20, 4), (24, 8), (32, 8)),
    ((0, 16), (16, 16), (32, 8), (40, 8), (48, 16), (64, 16)),
    ((0, 16), (16, 8), (24, 8), (32, 8), (40, 8), (48, 8)),
)
STARTS, SIZES = (0, 40, 120), (40, 80, 56)
MIB = 2**20

VMEM = pl.BlockSpec(memory_space=pltpu.VMEM)
SMEM = pl.BlockSpec(memory_space=pltpu.SMEM)
ANY = pl.BlockSpec(memory_space=pl.ANY)
HBM = pl.BlockSpec(memory_space=pltpu.HBM)


def shift(value, axis, k):
    n = {"group": NY, "z": NZ, "x": NX, "core": 2}[axis]
    return lax.ppermute(value, axis, [(i, (i + k) % n) for i in range(n)])


def pick_kernel(meta, row, out):
    x = meta[2]
    out[0] = 0
    for dx in range(NX):
        for r in range(2):
            base = (dx * 2 + r) * INTS

            @pl.loop(0, jnp.minimum(row[base + FC], NT))
            def _(t, dx=dx, r=r, base=base):
                slot = row[base + FT + t]
                column = ((slot - 2) >> 1) & 3
                here = jnp.where(slot < 66, column == x, dx == 0)

                @pl.when(here)
                def _():
                    n = out[0]
                    out[0] = n + 1
                    out[1 + n] = (dx * 2 + r) * NT + t


def choose(which, options, low, act):
    if len(options) == 1:
        act(options[0])
        return
    cut = len(options) // 2

    @pl.when(which < low + cut)
    def _():
        choose(which, options[:cut], low, act)

    @pl.when(which >= low + cut)
    def _():
        choose(which, options[cut:], low + cut, act)


def list_kernel(meta, row, picked, *refs):
    tile_refs, block_refs = refs[:10], refs[10:22]
    out, tiles, blocks, low, wide, words, sems, tile_sems, block_sems = refs[22:]
    heads = [block_refs[j] for j in HEADS]
    core, z, x, y = (meta[j] for j in range(4))
    copies = [pltpu.make_async_copy(v.at[pl.ds(0, HEAD)], low.at[j], sems.at[j]) for j, v in enumerate(heads)]
    for copy in copies:
        copy.start()
    for copy in copies:
        copy.wait()
    wide[...] = low[...].astype(f32).astype(i32)
    copy = pltpu.make_async_copy(wide.at[:, pl.ds(0, 8)], words, sems.at[0])
    copy.start()
    copy.wait()
    out[TOTAL] = 0
    for group in range(3):
        out[group * LIST] = 0

    def master(slot, dx, r):
        in_dom = slot < 66
        q = jnp.clip(slot - 2, 0, 63)
        dz = ((q >> 3) - z) & 7
        to_x = (((q >> 1) & 3) - x) & 3
        same = ((q & 1) ^ core)
        me = z * 8 + ((x + dx) & 3) * 2 + (core ^ r)
        v = jnp.clip(slot - 66, 0, 7)
        dy = ((v >> 1) - y) & 3
        word = jnp.where(
            in_dom,
            words[dz, to_x >> 1, ((to_x & 1) * 2 + same) * 64 + me],
            words[jnp.where(dy == 0, 0, 11 - dy), 2, (dx * 2 + r) * 8 + y * 2 + (v & 1)],
        )
        k = word & 1
        dz = jnp.where(in_dom, dz, 0)
        to_x = jnp.where(in_dom, to_x, dx)
        same = jnp.where(in_dom, same, r)
        dy = jnp.where(in_dom, 0, dy)
        return word >= 2, dy, dz, to_x, same, k

    def accumulator(slot, dx, r):
        live, dy, dz, to_x, same, k = master(slot, dx, r)
        own = slot < 2
        live = jnp.logical_or(own, live)
        dy, dz = jnp.where(own, 0, dy), jnp.where(own, 0, dz)
        to_x, same = jnp.where(own, dx, to_x), jnp.where(own, r, same)
        k = jnp.where(own, slot, k)
        a = jnp.where(to_x == 0, 120, jnp.where(to_x == 2, 0, 32 + 8 * to_x)) + dz * 2
        middle = jnp.where(dz == 4, 16, 72 + 4 * (dz - 3))
        outer = jnp.where(dz < 3, 136 + 8 * dz, 112 + 8 * dz)
        b = jnp.where((dz - 4) * (dz - 4) < 2, middle, outer) + to_x * 2
        c = jnp.where(dy == 2, 24, jnp.where(dy == 1, 88, 104)) + r * 8 + dx * 2
        return live, jnp.where(dy > 0, c, jnp.where(same == 0, a, b)) + k

    def append(live, tile_ref, options, tile, block_ref, start, place):
        middle, last = place >= STARTS[1], place >= STARTS[2]
        base = jnp.where(last, 2 * LIST, jnp.where(middle, LIST, 0))
        place = place - jnp.where(last, STARTS[2], jnp.where(middle, STARTS[1], 0))
        n, slot = out[base], out[TOTAL]
        out[base + 1 + n] = slot
        out[base + 1 + ENTRIES + n] = place
        out[base] = n + live.astype(i32)
        out[TOTAL] = slot + live.astype(i32)

        @pl.when(live)
        def _():
            at = pl.multiple_of(start, 16)

            def fetch_tile(ref):
                pltpu.make_async_copy(ref.at[tile], tiles.at[slot], tile_sems.at[slot]).start()

            def fetch_block(ref):
                pltpu.make_async_copy(ref.at[pl.ds(at, BLK)], blocks.at[slot], block_sems.at[slot]).start()

            choose(tile_ref, options[0], 0, fetch_tile)
            choose(block_ref, options[1], 0, fetch_block)

    for r in range(2):

        @pl.loop(0, NT)
        def _(t, r=r):
            live, place = accumulator(row[r * INTS + HS + t], 0, r)
            start = HEAD + BLK * (2 * r + row[r * INTS + HT + t])
            append(live, 0, (tile_refs[8 + r : 9 + r], block_refs[:1]), t, 0, start, place)

    @pl.loop(0, picked[0])
    def _(i):
        which = picked[1 + i]
        dx, r, t = which >> 5, (which >> 4) & 1, which & 15
        base = (which >> 4) * INTS
        target_live, dy, dz, _, same, k = master(row[base + FT + t], dx, r)
        source_live, place = accumulator(row[base + FS + t], dx, r)
        far = dz == 4
        block_ref = jnp.where(far, 4 + same, jnp.where(dz > 4, dz + 1, dz))
        block_ref = jnp.where(dy > 0, 12 - dy, block_ref)
        j = jnp.where(far, k, 2 * same + k)
        start = jnp.where(jnp.logical_and(far, same == 1), 0, HEAD) + BLK * j
        live = jnp.logical_and(target_live, source_live)
        append(live, which >> 4, (tile_refs[:8], block_refs), t, block_ref, start, place)

    @pl.loop(0, out[TOTAL])
    def _(slot):
        pltpu.make_async_copy(tile_refs[0].at[0], tiles.at[slot], tile_sems.at[slot]).wait()
        pltpu.make_async_copy(block_refs[0].at[pl.ds(0, BLK)], blocks.at[slot], block_sems.at[slot]).wait()


def list_tiles(meta, row, picked, tile_refs, block_refs):
    n = len(HEADS)
    return pl.pallas_call(
        list_kernel,
        out_shape=[
            jax.ShapeDtypeStruct((TOTAL + 1,), i32),
            jax.ShapeDtypeStruct((ENTRIES, BLK, BLK), bf16),
            jax.ShapeDtypeStruct((ENTRIES, BLK, HALF), bf16),
        ],
        in_specs=[SMEM] * 3 + [ANY] * 22,
        out_specs=[SMEM, HBM, HBM],
        scratch_shapes=[
            pltpu.VMEM((n, HEAD, HALF), bf16),
            pltpu.VMEM((n, HEAD, HALF), i32),
            pltpu.SMEM((n, 8, HALF), i32),
            pltpu.SemaphoreType.DMA((n,)),
            pltpu.SemaphoreType.DMA((ENTRIES,)),
            pltpu.SemaphoreType.DMA((ENTRIES,)),
        ],
        compiler_params=pltpu.CompilerParams(vmem_limit_bytes=3 * MIB),
    )(meta, row, picked, *tile_refs, *block_refs)


bar = lax.optimization_barrier


def tile_product(tile, block):
    return lax.dot_general(tile, block, (((0,), (0,)), ((), ())), preferred_element_type=f32)


def tile_kernel(group, todo, all_tiles, all_blocks, *refs):
    parts, base = GROUPS[group], group * LIST
    outs, (acc, tiles, blocks, tile_sems, block_sems, out_sems) = refs[: len(parts)], refs[len(parts) :]
    n = todo[base]

    def held(c):
        return jnp.clip(n - c * SLOTS, 0, SLOTS)

    def start(c):
        def one(j, _):
            slot = todo[base + 1 + c * SLOTS + j]
            pltpu.make_async_copy(all_tiles.at[slot], tiles.at[j], tile_sems.at[j]).start()
            pltpu.make_async_copy(all_blocks.at[slot], blocks.at[j], block_sems.at[j]).start()
            return 0

        lax.fori_loop(0, held(c), one, 0)

    def finish(c):
        def one(j, _):
            place = todo[base + 1 + ENTRIES + c * SLOTS + j]
            pltpu.make_async_copy(all_tiles.at[0], tiles.at[j], tile_sems.at[j]).wait()
            pltpu.make_async_copy(all_blocks.at[0], blocks.at[j], block_sems.at[j]).wait()
            term = tile_product(tiles[j], blocks[j])
            acc[place] = (acc[place].astype(f32) + term).astype(bf16)
            return 0

        lax.fori_loop(0, held(c), one, 0)

    start(0)

    @pl.loop(0, acc.shape[0])
    def _(b):
        acc[b] = jnp.zeros((BLK, HALF), bf16)

    def step(c, _):
        finish(c)
        start(c + 1)
        return 0

    lax.fori_loop(0, (n + SLOTS - 1) // SLOTS, step, 0)
    copies = [
        pltpu.make_async_copy(acc.at[pl.ds(s, m)], out, out_sems.at[j])
        for j, ((s, m), out) in enumerate(zip(parts, outs))
    ]
    for copy in copies:
        copy.start()
    for copy in copies:
        copy.wait()


def tile_sums(group, todo, all_tiles, all_blocks):
    parts, size = GROUPS[group], SIZES[group]
    return pl.pallas_call(
        lambda *refs: tile_kernel(group, *refs),
        out_shape=[jax.ShapeDtypeStruct((m, BLK, HALF), bf16) for _, m in parts],
        in_specs=[SMEM, HBM, HBM],
        out_specs=[VMEM if group else HBM] * len(parts),
        scratch_shapes=[
            pltpu.VMEM((size, BLK, HALF), bf16),
            pltpu.VMEM((SLOTS, BLK, BLK), bf16),
            pltpu.VMEM((SLOTS, BLK, HALF), bf16),
            pltpu.SemaphoreType.DMA((SLOTS,)),
            pltpu.SemaphoreType.DMA((SLOTS,)),
            pltpu.SemaphoreType.DMA((len(parts),)),
        ],
        compiler_params=pltpu.CompilerParams(vmem_limit_bytes=10 * MIB),
        cost_estimate=pl.CostEstimate(flops=10**9, bytes_accessed=2 * 10**7, transcendentals=0),
    )(todo, all_tiles, all_blocks)


def join_kernel(head, own, sib, out):
    out[:HEAD] = head[...]
    out[HEAD : HEAD + HALF] = own[...]
    out[HEAD + HALF :] = sib[...]


def join_chunk(head, own, sib):
    return pl.pallas_call(
        join_kernel,
        out_shape=jax.ShapeDtypeStruct((HEAD + 2 * HALF, HALF), bf16),
        in_specs=[VMEM] * 3,
        out_specs=VMEM,
        compiler_params=pltpu.CompilerParams(vmem_limit_bytes=4 * MIB),
    )(head, own, sib)


def weight_kernel(meta, grad_pre, feats, neigh, mine, other, source, sums, sems):
    loads = [pltpu.make_async_copy(v, source.at[j], sems.at[j]) for j, v in enumerate((feats, neigh))]
    for load in loads:
        load.start()
    core = meta[0]
    low, high = grad_pre[:, :HALF], grad_pre[:, HALF:]
    for load in loads:
        load.wait()
    stores = []
    for j, (out, from_low) in enumerate(((other, core == 1), (mine, core == 0))):
        part = jnp.where(from_low, low, high)
        bias = jnp.sum(part.astype(f32), axis=0, keepdims=True)
        for g in range(NY):
            cols = source[g // 2, :, (g % 2) * HALF : (g % 2 + 1) * HALF]
            sums[j, g, :, :HALF] = tile_product(cols, part)
            sums[j, g, :, HALF:] = jnp.zeros((HALF, BLK), f32)
            if g == 0:
                sums[j, g, 0:1, HALF:] = bias[:, :BLK]
                sums[j, g, 1:2, HALF:] = bias[:, BLK:]
        stores.append(pltpu.make_async_copy(sums.at[j], out, sems.at[2 + j]))
        stores[-1].start()
    for store in stores:
        store.wait()


def weight_terms(meta, feats, neigh, grad_pre):
    shape = (NY, HALF, HALF + BLK)
    return pl.pallas_call(
        weight_kernel,
        out_shape=[jax.ShapeDtypeStruct(shape, f32)] * 2,
        in_specs=[SMEM, VMEM, HBM, HBM],
        out_specs=[HBM] * 2,
        scratch_shapes=[
            pltpu.VMEM((2, *feats.shape), bf16),
            pltpu.VMEM((2, *shape), f32),
            pltpu.SemaphoreType.DMA((4,)),
        ],
        compiler_params=pltpu.CompilerParams(vmem_limit_bytes=8 * MIB),
    )(meta, grad_pre, feats, neigh)


def agg_kernel(meta, pre_act, cotan, w_neigh, grad_pre, agg_own, agg_other):
    grad = jnp.where(pre_act[...] > 0, cotan[...], jnp.zeros_like(cotan))
    grad_pre[...] = grad
    for out, half in ((agg_other, 1 - meta[0]), (agg_own, meta[0])):
        weight = w_neigh[pl.ds(pl.multiple_of(half * HALF, HALF), HALF), :]
        product = lax.dot_general(grad, weight, (((1,), (1,)), ((), ())), preferred_element_type=f32)
        out[...] = product.astype(bf16)


def agg_terms(meta, pre_act, cotan, w_neigh):
    half = jax.ShapeDtypeStruct((HALF, HALF), bf16)
    return pl.pallas_call(
        agg_kernel,
        out_shape=[jax.ShapeDtypeStruct(pre_act.shape, bf16), half, half],
        in_specs=[SMEM] + [VMEM] * 3,
        out_specs=[VMEM] * 3,
        compiler_params=pltpu.CompilerParams(vmem_limit_bytes=6 * MIB),
    )(meta, pre_act, cotan, w_neigh)


def join_kernel(head, own, sib, out):
    out[:HEAD] = head[...]
    out[HEAD : HEAD + HALF] = own[...]
    out[HEAD + HALF :] = sib[...]


def join_chunk(head, own, sib):
    return pl.pallas_call(
        join_kernel,
        out_shape=jax.ShapeDtypeStruct((HEAD + 2 * HALF, HALF), bf16),
        in_specs=[VMEM] * 3,
        out_specs=VMEM,
        compiler_params=pltpu.CompilerParams(vmem_limit_bytes=4 * MIB),
    )(head, own, sib)


def weight_kernel(meta, feats, neigh, grad_pre, mine, other):
    core = meta[0]
    low, high = grad_pre[:, :HALF], grad_pre[:, HALF:]
    for out, from_low in ((mine, core == 0), (other, core == 1)):
        part = jnp.where(from_low, low, high)
        bias = jnp.sum(part.astype(f32), axis=0, keepdims=True)
        for g in range(NY):
            source = feats if g < 2 else neigh
            cols = source[:, (g % 2) * HALF : (g % 2 + 1) * HALF]
            out[g, :, :HALF] = tile_product(cols, part)
            out[g, :, HALF:] = jnp.zeros((HALF, BLK), f32)
            if g == 0:
                out[g, 0:1, HALF:] = bias[:, :BLK]
                out[g, 1:2, HALF:] = bias[:, BLK:]


def weight_terms(meta, feats, neigh, grad_pre):
    return pl.pallas_call(
        weight_kernel,
        out_shape=[jax.ShapeDtypeStruct((NY, HALF, HALF + BLK), f32)] * 2,
        in_specs=[SMEM] + [VMEM] * 3,
        out_specs=[VMEM] * 2,
        compiler_params=pltpu.CompilerParams(vmem_limit_bytes=10 * MIB),
    )(meta, feats, neigh, grad_pre)


def scalars(kernel, sizes, *args):
    return pl.pallas_call(
        kernel,
        out_shape=[jax.ShapeDtypeStruct((n,), i32) for n in sizes],
        in_specs=[SMEM] * len(args),
        out_specs=[SMEM] * len(sizes),
        compiler_params=pltpu.CompilerParams(vmem_limit_bytes=3 * MIB),
    )(*args)


def add(*terms):
    total = terms[0].astype(f32)
    for term in terms[1:]:
        total = total + term.astype(f32)
    return total


def add_head(value, head):
    n = head.shape[0]
    return jnp.concatenate([add(value[:n], head).astype(bf16), value[n:].astype(bf16)])


def add_tail(value, tail):
    n = value.shape[0] - tail.shape[0]
    return jnp.concatenate([value[:n].astype(bf16), add(value[n:], tail).astype(bf16)])


def return_sums(first, sums_of, weights):
    a2h, a2t, b4h, b4t, y2h, y2t = first
    w = next(weights)
    b4h, b4t, a2h, a2t, y2h, y2t, w, (a1, a3, b3, b5, y1, y3) = sums_of(1, (b4h, b4t, a2h, a2t, y2h, y2t, w))
    w = weights.send(w)
    up, down = shift(b4h, "z", 1), shift(b4t, "z", -1)
    ax_p, ax_m = shift(a2h, "x", 1), shift(a2t, "x", -1)
    y_p = shift(y2h, "group", 1)

    up, down, ax_p, ax_m, y_p, y2t, a1, a3, b3, b5 = bar((up, down, ax_p, ax_m, y_p, y2t, a1, a3, b3, b5))
    up, down, ax_p, ax_m, y2t, (a0, b0, b1, b2, b6, b7) = sums_of(2, (up, down, ax_p, ax_m, y2t))
    up, down = shift(add_head(b3, up), "z", 1), shift(add_tail(b5, down), "z", -1)
    ax_p, ax_m = shift(add_head(a1, ax_p), "x", 1), shift(add_tail(a3, ax_m), "x", -1)
    y_m = shift(y2t, "group", -1)

    up, down, y_p, y_m, b2, b6 = bar((up, down, y_p, y_m, b2, b6))
    up, down = add(b2, up).astype(bf16), add(b6, down).astype(bf16)
    up, down = shift(up, "z", 1), shift(down, "z", -1)
    y_p = shift(add_head(y1, y_p), "group", 1)

    def part_a(dz):
        rows = slice(2 * dz, 2 * dz + 2)
        return add(a0[rows], ax_p[rows], ax_m[rows])

    def part_b(dx):
        rows = slice(2 * dx, 2 * dx + 2)
        cross = slice(8 + 2 * dx, 10 + 2 * dx)
        sums = add(b0[rows], up[rows], down[rows], y_p[cross], y_m[cross])
        return jnp.concatenate([sums, add(y_p[rows], y_m[rows])])

    up, down, ax_p, ax_m, y_p, y_m, w = bar((up, down, ax_p, ax_m, y_p, y_m, w))
    w = weights.send(w)
    far = part_a(4).astype(bf16)
    up, down = add(b1, up).astype(bf16), add(b7, down).astype(bf16)
    az_p, az_m = shift(far[:1], "z", 1), shift(far[1:], "z", -1)
    up, down = shift(up, "z", 1), shift(down, "z", -1)
    y_m = shift(add_tail(y3, y_m), "group", -1)
    az_p, az_m = add_head(part_a(3), az_p), add_tail(part_a(5), az_m)
    az_p, az_m = shift(az_p, "z", 1), shift(az_m, "z", -1)
    az_p, az_m = add(part_a(2), az_p).astype(bf16), add(part_a(6), az_m).astype(bf16)
    far = part_b(2).astype(bf16)
    az_p, az_m, far = bar((az_p, az_m, far))
    bx_p, bx_m = shift(far[:2], "x", 1), shift(far[2:], "x", -1)
    az_p, az_m = shift(az_p, "z", 1), shift(az_m, "z", -1)
    bx_p, bx_m = add_head(part_b(1), bx_p), add_tail(part_b(3), bx_m)
    az_p, az_m = add(part_a(1), az_p).astype(bf16), add(part_a(7), az_m).astype(bf16)
    az_p, az_m, bx_p, bx_m, w = bar((az_p, az_m, bx_p, bx_m, w))
    w_sib = shift(w, "core", 1)
    bx_p, bx_m = shift(bx_p, "x", 1), shift(bx_m, "x", -1)
    az_p, az_m = shift(az_p, "z", 1), shift(az_m, "z", -1)
    sum_b = add(part_b(0), bx_p, bx_m)
    return add(part_a(0), az_p, az_m, sum_b[2:]), sum_b[:2], w, w_sib


def body(
    feats,
    neigh,
    pre_act,
    cotan,
    w_self,
    w_neigh,
    send_list,
    send_live,
    cross_list,
    cross_live,
    home_tiles,
    home_target,
    home_source,
    far_tiles,
    far_target,
    far_source,
    far_count,
):
    y, z, x, core = (lax.axis_index(name) for name in AXES)
    meta = jnp.stack([core, z, x, y]).astype(i32)
    first_core = core == 0
    cols = (((1,), (1,)), ((), ()))
    ints = jnp.concatenate(
        [
            (send_live * 2 + send_list).reshape(-1),
            (cross_live * 2 + cross_list).reshape(-1),
            home_target[0, 0],
            home_source[0, 0],
            far_target[0, 0],
            far_source[0, 0],
            far_count[0],
            jnp.zeros((INTS - FC - 1,), i32),
        ]
    )
    row = jnp.stack([ints, shift(ints, "x", -1), shift(ints, "x", 2), shift(ints, "x", 1)])
    row = jnp.stack([row, shift(row, "core", 1)], axis=1)
    words = row[:, :, :CROSS].reshape(2, HALF).astype(bf16)
    cross_words = jnp.pad(row[:, :, CROSS:HT].reshape(1, BLK // 2).astype(bf16), ((0, 0), (0, HALF - BLK // 2)))
    row = row.reshape(-1)

    def join(mine, other):
        low, high = jnp.where(first_core, mine, other), jnp.where(first_core, other, mine)
        return jnp.concatenate([low, high], axis=-1)

    grad_pre = jnp.where(pre_act > 0, cotan, jnp.zeros_like(cotan))
    wn_mine = lax.dynamic_slice_in_dim(w_neigh, core * HALF, HALF)
    wn_other = lax.dynamic_slice_in_dim(w_neigh, (1 - core) * HALF, HALF)
    agg_other = lax.dot_general(grad_pre, wn_other, cols, preferred_element_type=f32).astype(bf16)
    agg_sib = shift(agg_other, "core", 1)
    agg_own = lax.dot_general(grad_pre, wn_mine, cols, preferred_element_type=f32).astype(bf16)
    head = jnp.concatenate([words, cross_words, jnp.zeros((HEAD - 3, HALF), bf16)])
    chunk = join_chunk(head, agg_own, agg_sib)

    far_own, home_own = far_tiles[0, 0], home_tiles[0, 0]
    mine, other = weight_terms(meta, feats, neigh, grad_pre)

    far_sib, home_sib = shift(far_own, "core", 1), shift(home_own, "core", 1)
    chunk, far_sib, home_sib, mine, other = bar((chunk, far_sib, home_sib, mine, other))
    up1, dn1 = shift(chunk, "z", 1), shift(chunk, "z", -1)
    own3, own1 = shift(far_own, "x", 1), shift(far_own, "x", -1)
    other = shift(other, "core", 1)
    up1, dn1, own1, own3, chunk, row, mine, other, far_sib = bar((up1, dn1, own1, own3, chunk, row, mine, other, far_sib))
    weights = (mine + other).reshape(4 * HALF, HALF + BLK)
    weights = lax.psum_scatter(weights, "group", scatter_dimension=0, tiled=True)
    up2, dn2 = shift(up1, "z", 1), shift(dn1, "z", -1)
    sib3, sib1 = shift(far_sib, "x", 1), shift(far_sib, "x", -1)
    y1 = shift(chunk, "group", 1)
    (picked,) = scalars(pick_kernel, (PICKED,), meta, row)
    up2, dn2, sib1, sib3, own3, y1, chunk, picked = bar((up2, dn2, sib1, sib3, own3, y1, chunk, picked))
    up3, dn3 = shift(up2, "z", 1), shift(dn2, "z", -1)
    own2, sib2 = shift(own3, "x", 1), shift(sib1, "x", -1)
    y3 = shift(chunk, "group", 3)
    up3, dn3, own2, sib2, y3, chunk, weights = bar((up3, dn3, own2, sib2, y3, chunk, weights))
    weights = lax.psum_scatter(weights, "z", scatter_dimension=0, tiled=True)
    middle = HEAD + 2 * BLK
    up4, dn4 = shift(up3[:middle], "z", 1), shift(dn3[middle:], "z", -1)
    y2 = shift(chunk, "group", 2)
    up4, dn4, y2 = bar((up4, dn4, y2))

    def weight_stages(w):
        w = yield w
        w = jnp.pad(w, ((0, 16), (0, 0)))
        w = yield lax.all_gather(w, ("group", "x"), axis=0)
        w = jnp.sum(w.reshape(NY, NX, 48, HALF + BLK)[:, :, :32], axis=1)
        yield lax.all_gather(w, "z", axis=0)

    tile_refs = [far_own, far_sib, own1, sib1, own2, sib2, own3, sib3, home_own, home_sib]
    block_refs = [chunk, dn1, dn2, dn3, up4, dn4, up3, up2, up1, y1, y2, y3]
    todo, all_tiles, all_blocks = list_tiles(meta, row, picked, tile_refs, block_refs)

    def sums_of(group, arrived):
        *arrived, now = bar((*arrived, todo))
        return *arrived, tile_sums(group, now, all_tiles, all_blocks)

    (first,) = sums_of(0, ())
    sum_a, sum_b, weights, weights_sib = return_sums(first, sums_of, weight_stages(weights))
    self_grad = lax.dot_general(grad_pre, w_self, cols, preferred_element_type=f32)
    other = shift(sum_b, "core", 1)

    def rows_of(value):
        return value.transpose(1, 0, 2, 3).reshape(4 * HALF, HALF + BLK)

    weights, weights_sib = rows_of(weights), rows_of(weights_sib)
    sums = join(weights[:, :HALF], weights_sib[:, :HALF])
    bias = join(weights[:2, HALF:].reshape(-1), weights_sib[:2, HALF:].reshape(-1))
    grad_input = self_grad + join(sum_a.reshape(2 * BLK, HALF), other.reshape(2 * BLK, HALF))
    return grad_input.astype(bf16), sums[:512], sums[512:], bias


def solution(mesh):
    fine = Mesh(mesh.devices.reshape(NY, NZ, NX, 2), AXES)
    rows = P(AXES, None)
    part = lambda extra: P("group", DOM, *([None] * extra))
    return jax.shard_map(
        body,
        mesh=fine,
        in_specs=(rows,) * 4
        + (P(), P())
        + (part(1), part(1), part(2), part(2), part(3), part(1), part(1), part(3), part(1), part(1), part(0)),
        out_specs=(rows, P(), P(), P()),
        check_vma=False,
    )
```

```python
import jax
import jax.numpy as jnp
from jax import lax
from jax.experimental import pallas as pl
from jax.experimental.pallas import tpu as pltpu
from jax.sharding import Mesh
from jax.sharding import PartitionSpec as P

AXES = ("group", "z", "x", "core")
DOM = ("z", "x", "core")
NY, NZ, NX = 4, 8, 4
BLK, HALF = 128, 256
NT = 16
SLOTS = 32
bf16, f32, i32 = jnp.bfloat16, jnp.float32, jnp.int32

SEND, CROSS, HT, HS, FT, FS, FC, INTS = 0, 64, 72, 88, 104, 120, 136, 256
HEAD = 16
ENTRIES = 161
LIST = 1 + 3 * ENTRIES
HEADS, TILES, STORE = 48, 64, 1024
PICKED = 1 + 128

GROUPS = (
    ((0, 8), (8, 8), (16, 4), (20, 4), (24, 8), (32, 8)),
    ((0, 16), (16, 16), (32, 8), (40, 8), (48, 16), (64, 16)),
    ((0, 16), (16, 8), (24, 8), (32, 8), (40, 8), (48, 8)),
)
STARTS, SIZES = (0, 40, 120), (40, 80, 56)
MIB = 2**20

VMEM = pl.BlockSpec(memory_space=pltpu.VMEM)
SMEM = pl.BlockSpec(memory_space=pltpu.SMEM)
ANY = pl.BlockSpec(memory_space=pl.ANY)
HBM = pl.BlockSpec(memory_space=pltpu.HBM)


def shift(value, axis, k):
    n = {"group": NY, "z": NZ, "x": NX, "core": 2}[axis]
    return lax.ppermute(value, axis, [(i, (i + k) % n) for i in range(n)])


def pick_kernel(meta, row, out):
    x = meta[2]
    out[0] = 0
    for dx in range(NX):
        for r in range(2):
            base = (dx * 2 + r) * INTS

            @pl.loop(0, jnp.minimum(row[base + FC], NT))
            def _(t, dx=dx, r=r, base=base):
                slot = row[base + FT + t]
                column = ((slot - 2) >> 1) & 3
                here = jnp.where(slot < 66, column == x, dx == 0)

                @pl.when(here)
                def _():
                    n = out[0]
                    out[0] = n + 1
                    out[1 + n] = (dx * 2 + r) * NT + t


def deposit_kernel(plan, *refs):
    sources, store, sems = refs[: len(plan)], refs[-2], refs[-1]
    copies = []

    def copy(source, target):
        copies.append(pltpu.make_async_copy(source, target, sems.at[len(copies)]))
        copies[-1].start()

    for source, (kind, i) in zip(sources, plan):
        if kind == "tiles":
            for half in range(2):
                lanes = pl.ds(half * BLK, BLK)
                copy(source.at[pl.ds(8 * half, 8)], store.at[pl.ds(TILES + 8 * i, 8), :, lanes])
            continue
        start, first = (0, 2) if kind == "tail" else (HEAD, 0)
        if kind != "tail":
            copy(source.at[pl.ds(0, HEAD)], store.at[HEADS + i, pl.ds(0, HEAD)])
        for j in range((source.shape[0] - start) // BLK):
            copy(source.at[pl.ds(start + BLK * j, BLK)], store.at[4 * i + first + j])
    for c in copies:
        c.wait()


def deposit(store, **arrived):
    plan = [(name.rstrip("0123456789"), int(name.strip("abcdefghijklmnopqrstuvwxyz"))) for name in arrived]
    old = [] if store is None else [store]
    return pl.pallas_call(
        lambda *refs: deposit_kernel(plan, *refs),
        out_shape=jax.ShapeDtypeStruct((STORE, BLK, HALF), bf16),
        in_specs=[ANY] * (len(plan) + len(old)),
        out_specs=ANY,
        input_output_aliases={len(plan): 0} if old else {},
        scratch_shapes=[pltpu.SemaphoreType.DMA((5 * len(plan),))],
        compiler_params=pltpu.CompilerParams(vmem_limit_bytes=MIB),
    )(*arrived.values(), *old)


def list_kernel(meta, row, picked, store, out, low, wide, words, sems):
    core, z, x, y = (meta[j] for j in range(4))
    heads = [store.at[HEADS + j, pl.ds(0, HEAD)] for j in range(11)]
    copies = [pltpu.make_async_copy(v, low.at[j], sems.at[j]) for j, v in enumerate(heads)]
    for copy in copies:
        copy.start()
    for copy in copies:
        copy.wait()
    wide[...] = low[...].astype(f32).astype(i32)
    copy = pltpu.make_async_copy(wide.at[:, pl.ds(0, 8)], words, sems.at[0])
    copy.start()
    copy.wait()
    for group in range(3):
        out[group * LIST] = 0

    def master(slot, dx, r):
        in_dom = slot < 66
        q = jnp.clip(slot - 2, 0, 63)
        dz = ((q >> 3) - z) & 7
        to_x = (((q >> 1) & 3) - x) & 3
        same = ((q & 1) ^ core)
        me = z * 8 + ((x + dx) & 3) * 2 + (core ^ r)
        v = jnp.clip(slot - 66, 0, 7)
        dy = ((v >> 1) - y) & 3
        word = jnp.where(
            in_dom,
            words[dz, to_x >> 1, ((to_x & 1) * 2 + same) * 64 + me],
            words[jnp.where(dy == 0, 0, 11 - dy), 2, (dx * 2 + r) * 8 + y * 2 + (v & 1)],
        )
        k = word & 1
        dz = jnp.where(in_dom, dz, 0)
        to_x = jnp.where(in_dom, to_x, dx)
        same = jnp.where(in_dom, same, r)
        dy = jnp.where(in_dom, 0, dy)
        return word >= 2, dy, dz, to_x, same, k

    def accumulator(slot, dx, r):
        live, dy, dz, to_x, same, k = master(slot, dx, r)
        own = slot < 2
        live = jnp.logical_or(own, live)
        dy, dz = jnp.where(own, 0, dy), jnp.where(own, 0, dz)
        to_x, same = jnp.where(own, dx, to_x), jnp.where(own, r, same)
        k = jnp.where(own, slot, k)
        a = jnp.where(to_x == 0, 120, jnp.where(to_x == 2, 0, 32 + 8 * to_x)) + dz * 2
        middle = jnp.where(dz == 4, 16, 72 + 4 * (dz - 3))
        outer = jnp.where(dz < 3, 136 + 8 * dz, 112 + 8 * dz)
        b = jnp.where((dz - 4) * (dz - 4) < 2, middle, outer) + to_x * 2
        c = jnp.where(dy == 2, 24, jnp.where(dy == 1, 88, 104)) + r * 8 + dx * 2
        return live, jnp.where(dy > 0, c, jnp.where(same == 0, a, b)) + k

    def append(live, tile, block, place):
        middle, last = place >= STARTS[1], place >= STARTS[2]
        base = jnp.where(last, 2 * LIST, jnp.where(middle, LIST, 0))
        place = place - jnp.where(last, STARTS[2], jnp.where(middle, STARTS[1], 0))
        n = out[base]
        for j, value in enumerate((tile, block, place)):
            out[base + 1 + ENTRIES * j + n] = value
        out[base] = n + live.astype(i32)

    for r in range(2):

        @pl.loop(0, NT, unroll=4)
        def _(t, r=r):
            live, place = accumulator(row[r * INTS + HS + t], 0, r)
            append(live, (8 + r) * NT + t, 2 * r + row[r * INTS + HT + t], place)

    @pl.loop(0, picked[0])
    def _(i):
        which = picked[1 + i]
        dx, r, t = which >> 5, (which >> 4) & 1, which & 15
        base = (which >> 4) * INTS
        target_live, dy, dz, _, same, k = master(row[base + FT + t], dx, r)
        source_live, place = accumulator(row[base + FS + t], dx, r)
        source = jnp.where(dy > 0, 11 - dy, dz)
        append(jnp.logical_and(target_live, source_live), which, 4 * source + 2 * same + k, place)


def list_tiles(meta, row, picked, store):
    return pl.pallas_call(
        list_kernel,
        out_shape=jax.ShapeDtypeStruct((3 * LIST,), i32),
        in_specs=[SMEM] * 3 + [ANY],
        out_specs=SMEM,
        scratch_shapes=[
            pltpu.VMEM((11, HEAD, HALF), bf16),
            pltpu.VMEM((11, HEAD, HALF), i32),
            pltpu.SMEM((11, 8, HALF), i32),
            pltpu.SemaphoreType.DMA((11,)),
        ],
        compiler_params=pltpu.CompilerParams(vmem_limit_bytes=3 * MIB),
    )(meta, row, picked, store)


bar = lax.optimization_barrier


def tile_product(tile, block):
    return lax.dot_general(tile, block, (((0,), (0,)), ((), ())), preferred_element_type=f32)


def tile_kernel(group, todo, store, *refs):
    parts, base = GROUPS[group], group * LIST
    outs, (acc, tiles, blocks, tile_sems, block_sems, out_sems) = refs[: len(parts)], refs[len(parts) :]
    n = todo[base]

    def held(c):
        return jnp.clip(n - c * SLOTS, 0, SLOTS)

    def start(c):
        def one(j, _):
            i = base + 1 + c * SLOTS + j
            which = todo[i]
            row = TILES + ((which >> 4) << 3) + (which & 7)
            lanes = pl.ds(pl.multiple_of(((which >> 3) & 1) * BLK, BLK), BLK)
            pltpu.make_async_copy(store.at[row, :, lanes], tiles.at[j], tile_sems.at[j]).start()
            pltpu.make_async_copy(store.at[todo[i + ENTRIES]], blocks.at[j], block_sems.at[j]).start()
            return 0

        lax.fori_loop(0, held(c), one, 0)

    def finish(c):
        def one(j, _):
            place = todo[base + 1 + 2 * ENTRIES + c * SLOTS + j]
            pltpu.make_async_copy(store.at[0, :, pl.ds(0, BLK)], tiles.at[j], tile_sems.at[j]).wait()
            pltpu.make_async_copy(store.at[0], blocks.at[j], block_sems.at[j]).wait()
            term = tile_product(tiles[j], blocks[j])
            acc[place] = (acc[place].astype(f32) + term).astype(bf16)
            return 0

        lax.fori_loop(0, held(c), one, 0)

    start(0)

    @pl.loop(0, acc.shape[0])
    def _(b):
        acc[b] = jnp.zeros((BLK, HALF), bf16)

    def step(c, _):
        finish(c)
        start(c + 1)
        return 0

    lax.fori_loop(0, (n + SLOTS - 1) // SLOTS, step, 0)
    copies = [
        pltpu.make_async_copy(acc.at[pl.ds(s, m)], out, out_sems.at[j])
        for j, ((s, m), out) in enumerate(zip(parts, outs))
    ]
    for copy in copies:
        copy.start()
    for copy in copies:
        copy.wait()


def tile_sums(group, todo, store):
    parts, size = GROUPS[group], SIZES[group]
    return pl.pallas_call(
        lambda *refs: tile_kernel(group, *refs),
        out_shape=[jax.ShapeDtypeStruct((m, BLK, HALF), bf16) for _, m in parts],
        in_specs=[SMEM, ANY],
        out_specs=[VMEM if group else HBM] * len(parts),
        scratch_shapes=[
            pltpu.VMEM((size, BLK, HALF), bf16),
            pltpu.VMEM((SLOTS, BLK, BLK), bf16),
            pltpu.VMEM((SLOTS, BLK, HALF), bf16),
            pltpu.SemaphoreType.DMA((SLOTS,)),
            pltpu.SemaphoreType.DMA((SLOTS,)),
            pltpu.SemaphoreType.DMA((len(parts),)),
        ],
        compiler_params=pltpu.CompilerParams(vmem_limit_bytes=10 * MIB),
        cost_estimate=pl.CostEstimate(flops=10**9, bytes_accessed=2 * 10**7, transcendentals=0),
    )(todo, store)


def join_kernel(head, own, sib, out):
    out[:HEAD] = head[...]
    out[HEAD : HEAD + HALF] = own[...]
    out[HEAD + HALF :] = sib[...]


def join_chunk(head, own, sib):
    return pl.pallas_call(
        join_kernel,
        out_shape=jax.ShapeDtypeStruct((HEAD + 2 * HALF, HALF), bf16),
        in_specs=[VMEM] * 3,
        out_specs=VMEM,
        compiler_params=pltpu.CompilerParams(vmem_limit_bytes=4 * MIB),
    )(head, own, sib)


def weight_kernel(meta, grad_pre, feats, neigh, mine, other, source, sums, sems):
    loads = [pltpu.make_async_copy(v, source.at[j], sems.at[j]) for j, v in enumerate((feats, neigh))]
    for load in loads:
        load.start()
    core = meta[0]
    low, high = grad_pre[:, :HALF], grad_pre[:, HALF:]
    for load in loads:
        load.wait()
    stores = []
    for j, (out, from_low) in enumerate(((other, core == 1), (mine, core == 0))):
        part = jnp.where(from_low, low, high)
        bias = jnp.sum(part.astype(f32), axis=0, keepdims=True)
        for g in range(NY):
            cols = source[g // 2, :, (g % 2) * HALF : (g % 2 + 1) * HALF]
            sums[j, g, :, :HALF] = tile_product(cols, part)
            sums[j, g, :, HALF:] = jnp.zeros((HALF, BLK), f32)
            if g == 0:
                sums[j, g, 0:1, HALF:] = bias[:, :BLK]
                sums[j, g, 1:2, HALF:] = bias[:, BLK:]
        stores.append(pltpu.make_async_copy(sums.at[j], out, sems.at[2 + j]))
        stores[-1].start()
    for store in stores:
        store.wait()


def weight_terms(meta, feats, neigh, grad_pre):
    shape = (NY, HALF, HALF + BLK)
    return pl.pallas_call(
        weight_kernel,
        out_shape=[jax.ShapeDtypeStruct(shape, f32)] * 2,
        in_specs=[SMEM, VMEM, HBM, HBM],
        out_specs=[HBM] * 2,
        scratch_shapes=[
            pltpu.VMEM((2, *feats.shape), bf16),
            pltpu.VMEM((2, *shape), f32),
            pltpu.SemaphoreType.DMA((4,)),
        ],
        compiler_params=pltpu.CompilerParams(vmem_limit_bytes=8 * MIB),
    )(meta, grad_pre, feats, neigh)


def agg_kernel(meta, pre_act, cotan, w_neigh, grad_pre, agg_own, agg_other):
    grad = jnp.where(pre_act[...] > 0, cotan[...], jnp.zeros_like(cotan))
    grad_pre[...] = grad
    for out, half in ((agg_other, 1 - meta[0]), (agg_own, meta[0])):
        weight = w_neigh[pl.ds(pl.multiple_of(half * HALF, HALF), HALF), :]
        product = lax.dot_general(grad, weight, (((1,), (1,)), ((), ())), preferred_element_type=f32)
        out[...] = product.astype(bf16)


def agg_terms(meta, pre_act, cotan, w_neigh):
    half = jax.ShapeDtypeStruct((HALF, HALF), bf16)
    return pl.pallas_call(
        agg_kernel,
        out_shape=[jax.ShapeDtypeStruct(pre_act.shape, bf16), half, half],
        in_specs=[SMEM] + [VMEM] * 3,
        out_specs=[VMEM] * 3,
        compiler_params=pltpu.CompilerParams(vmem_limit_bytes=6 * MIB),
    )(meta, pre_act, cotan, w_neigh)


def join_kernel(head, own, sib, out):
    out[:HEAD] = head[...]
    out[HEAD : HEAD + HALF] = own[...]
    out[HEAD + HALF :] = sib[...]


def join_chunk(head, own, sib):
    return pl.pallas_call(
        join_kernel,
        out_shape=jax.ShapeDtypeStruct((HEAD + 2 * HALF, HALF), bf16),
        in_specs=[VMEM] * 3,
        out_specs=VMEM,
        compiler_params=pltpu.CompilerParams(vmem_limit_bytes=4 * MIB),
    )(head, own, sib)


def weight_kernel(meta, feats, neigh, grad_pre, mine, other):
    core = meta[0]
    low, high = grad_pre[:, :HALF], grad_pre[:, HALF:]
    for out, from_low in ((mine, core == 0), (other, core == 1)):
        part = jnp.where(from_low, low, high)
        bias = jnp.sum(part.astype(f32), axis=0, keepdims=True)
        for g in range(NY):
            source = feats if g < 2 else neigh
            cols = source[:, (g % 2) * HALF : (g % 2 + 1) * HALF]
            out[g, :, :HALF] = tile_product(cols, part)
            out[g, :, HALF:] = jnp.zeros((HALF, BLK), f32)
            if g == 0:
                out[g, 0:1, HALF:] = bias[:, :BLK]
                out[g, 1:2, HALF:] = bias[:, BLK:]


def weight_terms(meta, feats, neigh, grad_pre):
    return pl.pallas_call(
        weight_kernel,
        out_shape=[jax.ShapeDtypeStruct((NY, HALF, HALF + BLK), f32)] * 2,
        in_specs=[SMEM] + [VMEM] * 3,
        out_specs=[VMEM] * 2,
        compiler_params=pltpu.CompilerParams(vmem_limit_bytes=10 * MIB),
    )(meta, feats, neigh, grad_pre)


def scalars(kernel, sizes, *args):
    return pl.pallas_call(
        kernel,
        out_shape=[jax.ShapeDtypeStruct((n,), i32) for n in sizes],
        in_specs=[SMEM] * len(args),
        out_specs=[SMEM] * len(sizes),
        compiler_params=pltpu.CompilerParams(vmem_limit_bytes=3 * MIB),
    )(*args)


def add(*terms):
    total = terms[0].astype(f32)
    for term in terms[1:]:
        total = total + term.astype(f32)
    return total


def add_head(value, head):
    n = head.shape[0]
    return jnp.concatenate([add(value[:n], head).astype(bf16), value[n:].astype(bf16)])


def add_tail(value, tail):
    n = value.shape[0] - tail.shape[0]
    return jnp.concatenate([value[:n].astype(bf16), add(value[n:], tail).astype(bf16)])


def return_sums(first, sums_of, weights):
    a2h, a2t, b4h, b4t, y2h, y2t = first
    w = next(weights)
    b4h, b4t, a2h, a2t, y2h, y2t, w, (a1, a3, b3, b5, y1, y3) = sums_of(1, (b4h, b4t, a2h, a2t, y2h, y2t, w))
    w = weights.send(w)
    up, down = shift(b4h, "z", 1), shift(b4t, "z", -1)
    ax_p, ax_m = shift(a2h, "x", 1), shift(a2t, "x", -1)
    y_p = shift(y2h, "group", 1)

    up, down, ax_p, ax_m, y_p, y2t, a1, a3, b3, b5 = bar((up, down, ax_p, ax_m, y_p, y2t, a1, a3, b3, b5))
    up, down, ax_p, ax_m, y2t, (a0, b0, b1, b2, b6, b7) = sums_of(2, (up, down, ax_p, ax_m, y2t))
    up, down = shift(add_head(b3, up), "z", 1), shift(add_tail(b5, down), "z", -1)
    ax_p, ax_m = shift(add_head(a1, ax_p), "x", 1), shift(add_tail(a3, ax_m), "x", -1)
    y_m = shift(y2t, "group", -1)

    up, down, y_p, y_m, b2, b6 = bar((up, down, y_p, y_m, b2, b6))
    up, down = add(b2, up).astype(bf16), add(b6, down).astype(bf16)
    up, down = shift(up, "z", 1), shift(down, "z", -1)
    y_p = shift(add_head(y1, y_p), "group", 1)

    def part_a(dz):
        rows = slice(2 * dz, 2 * dz + 2)
        return add(a0[rows], ax_p[rows], ax_m[rows])

    def part_b(dx):
        rows = slice(2 * dx, 2 * dx + 2)
        cross = slice(8 + 2 * dx, 10 + 2 * dx)
        sums = add(b0[rows], up[rows], down[rows], y_p[cross], y_m[cross])
        return jnp.concatenate([sums, add(y_p[rows], y_m[rows])])

    up, down, ax_p, ax_m, y_p, y_m, w = bar((up, down, ax_p, ax_m, y_p, y_m, w))
    w = weights.send(w)
    far = part_a(4).astype(bf16)
    up, down = add(b1, up).astype(bf16), add(b7, down).astype(bf16)
    az_p, az_m = shift(far[:1], "z", 1), shift(far[1:], "z", -1)
    up, down = shift(up, "z", 1), shift(down, "z", -1)
    y_m = shift(add_tail(y3, y_m), "group", -1)
    az_p, az_m = add_head(part_a(3), az_p), add_tail(part_a(5), az_m)
    az_p, az_m = shift(az_p, "z", 1), shift(az_m, "z", -1)
    az_p, az_m = add(part_a(2), az_p).astype(bf16), add(part_a(6), az_m).astype(bf16)
    far = part_b(2).astype(bf16)
    az_p, az_m, far = bar((az_p, az_m, far))
    bx_p, bx_m = shift(far[:2], "x", 1), shift(far[2:], "x", -1)
    az_p, az_m = shift(az_p, "z", 1), shift(az_m, "z", -1)
    bx_p, bx_m = add_head(part_b(1), bx_p), add_tail(part_b(3), bx_m)
    az_p, az_m = add(part_a(1), az_p).astype(bf16), add(part_a(7), az_m).astype(bf16)
    az_p, az_m, bx_p, bx_m, w = bar((az_p, az_m, bx_p, bx_m, w))
    w_sib = shift(w, "core", 1)
    bx_p, bx_m = shift(bx_p, "x", 1), shift(bx_m, "x", -1)
    az_p, az_m = shift(az_p, "z", 1), shift(az_m, "z", -1)
    sum_b = add(part_b(0), bx_p, bx_m)
    return add(part_a(0), az_p, az_m, sum_b[2:]), sum_b[:2], w, w_sib


def body(
    feats,
    neigh,
    pre_act,
    cotan,
    w_self,
    w_neigh,
    send_list,
    send_live,
    cross_list,
    cross_live,
    home_tiles,
    home_target,
    home_source,
    far_tiles,
    far_target,
    far_source,
    far_count,
):
    y, z, x, core = (lax.axis_index(name) for name in AXES)
    meta = jnp.stack([core, z, x, y]).astype(i32)
    first_core = core == 0
    cols = (((1,), (1,)), ((), ()))
    ints = jnp.concatenate(
        [
            (send_live * 2 + send_list).reshape(-1),
            (cross_live * 2 + cross_list).reshape(-1),
            home_target[0, 0],
            home_source[0, 0],
            far_target[0, 0],
            far_source[0, 0],
            far_count[0],
            jnp.zeros((INTS - FC - 1,), i32),
        ]
    )
    row = jnp.stack([ints, shift(ints, "x", -1), shift(ints, "x", 2), shift(ints, "x", 1)])
    row = jnp.stack([row, shift(row, "core", 1)], axis=1)
    words = row[:, :, :CROSS].reshape(2, HALF).astype(bf16)
    cross_words = jnp.pad(row[:, :, CROSS:HT].reshape(1, BLK // 2).astype(bf16), ((0, 0), (0, HALF - BLK // 2)))
    row = row.reshape(-1)

    def join(mine, other):
        low, high = jnp.where(first_core, mine, other), jnp.where(first_core, other, mine)
        return jnp.concatenate([low, high], axis=-1)

    grad_pre = jnp.where(pre_act > 0, cotan, jnp.zeros_like(cotan))
    wn_mine = lax.dynamic_slice_in_dim(w_neigh, core * HALF, HALF)
    wn_other = lax.dynamic_slice_in_dim(w_neigh, (1 - core) * HALF, HALF)
    agg_other = lax.dot_general(grad_pre, wn_other, cols, preferred_element_type=f32).astype(bf16)
    agg_sib = shift(agg_other, "core", 1)
    agg_own = lax.dot_general(grad_pre, wn_mine, cols, preferred_element_type=f32).astype(bf16)
    head = jnp.concatenate([words, cross_words, jnp.zeros((HEAD - 3, HALF), bf16)])
    chunk = join_chunk(head, agg_own, agg_sib)

    far_own, home_own = far_tiles[0, 0], home_tiles[0, 0]
    mine, other = weight_terms(meta, feats, neigh, grad_pre)

    far_sib, home_sib = shift(far_own, "core", 1), shift(home_own, "core", 1)
    chunk, far_sib, home_sib, mine, other = bar((chunk, far_sib, home_sib, mine, other))
    up1, dn1 = shift(chunk, "z", 1), shift(chunk, "z", -1)
    own3, own1 = shift(far_own, "x", 1), shift(far_own, "x", -1)
    other = shift(other, "core", 1)
    up1, dn1, own1, own3, chunk, row, mine, other, far_sib = bar((up1, dn1, own1, own3, chunk, row, mine, other, far_sib))
    store = deposit(None, chunk0=chunk, tiles0=far_own, tiles1=far_sib, tiles8=home_own, tiles9=home_sib)
    store = deposit(store, chunk7=up1, chunk1=dn1, tiles2=own1, tiles6=own3)
    weights = (mine + other).reshape(4 * HALF, HALF + BLK)
    weights = lax.psum_scatter(weights, "group", scatter_dimension=0, tiled=True)
    up2, dn2 = shift(up1, "z", 1), shift(dn1, "z", -1)
    sib3, sib1 = shift(far_sib, "x", 1), shift(far_sib, "x", -1)
    y1 = shift(chunk, "group", 1)
    (picked,) = scalars(pick_kernel, (PICKED,), meta, row)
    up2, dn2, sib1, sib3, own3, y1, chunk, picked, store = bar((up2, dn2, sib1, sib3, own3, y1, chunk, picked, store))
    store = deposit(store, chunk6=up2, chunk2=dn2, tiles3=sib1, tiles7=sib3, chunk8=y1)
    up3, dn3 = shift(up2, "z", 1), shift(dn2, "z", -1)
    own2, sib2 = shift(own3, "x", 1), shift(sib1, "x", -1)
    y3 = shift(chunk, "group", 3)
    up3, dn3, own2, sib2, y3, chunk, weights, store = bar((up3, dn3, own2, sib2, y3, chunk, weights, store))
    store = deposit(store, chunk5=up3, chunk3=dn3, tiles4=own2, tiles5=sib2, chunk10=y3)
    weights = lax.psum_scatter(weights, "z", scatter_dimension=0, tiled=True)
    middle = HEAD + 2 * BLK
    up4, dn4 = shift(up3[:middle], "z", 1), shift(dn3[middle:], "z", -1)
    y2 = shift(chunk, "group", 2)
    up4, dn4, y2, store = bar((up4, dn4, y2, store))
    store = deposit(store, chunk4=up4, tail4=dn4, chunk9=y2)
    todo = list_tiles(meta, row, picked, store)

    def weight_stages(w):
        w = yield w
        w = jnp.pad(w, ((0, 16), (0, 0)))
        w = yield lax.all_gather(w, ("group", "x"), axis=0)
        w = jnp.sum(w.reshape(NY, NX, 48, HALF + BLK)[:, :, :32], axis=1)
        yield lax.all_gather(w, "z", axis=0)

    def sums_of(group, arrived):
        *arrived, now = bar((*arrived, todo))
        return *arrived, tile_sums(group, now, store)

    (first,) = sums_of(0, ())
    sum_a, sum_b, weights, weights_sib = return_sums(first, sums_of, weight_stages(weights))
    self_grad = lax.dot_general(grad_pre, w_self, cols, preferred_element_type=f32)
    other = shift(sum_b, "core", 1)

    def rows_of(value):
        return value.transpose(1, 0, 2, 3).reshape(4 * HALF, HALF + BLK)

    weights, weights_sib = rows_of(weights), rows_of(weights_sib)
    sums = join(weights[:, :HALF], weights_sib[:, :HALF])
    bias = join(weights[:2, HALF:].reshape(-1), weights_sib[:2, HALF:].reshape(-1))
    grad_input = self_grad + join(sum_a.reshape(2 * BLK, HALF), other.reshape(2 * BLK, HALF))
    return grad_input.astype(bf16), sums[:512], sums[512:], bias


def solution(mesh):
    fine = Mesh(mesh.devices.reshape(NY, NZ, NX, 2), AXES)
    rows = P(AXES, None)
    part = lambda extra: P("group", DOM, *([None] * extra))
    return jax.shard_map(
        body,
        mesh=fine,
        in_specs=(rows,) * 4
        + (P(), P())
        + (part(1), part(1), part(2), part(2), part(3), part(1), part(1), part(3), part(1), part(1), part(0)),
        out_specs=(rows, P(), P(), P()),
        check_vma=False,
    )
```

```python
import jax
import jax.numpy as jnp
from jax import lax
from jax.experimental import pallas as pl
from jax.experimental.pallas import tpu as pltpu
from jax.sharding import Mesh
from jax.sharding import PartitionSpec as P

AXES = ("group", "z", "x", "core")
DOM = ("z", "x", "core")
NY, NZ, NX = 4, 8, 4
BLK, HALF = 128, 256
NT = 16
SLOTS = 32
bf16, f32, i32 = jnp.bfloat16, jnp.float32, jnp.int32

SEND, CROSS, HT, HS, FT, FS, FC, INTS = 0, 64, 72, 88, 104, 120, 136, 256
HEAD = 16
ENTRIES = 161
LIST = 1 + 3 * ENTRIES
HEADS, TILES, STORE = 48, 64, 1024
PICKED = 1 + 128

GROUPS = (
    ((0, 8), (8, 8), (16, 4), (20, 4), (24, 8), (32, 8)),
    ((0, 16), (16, 16), (32, 8), (40, 8), (48, 16), (64, 16)),
    ((0, 16), (16, 8), (24, 8), (32, 8), (40, 8), (48, 8)),
)
STARTS, SIZES = (0, 40, 120), (40, 80, 56)
MIB = 2**20

VMEM = pl.BlockSpec(memory_space=pltpu.VMEM)
SMEM = pl.BlockSpec(memory_space=pltpu.SMEM)
ANY = pl.BlockSpec(memory_space=pl.ANY)
HBM = pl.BlockSpec(memory_space=pltpu.HBM)


def shift(value, axis, k):
    n = {"group": NY, "z": NZ, "x": NX, "core": 2}[axis]
    return lax.ppermute(value, axis, [(i, (i + k) % n) for i in range(n)])


def pick_kernel(meta, row, out):
    x = meta[2]
    out[0] = 0
    for dx in range(NX):
        for r in range(2):
            base = (dx * 2 + r) * INTS

            @pl.loop(0, jnp.minimum(row[base + FC], NT))
            def _(t, dx=dx, r=r, base=base):
                slot = row[base + FT + t]
                column = ((slot - 2) >> 1) & 3
                here = jnp.where(slot < 66, column == x, dx == 0)

                @pl.when(here)
                def _():
                    n = out[0]
                    out[0] = n + 1
                    out[1 + n] = (dx * 2 + r) * NT + t


def deposit_kernel(plan, *refs):
    sources, store, sems = refs[: len(plan)], refs[-2], refs[-1]
    copies = []

    def copy(source, target):
        copies.append(pltpu.make_async_copy(source, target, sems.at[len(copies)]))
        copies[-1].start()

    for source, (kind, i) in zip(sources, plan):
        if kind == "tiles":
            for half in range(2):
                lanes = pl.ds(half * BLK, BLK)
                copy(source.at[pl.ds(8 * half, 8)], store.at[pl.ds(TILES + 8 * i, 8), :, lanes])
            continue
        start, first = (0, 2) if kind == "tail" else (HEAD, 0)
        if kind != "tail":
            copy(source.at[pl.ds(0, HEAD)], store.at[HEADS + i, pl.ds(0, HEAD)])
        for j in range((source.shape[0] - start) // BLK):
            copy(source.at[pl.ds(start + BLK * j, BLK)], store.at[4 * i + first + j])
    for c in copies:
        c.wait()


def deposit(store, **arrived):
    plan = [(name.rstrip("0123456789"), int(name.strip("abcdefghijklmnopqrstuvwxyz"))) for name in arrived]
    old = [] if store is None else [store]
    return pl.pallas_call(
        lambda *refs: deposit_kernel(plan, *refs),
        out_shape=jax.ShapeDtypeStruct((STORE, BLK, HALF), bf16),
        in_specs=[ANY] * (len(plan) + len(old)),
        out_specs=ANY,
        input_output_aliases={len(plan): 0} if old else {},
        scratch_shapes=[pltpu.SemaphoreType.DMA((5 * len(plan),))],
        compiler_params=pltpu.CompilerParams(vmem_limit_bytes=MIB),
    )(*arrived.values(), *old)


def list_kernel(meta, row, picked, store, out, low, wide, words, sems):
    core, z, x, y = (meta[j] for j in range(4))
    heads = [store.at[HEADS + j, pl.ds(0, HEAD)] for j in range(11)]
    copies = [pltpu.make_async_copy(v, low.at[j], sems.at[j]) for j, v in enumerate(heads)]
    for copy in copies:
        copy.start()
    for copy in copies:
        copy.wait()
    wide[...] = low[...].astype(f32).astype(i32)
    copy = pltpu.make_async_copy(wide.at[:, pl.ds(0, 8)], words, sems.at[0])
    copy.start()
    copy.wait()
    for group in range(3):
        out[group * LIST] = 0

    def master(slot, dx, r):
        in_dom = slot < 66
        q = jnp.clip(slot - 2, 0, 63)
        dz = ((q >> 3) - z) & 7
        to_x = (((q >> 1) & 3) - x) & 3
        same = ((q & 1) ^ core)
        me = z * 8 + ((x + dx) & 3) * 2 + (core ^ r)
        v = jnp.clip(slot - 66, 0, 7)
        dy = ((v >> 1) - y) & 3
        word = jnp.where(
            in_dom,
            words[dz, to_x >> 1, ((to_x & 1) * 2 + same) * 64 + me],
            words[jnp.where(dy == 0, 0, 11 - dy), 2, (dx * 2 + r) * 8 + y * 2 + (v & 1)],
        )
        k = word & 1
        dz = jnp.where(in_dom, dz, 0)
        to_x = jnp.where(in_dom, to_x, dx)
        same = jnp.where(in_dom, same, r)
        dy = jnp.where(in_dom, 0, dy)
        return word >= 2, dy, dz, to_x, same, k

    def accumulator(slot, dx, r):
        live, dy, dz, to_x, same, k = master(slot, dx, r)
        own = slot < 2
        live = jnp.logical_or(own, live)
        dy, dz = jnp.where(own, 0, dy), jnp.where(own, 0, dz)
        to_x, same = jnp.where(own, dx, to_x), jnp.where(own, r, same)
        k = jnp.where(own, slot, k)
        a = jnp.where(to_x == 0, 120, jnp.where(to_x == 2, 0, 32 + 8 * to_x)) + dz * 2
        middle = jnp.where(dz == 4, 16, 72 + 4 * (dz - 3))
        outer = jnp.where(dz < 3, 136 + 8 * dz, 112 + 8 * dz)
        b = jnp.where((dz - 4) * (dz - 4) < 2, middle, outer) + to_x * 2
        c = jnp.where(dy == 2, 24, jnp.where(dy == 1, 88, 104)) + r * 8 + dx * 2
        return live, jnp.where(dy > 0, c, jnp.where(same == 0, a, b)) + k

    def append(live, tile, block, place):
        middle, last = place >= STARTS[1], place >= STARTS[2]
        base = jnp.where(last, 2 * LIST, jnp.where(middle, LIST, 0))
        place = place - jnp.where(last, STARTS[2], jnp.where(middle, STARTS[1], 0))
        n = out[base]
        for j, value in enumerate((tile, block, place)):
            out[base + 1 + ENTRIES * j + n] = value
        out[base] = n + live.astype(i32)

    for r in range(2):

        @pl.loop(0, NT, unroll=4)
        def _(t, r=r):
            live, place = accumulator(row[r * INTS + HS + t], 0, r)
            append(live, (8 + r) * NT + t, 2 * r + row[r * INTS + HT + t], place)

    @pl.loop(0, picked[0])
    def _(i):
        which = picked[1 + i]
        dx, r, t = which >> 5, (which >> 4) & 1, which & 15
        base = (which >> 4) * INTS
        target_live, dy, dz, _, same, k = master(row[base + FT + t], dx, r)
        source_live, place = accumulator(row[base + FS + t], dx, r)
        source = jnp.where(dy > 0, 11 - dy, dz)
        append(jnp.logical_and(target_live, source_live), which, 4 * source + 2 * same + k, place)


def list_tiles(meta, row, picked, store):
    return pl.pallas_call(
        list_kernel,
        out_shape=jax.ShapeDtypeStruct((3 * LIST,), i32),
        in_specs=[SMEM] * 3 + [ANY],
        out_specs=SMEM,
        scratch_shapes=[
            pltpu.VMEM((11, HEAD, HALF), bf16),
            pltpu.VMEM((11, HEAD, HALF), i32),
            pltpu.SMEM((11, 8, HALF), i32),
            pltpu.SemaphoreType.DMA((11,)),
        ],
        compiler_params=pltpu.CompilerParams(vmem_limit_bytes=3 * MIB),
    )(meta, row, picked, store)


bar = lax.optimization_barrier


def tile_product(tile, block):
    return lax.dot_general(tile, block, (((0,), (0,)), ((), ())), preferred_element_type=f32)


def tile_kernel(group, todo, store, *refs):
    parts, base = GROUPS[group], group * LIST
    outs, (acc, tiles, blocks, tile_sems, block_sems, out_sems) = refs[: len(parts)], refs[len(parts) :]
    n = todo[base]

    def held(c):
        return jnp.clip(n - c * SLOTS, 0, SLOTS)

    def start(c):
        def one(j, _):
            i = base + 1 + c * SLOTS + j
            which = todo[i]
            row = TILES + ((which >> 4) << 3) + (which & 7)
            lanes = pl.ds(pl.multiple_of(((which >> 3) & 1) * BLK, BLK), BLK)
            pltpu.make_async_copy(store.at[row, :, lanes], tiles.at[j], tile_sems.at[j]).start()
            pltpu.make_async_copy(store.at[todo[i + ENTRIES]], blocks.at[j], block_sems.at[j]).start()
            return 0

        lax.fori_loop(0, held(c), one, 0)

    def finish(c):
        def one(j, _):
            place = todo[base + 1 + 2 * ENTRIES + c * SLOTS + j]
            pltpu.make_async_copy(store.at[0, :, pl.ds(0, BLK)], tiles.at[j], tile_sems.at[j]).wait()
            pltpu.make_async_copy(store.at[0], blocks.at[j], block_sems.at[j]).wait()
            term = tile_product(tiles[j], blocks[j])
            acc[place] = (acc[place].astype(f32) + term).astype(bf16)
            return 0

        lax.fori_loop(0, held(c), one, 0)

    start(0)

    @pl.loop(0, acc.shape[0])
    def _(b):
        acc[b] = jnp.zeros((BLK, HALF), bf16)

    def step(c, _):
        finish(c)
        start(c + 1)
        return 0

    lax.fori_loop(0, (n + SLOTS - 1) // SLOTS, step, 0)
    copies = [
        pltpu.make_async_copy(acc.at[pl.ds(s, m)], out, out_sems.at[j])
        for j, ((s, m), out) in enumerate(zip(parts, outs))
    ]
    for copy in copies:
        copy.start()
    for copy in copies:
        copy.wait()


def tile_sums(group, todo, store):
    parts, size = GROUPS[group], SIZES[group]
    return pl.pallas_call(
        lambda *refs: tile_kernel(group, *refs),
        out_shape=[jax.ShapeDtypeStruct((m, BLK, HALF), bf16) for _, m in parts],
        in_specs=[SMEM, ANY],
        out_specs=[VMEM if group else HBM] * len(parts),
        scratch_shapes=[
            pltpu.VMEM((size, BLK, HALF), bf16),
            pltpu.VMEM((SLOTS, BLK, BLK), bf16),
            pltpu.VMEM((SLOTS, BLK, HALF), bf16),
            pltpu.SemaphoreType.DMA((SLOTS,)),
            pltpu.SemaphoreType.DMA((SLOTS,)),
            pltpu.SemaphoreType.DMA((len(parts),)),
        ],
        compiler_params=pltpu.CompilerParams(vmem_limit_bytes=10 * MIB),
        cost_estimate=pl.CostEstimate(flops=10**9, bytes_accessed=2 * 10**7, transcendentals=0),
    )(todo, store)


def join_kernel(head, own, sib, out):
    out[:HEAD] = head[...]
    out[HEAD : HEAD + HALF] = own[...]
    out[HEAD + HALF :] = sib[...]


def join_chunk(head, own, sib):
    return pl.pallas_call(
        join_kernel,
        out_shape=jax.ShapeDtypeStruct((HEAD + 2 * HALF, HALF), bf16),
        in_specs=[VMEM] * 3,
        out_specs=VMEM,
        compiler_params=pltpu.CompilerParams(vmem_limit_bytes=4 * MIB),
    )(head, own, sib)


def weight_kernel(meta, grad_pre, feats, neigh, mine, other, source, sums, sems):
    loads = [pltpu.make_async_copy(v, source.at[j], sems.at[j]) for j, v in enumerate((feats, neigh))]
    for load in loads:
        load.start()
    core = meta[0]
    low, high = grad_pre[:, :HALF], grad_pre[:, HALF:]
    for load in loads:
        load.wait()
    stores = []
    for j, (out, from_low) in enumerate(((other, core == 1), (mine, core == 0))):
        part = jnp.where(from_low, low, high)
        bias = jnp.sum(part.astype(f32), axis=0, keepdims=True)
        for g in range(NY):
            cols = source[g // 2, :, (g % 2) * HALF : (g % 2 + 1) * HALF]
            sums[j, g, :, :HALF] = tile_product(cols, part)
            sums[j, g, :, HALF:] = jnp.zeros((HALF, BLK), f32)
            if g == 0:
                sums[j, g, 0:1, HALF:] = bias[:, :BLK]
                sums[j, g, 1:2, HALF:] = bias[:, BLK:]
        stores.append(pltpu.make_async_copy(sums.at[j], out, sems.at[2 + j]))
        stores[-1].start()
    for store in stores:
        store.wait()


def weight_terms(meta, feats, neigh, grad_pre):
    shape = (NY, HALF, HALF + BLK)
    return pl.pallas_call(
        weight_kernel,
        out_shape=[jax.ShapeDtypeStruct(shape, f32)] * 2,
        in_specs=[SMEM, VMEM, HBM, HBM],
        out_specs=[HBM] * 2,
        scratch_shapes=[
            pltpu.VMEM((2, *feats.shape), bf16),
            pltpu.VMEM((2, *shape), f32),
            pltpu.SemaphoreType.DMA((4,)),
        ],
        compiler_params=pltpu.CompilerParams(vmem_limit_bytes=8 * MIB),
    )(meta, grad_pre, feats, neigh)


def agg_kernel(meta, pre_act, cotan, w_neigh, grad_pre, agg_own, agg_other):
    grad = jnp.where(pre_act[...] > 0, cotan[...], jnp.zeros_like(cotan))
    grad_pre[...] = grad
    for out, half in ((agg_other, 1 - meta[0]), (agg_own, meta[0])):
        weight = w_neigh[pl.ds(pl.multiple_of(half * HALF, HALF), HALF), :]
        product = lax.dot_general(grad, weight, (((1,), (1,)), ((), ())), preferred_element_type=f32)
        out[...] = product.astype(bf16)


def agg_terms(meta, pre_act, cotan, w_neigh):
    half = jax.ShapeDtypeStruct((HALF, HALF), bf16)
    return pl.pallas_call(
        agg_kernel,
        out_shape=[jax.ShapeDtypeStruct(pre_act.shape, bf16), half, half],
        in_specs=[SMEM] + [VMEM] * 3,
        out_specs=[VMEM] * 3,
        compiler_params=pltpu.CompilerParams(vmem_limit_bytes=6 * MIB),
    )(meta, pre_act, cotan, w_neigh)


def join_kernel(head, own, sib, out):
    out[:HEAD] = head[...]
    out[HEAD : HEAD + HALF] = own[...]
    out[HEAD + HALF :] = sib[...]


def join_chunk(head, own, sib):
    return pl.pallas_call(
        join_kernel,
        out_shape=jax.ShapeDtypeStruct((HEAD + 2 * HALF, HALF), bf16),
        in_specs=[VMEM] * 3,
        out_specs=VMEM,
        compiler_params=pltpu.CompilerParams(vmem_limit_bytes=4 * MIB),
    )(head, own, sib)


def weight_kernel(meta, feats, neigh, grad_pre, mine, other):
    core = meta[0]
    low, high = grad_pre[:, :HALF], grad_pre[:, HALF:]
    for out, from_low in ((mine, core == 0), (other, core == 1)):
        part = jnp.where(from_low, low, high)
        bias = jnp.sum(part.astype(f32), axis=0, keepdims=True)
        for g in range(NY):
            source = feats if g < 2 else neigh
            cols = source[:, (g % 2) * HALF : (g % 2 + 1) * HALF]
            out[g, :, :HALF] = tile_product(cols, part)
            out[g, :, HALF:] = jnp.zeros((HALF, BLK), f32)
            if g == 0:
                out[g, 0:1, HALF:] = bias[:, :BLK]
                out[g, 1:2, HALF:] = bias[:, BLK:]


def weight_terms(meta, feats, neigh, grad_pre):
    return pl.pallas_call(
        weight_kernel,
        out_shape=[jax.ShapeDtypeStruct((NY, HALF, HALF + BLK), f32)] * 2,
        in_specs=[SMEM] + [VMEM] * 3,
        out_specs=[VMEM] * 2,
        compiler_params=pltpu.CompilerParams(vmem_limit_bytes=10 * MIB),
    )(meta, feats, neigh, grad_pre)


def scalars(kernel, sizes, *args):
    return pl.pallas_call(
        kernel,
        out_shape=[jax.ShapeDtypeStruct((n,), i32) for n in sizes],
        in_specs=[SMEM] * len(args),
        out_specs=[SMEM] * len(sizes),
        compiler_params=pltpu.CompilerParams(vmem_limit_bytes=3 * MIB),
    )(*args)


def add(*terms):
    total = terms[0].astype(f32)
    for term in terms[1:]:
        total = total + term.astype(f32)
    return total


def add_head(value, head):
    n = head.shape[0]
    return jnp.concatenate([add(value[:n], head).astype(bf16), value[n:].astype(bf16)])


def add_tail(value, tail):
    n = value.shape[0] - tail.shape[0]
    return jnp.concatenate([value[:n].astype(bf16), add(value[n:], tail).astype(bf16)])


def return_sums(first, sums_of, weights, join_weights):
    a2h, a2t, b4h, b4t, y2h, y2t = first
    w = next(weights)
    b4h, b4t, a2h, a2t, y2h, y2t, (a1, a3, b3, b5, y1, y3) = sums_of(1, (b4h, b4t, a2h, a2t, y2h, y2t))
    up, down = shift(b4h, "z", 1), shift(b4t, "z", -1)
    ax_p, ax_m = shift(a2h, "x", 1), shift(a2t, "x", -1)
    y_p = shift(y2h, "group", 1)

    up, down, ax_p, ax_m, y_p, y2t, a1, a3, b3, b5, w = bar((up, down, ax_p, ax_m, y_p, y2t, a1, a3, b3, b5, w))
    w = weights.send(w)
    up, down, ax_p, ax_m, y2t, (a0, b0, b1, b2, b6, b7) = sums_of(2, (up, down, ax_p, ax_m, y2t))
    up, down = shift(add_head(b3, up), "z", 1), shift(add_tail(b5, down), "z", -1)
    ax_p, ax_m = shift(add_head(a1, ax_p), "x", 1), shift(add_tail(a3, ax_m), "x", -1)
    y_m = shift(y2t, "group", -1)

    up, down, y_p, y_m, b2, b6 = bar((up, down, y_p, y_m, b2, b6))
    up, down = add(b2, up).astype(bf16), add(b6, down).astype(bf16)
    up, down = shift(up, "z", 1), shift(down, "z", -1)
    y_p = shift(add_head(y1, y_p), "group", 1)

    def part_a(dz):
        rows = slice(2 * dz, 2 * dz + 2)
        return add(a0[rows], ax_p[rows], ax_m[rows])

    def part_b(dx):
        rows = slice(2 * dx, 2 * dx + 2)
        cross = slice(8 + 2 * dx, 10 + 2 * dx)
        sums = add(b0[rows], up[rows], down[rows], y_p[cross], y_m[cross])
        return jnp.concatenate([sums, add(y_p[rows], y_m[rows])])

    up, down, ax_p, ax_m, y_m = bar((up, down, ax_p, ax_m, y_m))
    far = part_a(4).astype(bf16)
    up, down = add(b1, up).astype(bf16), add(b7, down).astype(bf16)
    az_p, az_m = shift(far[:1], "z", 1), shift(far[1:], "z", -1)
    up, down = shift(up, "z", 1), shift(down, "z", -1)
    y_m = shift(add_tail(y3, y_m), "group", -1)
    az_p, az_m, w = bar((az_p, az_m, w))
    w = weights.send(w)
    az_p, az_m = add_head(part_a(3), az_p), add_tail(part_a(5), az_m)
    az_p, az_m = shift(az_p, "z", 1), shift(az_m, "z", -1)
    az_p, az_m = add(part_a(2), az_p).astype(bf16), add(part_a(6), az_m).astype(bf16)
    far = part_b(2).astype(bf16)
    az_p, az_m, far = bar((az_p, az_m, far))
    bx_p, bx_m = shift(far[:2], "x", 1), shift(far[2:], "x", -1)
    az_p, az_m = shift(az_p, "z", 1), shift(az_m, "z", -1)
    bx_p, bx_m = add_head(part_b(1), bx_p), add_tail(part_b(3), bx_m)
    az_p, az_m = add(part_a(1), az_p).astype(bf16), add(part_a(7), az_m).astype(bf16)
    az_p, az_m, bx_p, bx_m, w = bar((az_p, az_m, bx_p, bx_m, w))
    w_sib = shift(w, "core", 1)
    bx_p, bx_m = shift(bx_p, "x", 1), shift(bx_m, "x", -1)
    az_p, az_m = shift(az_p, "z", 1), shift(az_m, "z", -1)
    joined = join_weights(w, w_sib)
    bx_p, bx_m, *joined = bar((bx_p, bx_m, *joined))
    sum_b = add(part_b(0), bx_p, bx_m)
    return add(part_a(0), az_p, az_m, sum_b[2:]), sum_b[:2], joined


def body(
    feats,
    neigh,
    pre_act,
    cotan,
    w_self,
    w_neigh,
    send_list,
    send_live,
    cross_list,
    cross_live,
    home_tiles,
    home_target,
    home_source,
    far_tiles,
    far_target,
    far_source,
    far_count,
):
    y, z, x, core = (lax.axis_index(name) for name in AXES)
    meta = jnp.stack([core, z, x, y]).astype(i32)
    first_core = core == 0
    cols = (((1,), (1,)), ((), ()))
    ints = jnp.concatenate(
        [
            (send_live * 2 + send_list).reshape(-1),
            (cross_live * 2 + cross_list).reshape(-1),
            home_target[0, 0],
            home_source[0, 0],
            far_target[0, 0],
            far_source[0, 0],
            far_count[0],
            jnp.zeros((INTS - FC - 1,), i32),
        ]
    )
    row = jnp.stack([ints, shift(ints, "x", -1), shift(ints, "x", 2), shift(ints, "x", 1)])
    row = jnp.stack([row, shift(row, "core", 1)], axis=1)
    words = row[:, :, :CROSS].reshape(2, HALF).astype(bf16)
    cross_words = jnp.pad(row[:, :, CROSS:HT].reshape(1, BLK // 2).astype(bf16), ((0, 0), (0, HALF - BLK // 2)))
    row = row.reshape(-1)

    def join(mine, other):
        low, high = jnp.where(first_core, mine, other), jnp.where(first_core, other, mine)
        return jnp.concatenate([low, high], axis=-1)

    grad_pre = jnp.where(pre_act > 0, cotan, jnp.zeros_like(cotan))
    wn_mine = lax.dynamic_slice_in_dim(w_neigh, core * HALF, HALF)
    wn_other = lax.dynamic_slice_in_dim(w_neigh, (1 - core) * HALF, HALF)
    agg_other = lax.dot_general(grad_pre, wn_other, cols, preferred_element_type=f32).astype(bf16)
    agg_sib = shift(agg_other, "core", 1)
    agg_own = lax.dot_general(grad_pre, wn_mine, cols, preferred_element_type=f32).astype(bf16)
    head = jnp.concatenate([words, cross_words, jnp.zeros((HEAD - 3, HALF), bf16)])
    chunk = join_chunk(head, agg_own, agg_sib)

    far_own, home_own = far_tiles[0, 0], home_tiles[0, 0]
    mine, other = weight_terms(meta, feats, neigh, grad_pre)

    far_sib, home_sib = shift(far_own, "core", 1), shift(home_own, "core", 1)
    chunk, far_sib, home_sib, mine, other = bar((chunk, far_sib, home_sib, mine, other))
    up1, dn1 = shift(chunk, "z", 1), shift(chunk, "z", -1)
    own3, own1 = shift(far_own, "x", 1), shift(far_own, "x", -1)
    other = shift(other, "core", 1)
    store = deposit(None, chunk0=chunk, tiles0=far_own, tiles1=far_sib, tiles8=home_own, tiles9=home_sib)
    up1, dn1, own1, own3, chunk, row, mine, other, far_sib, store = bar(
        (up1, dn1, own1, own3, chunk, row, mine, other, far_sib, store)
    )
    store = deposit(store, chunk7=up1, chunk1=dn1, tiles2=own1, tiles6=own3)
    weights = (mine + other).reshape(4 * HALF, HALF + BLK)
    weights = lax.psum_scatter(weights, "group", scatter_dimension=0, tiled=True)
    up2, dn2 = shift(up1, "z", 1), shift(dn1, "z", -1)
    sib3, sib1 = shift(far_sib, "x", 1), shift(far_sib, "x", -1)
    y1 = shift(chunk, "group", 1)
    (picked,) = scalars(pick_kernel, (PICKED,), meta, row)
    up2, dn2, sib1, sib3, own3, y1, chunk, picked, store = bar((up2, dn2, sib1, sib3, own3, y1, chunk, picked, store))
    store = deposit(store, chunk6=up2, chunk2=dn2, tiles3=sib1, tiles7=sib3, chunk8=y1)
    up3, dn3 = shift(up2, "z", 1), shift(dn2, "z", -1)
    own2, sib2 = shift(own3, "x", 1), shift(sib1, "x", -1)
    y3 = shift(chunk, "group", 3)
    up3, dn3, own2, sib2, y3, chunk, weights, store = bar((up3, dn3, own2, sib2, y3, chunk, weights, store))
    store = deposit(store, chunk5=up3, chunk3=dn3, tiles4=own2, tiles5=sib2, chunk10=y3)
    weights = lax.psum_scatter(weights, "z", scatter_dimension=0, tiled=True)
    middle = HEAD + 2 * BLK
    up4, dn4 = shift(up3[:middle], "z", 1), shift(dn3[middle:], "z", -1)
    y2 = shift(chunk, "group", 2)
    up4, dn4, y2, store = bar((up4, dn4, y2, store))
    store = deposit(store, chunk4=up4, tail4=dn4, chunk9=y2)
    todo = list_tiles(meta, row, picked, store)

    def weight_stages(w):
        w = yield w
        w = jnp.pad(w, ((0, 16), (0, 0)))
        w = yield lax.all_gather(w, ("group", "x"), axis=0)
        w = jnp.sum(w.reshape(NY, NX, 48, HALF + BLK)[:, :, :32], axis=1)
        yield lax.all_gather(w, "z", axis=0)

    def sums_of(group, arrived):
        *arrived, now = bar((*arrived, todo))
        return *arrived, tile_sums(group, now, store)

    (first,) = sums_of(0, ())
    def rows_of(value):
        return value.transpose(1, 0, 2, 3).reshape(4 * HALF, HALF + BLK)

    def join_weights(mine, other):
        mine, other = rows_of(mine), rows_of(other)
        sums = join(mine[:, :HALF], other[:, :HALF])
        return sums[:512], sums[512:], join(mine[:2, HALF:].reshape(-1), other[:2, HALF:].reshape(-1))

    sum_a, sum_b, joined = return_sums(first, sums_of, weight_stages(weights), join_weights)
    self_grad = lax.dot_general(grad_pre, w_self, cols, preferred_element_type=f32)
    other = shift(sum_b, "core", 1)
    grad_input = self_grad + join(sum_a.reshape(2 * BLK, HALF), other.reshape(2 * BLK, HALF))
    return grad_input.astype(bf16), *joined


def solution(mesh):
    fine = Mesh(mesh.devices.reshape(NY, NZ, NX, 2), AXES)
    rows = P(AXES, None)
    part = lambda extra: P("group", DOM, *([None] * extra))
    return jax.shard_map(
        body,
        mesh=fine,
        in_specs=(rows,) * 4
        + (P(), P())
        + (part(1), part(1), part(2), part(2), part(3), part(1), part(1), part(3), part(1), part(1), part(0)),
        out_specs=(rows, P(), P(), P()),
        check_vma=False,
    )
```

```python
import jax
import jax.numpy as jnp
from jax import lax
from jax.experimental import pallas as pl
from jax.experimental.pallas import tpu as pltpu
from jax.sharding import Mesh
from jax.sharding import PartitionSpec as P

AXES = ("group", "z", "x", "core")
DOM = ("z", "x", "core")
NY, NZ, NX = 4, 8, 4
BLK, HALF = 128, 256
NT = 16
SLOTS = 32
bf16, f32, i32 = jnp.bfloat16, jnp.float32, jnp.int32

SEND, CROSS, HT, HS, FT, FS, FC, INTS = 0, 64, 72, 88, 104, 120, 136, 256
HEAD = 16
ENTRIES = 161
LIST = 1 + 3 * ENTRIES
HEADS, TILES, STORE = 48, 64, 1024
PICKED = 1 + 128

GROUPS = (
    ((0, 8), (8, 8), (16, 4), (20, 4), (24, 8), (32, 8)),
    ((0, 16), (16, 16), (32, 8), (40, 8), (48, 16), (64, 16), (80, 8), (88, 8)),
    ((0, 16), (16, 8), (24, 8), (32, 8)),
)
STARTS, SIZES = (0, 40, 136), (40, 96, 40)
MIB = 2**20

VMEM = pl.BlockSpec(memory_space=pltpu.VMEM)
SMEM = pl.BlockSpec(memory_space=pltpu.SMEM)
ANY = pl.BlockSpec(memory_space=pl.ANY)
HBM = pl.BlockSpec(memory_space=pltpu.HBM)


def shift(value, axis, k):
    n = {"group": NY, "z": NZ, "x": NX, "core": 2}[axis]
    return lax.ppermute(value, axis, [(i, (i + k) % n) for i in range(n)])


def pick_kernel(meta, row, out):
    x = meta[2]
    out[0] = 0
    for dx in range(NX):
        for r in range(2):
            base = (dx * 2 + r) * INTS

            @pl.loop(0, jnp.minimum(row[base + FC], NT))
            def _(t, dx=dx, r=r, base=base):
                slot = row[base + FT + t]
                column = ((slot - 2) >> 1) & 3
                here = jnp.where(slot < 66, column == x, dx == 0)

                @pl.when(here)
                def _():
                    n = out[0]
                    out[0] = n + 1
                    out[1 + n] = (dx * 2 + r) * NT + t


def deposit_kernel(plan, *refs):
    sources, (store, staged, sems) = refs[: len(plan)], refs[-3:]
    copies = []

    def copy(source, target):
        copies.append(pltpu.make_async_copy(source, target, sems.at[len(copies)]))
        copies[-1].start()

    loads = {}
    for source, (kind, i) in zip(sources, plan):
        if kind == "tiles":
            loads[i] = pltpu.make_async_copy(source, staged.at[len(loads)], sems.at[5 * len(plan) + len(loads)])
            loads[i].start()
    slots = {i: j for j, i in enumerate(loads)}
    for source, (kind, i) in sorted(zip(sources, plan), key=lambda pair: pair[1][0]):
        if kind == "tiles":
            loads[i].wait()
            source = staged.at[slots[i]]
            for half in range(2):
                lanes = pl.ds(half * BLK, BLK)
                copy(source.at[pl.ds(8 * half, 8)], store.at[pl.ds(TILES + 8 * i, 8), :, lanes])
            continue
        start, first = (0, 2) if kind == "tail" else (HEAD, 0)
        if kind != "tail":
            copy(source.at[pl.ds(0, HEAD)], store.at[HEADS + i, pl.ds(0, HEAD)])
        for j in range((source.shape[0] - start) // BLK):
            copy(source.at[pl.ds(start + BLK * j, BLK)], store.at[4 * i + first + j])
    for c in copies:
        c.wait()


def deposit(store, **arrived):
    plan = [(name.rstrip("0123456789"), int(name.strip("abcdefghijklmnopqrstuvwxyz"))) for name in arrived]
    old = [] if store is None else [store]
    return pl.pallas_call(
        lambda *refs: deposit_kernel(plan, *refs),
        out_shape=jax.ShapeDtypeStruct((STORE, BLK, HALF), bf16),
        in_specs=[ANY] * (len(plan) + len(old)),
        out_specs=ANY,
        input_output_aliases={len(plan): 0} if old else {},
        scratch_shapes=[
            pltpu.VMEM((4, NT, BLK, BLK), bf16),
            pltpu.SemaphoreType.DMA((5 * len(plan) + 4,)),
        ],
        compiler_params=pltpu.CompilerParams(vmem_limit_bytes=4 * MIB),
    )(*arrived.values(), *old)


def list_kernel(meta, row, picked, store, out, low, wide, words, sems):
    core, z, x, y = (meta[j] for j in range(4))
    heads = [store.at[HEADS + j, pl.ds(0, HEAD)] for j in range(11)]
    copies = [pltpu.make_async_copy(v, low.at[j], sems.at[j]) for j, v in enumerate(heads)]
    for copy in copies:
        copy.start()
    for copy in copies:
        copy.wait()
    wide[...] = low[...].astype(f32).astype(i32)
    copy = pltpu.make_async_copy(wide.at[:, pl.ds(0, 8)], words, sems.at[0])
    copy.start()
    copy.wait()
    for group in range(3):
        out[group * LIST] = 0

    def master(slot, dx, r):
        in_dom = slot < 66
        q = jnp.clip(slot - 2, 0, 63)
        dz = ((q >> 3) - z) & 7
        to_x = (((q >> 1) & 3) - x) & 3
        same = ((q & 1) ^ core)
        me = z * 8 + ((x + dx) & 3) * 2 + (core ^ r)
        v = jnp.clip(slot - 66, 0, 7)
        dy = ((v >> 1) - y) & 3
        word = jnp.where(
            in_dom,
            words[dz, to_x >> 1, ((to_x & 1) * 2 + same) * 64 + me],
            words[jnp.where(dy == 0, 0, 11 - dy), 2, (dx * 2 + r) * 8 + y * 2 + (v & 1)],
        )
        k = word & 1
        dz = jnp.where(in_dom, dz, 0)
        to_x = jnp.where(in_dom, to_x, dx)
        same = jnp.where(in_dom, same, r)
        dy = jnp.where(in_dom, 0, dy)
        return word >= 2, dy, dz, to_x, same, k

    def accumulator(slot, dx, r):
        live, dy, dz, to_x, same, k = master(slot, dx, r)
        own = slot < 2
        live = jnp.logical_or(own, live)
        dy, dz = jnp.where(own, 0, dy), jnp.where(own, 0, dz)
        to_x, same = jnp.where(own, dx, to_x), jnp.where(own, r, same)
        k = jnp.where(own, slot, k)
        a = jnp.where(to_x == 0, 136, jnp.where(to_x == 2, 0, 32 + 8 * to_x)) + dz * 2
        middle = jnp.where(dz == 4, 16, 72 + 4 * (dz - 3))
        outer = jnp.where(dz < 2, 152 + 8 * dz, jnp.where(dz == 7, 168, 116 + 2 * dz))
        b = jnp.where((dz - 4) * (dz - 4) < 2, middle, outer) + to_x * 2
        c = jnp.where(dy == 2, 24, jnp.where(dy == 1, 88, 104)) + r * 8 + dx * 2
        return live, jnp.where(dy > 0, c, jnp.where(same == 0, a, b)) + k

    def append(live, tile, block, place):
        middle, last = place >= STARTS[1], place >= STARTS[2]
        base = jnp.where(last, 2 * LIST, jnp.where(middle, LIST, 0))
        place = place - jnp.where(last, STARTS[2], jnp.where(middle, STARTS[1], 0))
        n = out[base]
        for j, value in enumerate((tile, block, place)):
            out[base + 1 + ENTRIES * j + n] = value
        out[base] = n + live.astype(i32)

    for r in range(2):

        @pl.loop(0, NT, unroll=4)
        def _(t, r=r):
            live, place = accumulator(row[r * INTS + HS + t], 0, r)
            append(live, (8 + r) * NT + t, 2 * r + row[r * INTS + HT + t], place)

    @pl.loop(0, picked[0])
    def _(i):
        which = picked[1 + i]
        dx, r, t = which >> 5, (which >> 4) & 1, which & 15
        base = (which >> 4) * INTS
        target_live, dy, dz, _, same, k = master(row[base + FT + t], dx, r)
        source_live, place = accumulator(row[base + FS + t], dx, r)
        source = jnp.where(dy > 0, 11 - dy, dz)
        append(jnp.logical_and(target_live, source_live), which, 4 * source + 2 * same + k, place)


def list_tiles(meta, row, picked, store):
    return pl.pallas_call(
        list_kernel,
        out_shape=jax.ShapeDtypeStruct((3 * LIST,), i32),
        in_specs=[SMEM] * 3 + [ANY],
        out_specs=SMEM,
        scratch_shapes=[
            pltpu.VMEM((11, HEAD, HALF), bf16),
            pltpu.VMEM((11, HEAD, HALF), i32),
            pltpu.SMEM((11, 8, HALF), i32),
            pltpu.SemaphoreType.DMA((11,)),
        ],
        compiler_params=pltpu.CompilerParams(vmem_limit_bytes=3 * MIB),
    )(meta, row, picked, store)


bar = lax.optimization_barrier


def tile_product(tile, block):
    return lax.dot_general(tile, block, (((0,), (0,)), ((), ())), preferred_element_type=f32)


def tile_kernel(group, todo, store, *refs):
    parts, base = GROUPS[group], group * LIST
    outs, (acc, tiles, blocks, tile_sems, block_sems, out_sems) = refs[: len(parts)], refs[len(parts) :]
    n = todo[base]

    def held(c):
        return jnp.clip(n - c * SLOTS, 0, SLOTS)

    def start(c):
        def one(j, _):
            i = base + 1 + c * SLOTS + j
            which = todo[i]
            row = TILES + ((which >> 4) << 3) + (which & 7)
            lanes = pl.ds(pl.multiple_of(((which >> 3) & 1) * BLK, BLK), BLK)
            pltpu.make_async_copy(store.at[row, :, lanes], tiles.at[j], tile_sems.at[j]).start()
            pltpu.make_async_copy(store.at[todo[i + ENTRIES]], blocks.at[j], block_sems.at[j]).start()
            return 0

        lax.fori_loop(0, held(c), one, 0)

    def finish(c):
        def one(j, _):
            place = todo[base + 1 + 2 * ENTRIES + c * SLOTS + j]
            pltpu.make_async_copy(store.at[0, :, pl.ds(0, BLK)], tiles.at[j], tile_sems.at[j]).wait()
            pltpu.make_async_copy(store.at[0], blocks.at[j], block_sems.at[j]).wait()
            term = tile_product(tiles[j], blocks[j])
            acc[place] = (acc[place].astype(f32) + term).astype(bf16)
            return 0

        lax.fori_loop(0, held(c), one, 0)

    start(0)

    @pl.loop(0, acc.shape[0])
    def _(b):
        acc[b] = jnp.zeros((BLK, HALF), bf16)

    def step(c, _):
        finish(c)
        start(c + 1)
        return 0

    lax.fori_loop(0, (n + SLOTS - 1) // SLOTS, step, 0)
    copies = [
        pltpu.make_async_copy(acc.at[pl.ds(s, m)], out, out_sems.at[j])
        for j, ((s, m), out) in enumerate(zip(parts, outs))
    ]
    for copy in copies:
        copy.start()
    for copy in copies:
        copy.wait()


def tile_sums(group, todo, store):
    parts, size = GROUPS[group], SIZES[group]
    return pl.pallas_call(
        lambda *refs: tile_kernel(group, *refs),
        out_shape=[jax.ShapeDtypeStruct((m, BLK, HALF), bf16) for _, m in parts],
        in_specs=[SMEM, ANY],
        out_specs=[VMEM if group else HBM] * len(parts),
        scratch_shapes=[
            pltpu.VMEM((size, BLK, HALF), bf16),
            pltpu.VMEM((SLOTS, BLK, BLK), bf16),
            pltpu.VMEM((SLOTS, BLK, HALF), bf16),
            pltpu.SemaphoreType.DMA((SLOTS,)),
            pltpu.SemaphoreType.DMA((SLOTS,)),
            pltpu.SemaphoreType.DMA((len(parts),)),
        ],
        compiler_params=pltpu.CompilerParams(vmem_limit_bytes=11 * MIB),
        cost_estimate=pl.CostEstimate(flops=10**9, bytes_accessed=2 * 10**7, transcendentals=0),
    )(todo, store)


def join_kernel(head, own, sib, out):
    out[:HEAD] = head[...]
    out[HEAD : HEAD + HALF] = own[...]
    out[HEAD + HALF :] = sib[...]


def join_chunk(head, own, sib):
    return pl.pallas_call(
        join_kernel,
        out_shape=jax.ShapeDtypeStruct((HEAD + 2 * HALF, HALF), bf16),
        in_specs=[VMEM] * 3,
        out_specs=VMEM,
        compiler_params=pltpu.CompilerParams(vmem_limit_bytes=4 * MIB),
    )(head, own, sib)


def weight_kernel(meta, grad_pre, feats, neigh, mine, other, source, sums, sems):
    loads = [pltpu.make_async_copy(v, source.at[j], sems.at[j]) for j, v in enumerate((feats, neigh))]
    for load in loads:
        load.start()
    core = meta[0]
    low, high = grad_pre[:, :HALF], grad_pre[:, HALF:]
    for load in loads:
        load.wait()
    stores = []
    for j, (out, from_low) in enumerate(((other, core == 1), (mine, core == 0))):
        part = jnp.where(from_low, low, high)
        bias = jnp.sum(part.astype(f32), axis=0, keepdims=True)
        for g in range(NY):
            cols = source[g // 2, :, (g % 2) * HALF : (g % 2 + 1) * HALF]
            sums[j, g, :, :HALF] = tile_product(cols, part)
            sums[j, g, :, HALF:] = jnp.zeros((HALF, BLK), f32)
            if g == 0:
                sums[j, g, 0:1, HALF:] = bias[:, :BLK]
                sums[j, g, 1:2, HALF:] = bias[:, BLK:]
        stores.append(pltpu.make_async_copy(sums.at[j], out, sems.at[2 + j]))
        stores[-1].start()
    for store in stores:
        store.wait()


def weight_terms(meta, feats, neigh, grad_pre):
    shape = (NY, HALF, HALF + BLK)
    return pl.pallas_call(
        weight_kernel,
        out_shape=[jax.ShapeDtypeStruct(shape, f32)] * 2,
        in_specs=[SMEM, VMEM, HBM, HBM],
        out_specs=[HBM] * 2,
        scratch_shapes=[
            pltpu.VMEM((2, *feats.shape), bf16),
            pltpu.VMEM((2, *shape), f32),
            pltpu.SemaphoreType.DMA((4,)),
        ],
        compiler_params=pltpu.CompilerParams(vmem_limit_bytes=8 * MIB),
    )(meta, grad_pre, feats, neigh)


def agg_kernel(meta, pre_act, cotan, w_neigh, grad_pre, agg_own, agg_other):
    grad = jnp.where(pre_act[...] > 0, cotan[...], jnp.zeros_like(cotan))
    grad_pre[...] = grad
    for out, half in ((agg_other, 1 - meta[0]), (agg_own, meta[0])):
        weight = w_neigh[pl.ds(pl.multiple_of(half * HALF, HALF), HALF), :]
        product = lax.dot_general(grad, weight, (((1,), (1,)), ((), ())), preferred_element_type=f32)
        out[...] = product.astype(bf16)


def agg_terms(meta, pre_act, cotan, w_neigh):
    half = jax.ShapeDtypeStruct((HALF, HALF), bf16)
    return pl.pallas_call(
        agg_kernel,
        out_shape=[jax.ShapeDtypeStruct(pre_act.shape, bf16), half, half],
        in_specs=[SMEM] + [VMEM] * 3,
        out_specs=[VMEM] * 3,
        compiler_params=pltpu.CompilerParams(vmem_limit_bytes=6 * MIB),
    )(meta, pre_act, cotan, w_neigh)


def join_kernel(head, own, sib, out):
    out[:HEAD] = head[...]
    out[HEAD : HEAD + HALF] = own[...]
    out[HEAD + HALF :] = sib[...]


def join_chunk(head, own, sib):
    return pl.pallas_call(
        join_kernel,
        out_shape=jax.ShapeDtypeStruct((HEAD + 2 * HALF, HALF), bf16),
        in_specs=[VMEM] * 3,
        out_specs=VMEM,
        compiler_params=pltpu.CompilerParams(vmem_limit_bytes=4 * MIB),
    )(head, own, sib)


def weight_kernel(meta, feats, neigh, grad_pre, mine, other):
    core = meta[0]
    low, high = grad_pre[:, :HALF], grad_pre[:, HALF:]
    for out, from_low in ((mine, core == 0), (other, core == 1)):
        part = jnp.where(from_low, low, high)
        bias = jnp.sum(part.astype(f32), axis=0, keepdims=True)
        for g in range(NY):
            source = feats if g < 2 else neigh
            cols = source[:, (g % 2) * HALF : (g % 2 + 1) * HALF]
            out[g, :, :HALF] = tile_product(cols, part)
            out[g, :, HALF:] = jnp.zeros((HALF, BLK), f32)
            if g == 0:
                out[g, 0:1, HALF:] = bias[:, :BLK]
                out[g, 1:2, HALF:] = bias[:, BLK:]


def weight_terms(meta, feats, neigh, grad_pre):
    return pl.pallas_call(
        weight_kernel,
        out_shape=[jax.ShapeDtypeStruct((NY, HALF, HALF + BLK), f32)] * 2,
        in_specs=[SMEM] + [VMEM] * 3,
        out_specs=[VMEM] * 2,
        compiler_params=pltpu.CompilerParams(vmem_limit_bytes=10 * MIB),
    )(meta, feats, neigh, grad_pre)


def scalars(kernel, sizes, *args):
    return pl.pallas_call(
        kernel,
        out_shape=[jax.ShapeDtypeStruct((n,), i32) for n in sizes],
        in_specs=[SMEM] * len(args),
        out_specs=[SMEM] * len(sizes),
        compiler_params=pltpu.CompilerParams(vmem_limit_bytes=3 * MIB),
    )(*args)


def add(*terms):
    total = terms[0].astype(f32)
    for term in terms[1:]:
        total = total + term.astype(f32)
    return total


def add_head(value, head):
    n = head.shape[0]
    return jnp.concatenate([add(value[:n], head).astype(bf16), value[n:].astype(bf16)])


def add_tail(value, tail):
    n = value.shape[0] - tail.shape[0]
    return jnp.concatenate([value[:n].astype(bf16), add(value[n:], tail).astype(bf16)])


def return_sums(first, sums_of, weights, join_weights):
    a2h, a2t, b4h, b4t, y2h, y2t = first
    w = next(weights)
    b4h, b4t, a2h, a2t, y2h, y2t, (a1, a3, b3, b5, y1, y3, b2, b6) = sums_of(1, (b4h, b4t, a2h, a2t, y2h, y2t))
    up, down = shift(b4h, "z", 1), shift(b4t, "z", -1)
    ax_p, ax_m = shift(a2h, "x", 1), shift(a2t, "x", -1)
    y_p = shift(y2h, "group", 1)

    up, down, ax_p, ax_m, y_p, y2t, a1, a3, b3, b5, w = bar((up, down, ax_p, ax_m, y_p, y2t, a1, a3, b3, b5, w))
    w = weights.send(w)
    up, down = shift(add_head(b3, up), "z", 1), shift(add_tail(b5, down), "z", -1)
    ax_p, ax_m = shift(add_head(a1, ax_p), "x", 1), shift(add_tail(a3, ax_m), "x", -1)
    y_m = shift(y2t, "group", -1)

    up, down, y_p, y_m, (a0, b0, b1, b7) = sums_of(2, (up, down, y_p, y_m))
    up, down = add(b2, up).astype(bf16), add(b6, down).astype(bf16)
    up, down = shift(up, "z", 1), shift(down, "z", -1)
    y_p = shift(add_head(y1, y_p), "group", 1)

    def part_a(dz):
        rows = slice(2 * dz, 2 * dz + 2)
        return add(a0[rows], ax_p[rows], ax_m[rows])

    def part_b(dx):
        rows = slice(2 * dx, 2 * dx + 2)
        cross = slice(8 + 2 * dx, 10 + 2 * dx)
        sums = add(b0[rows], up[rows], down[rows], y_p[cross], y_m[cross])
        return jnp.concatenate([sums, add(y_p[rows], y_m[rows])])

    up, down, ax_p, ax_m, y_m, a0, b1, b7 = bar((up, down, ax_p, ax_m, y_m, a0, b1, b7))
    far = part_a(4).astype(bf16)
    up, down = add(b1, up).astype(bf16), add(b7, down).astype(bf16)
    az_p, az_m = shift(far[:1], "z", 1), shift(far[1:], "z", -1)
    up, down = shift(up, "z", 1), shift(down, "z", -1)
    y_m = shift(add_tail(y3, y_m), "group", -1)
    az_p, az_m, w = bar((az_p, az_m, w))
    w = weights.send(w)
    az_p, az_m = add_head(part_a(3), az_p), add_tail(part_a(5), az_m)
    az_p, az_m = shift(az_p, "z", 1), shift(az_m, "z", -1)
    az_p, az_m = add(part_a(2), az_p).astype(bf16), add(part_a(6), az_m).astype(bf16)
    far = part_b(2).astype(bf16)
    az_p, az_m, far = bar((az_p, az_m, far))
    bx_p, bx_m = shift(far[:2], "x", 1), shift(far[2:], "x", -1)
    az_p, az_m = shift(az_p, "z", 1), shift(az_m, "z", -1)
    bx_p, bx_m = add_head(part_b(1), bx_p), add_tail(part_b(3), bx_m)
    az_p, az_m = add(part_a(1), az_p).astype(bf16), add(part_a(7), az_m).astype(bf16)
    az_p, az_m, bx_p, bx_m, w = bar((az_p, az_m, bx_p, bx_m, w))
    w_sib = shift(w, "core", 1)
    bx_p, bx_m = shift(bx_p, "x", 1), shift(bx_m, "x", -1)
    az_p, az_m = shift(az_p, "z", 1), shift(az_m, "z", -1)
    joined = join_weights(w, w_sib)
    az_p, az_m, bx_p, bx_m, *joined = bar((az_p, az_m, bx_p, bx_m, *joined))
    sum_b = add(part_b(0), bx_p, bx_m)
    return add(part_a(0), az_p, az_m, sum_b[2:]), sum_b[:2], joined


def body(
    feats,
    neigh,
    pre_act,
    cotan,
    w_self,
    w_neigh,
    send_list,
    send_live,
    cross_list,
    cross_live,
    home_tiles,
    home_target,
    home_source,
    far_tiles,
    far_target,
    far_source,
    far_count,
):
    y, z, x, core = (lax.axis_index(name) for name in AXES)
    meta = jnp.stack([core, z, x, y]).astype(i32)
    first_core = core == 0
    cols = (((1,), (1,)), ((), ()))
    ints = jnp.concatenate(
        [
            (send_live * 2 + send_list).reshape(-1),
            (cross_live * 2 + cross_list).reshape(-1),
            home_target[0, 0],
            home_source[0, 0],
            far_target[0, 0],
            far_source[0, 0],
            far_count[0],
            jnp.zeros((INTS - FC - 1,), i32),
        ]
    )
    row = jnp.stack([ints, shift(ints, "x", -1), shift(ints, "x", 2), shift(ints, "x", 1)])
    row = jnp.stack([row, shift(row, "core", 1)], axis=1)
    words = row[:, :, :CROSS].reshape(2, HALF).astype(bf16)
    cross_words = jnp.pad(row[:, :, CROSS:HT].reshape(1, BLK // 2).astype(bf16), ((0, 0), (0, HALF - BLK // 2)))
    row = row.reshape(-1)

    def join(mine, other):
        low, high = jnp.where(first_core, mine, other), jnp.where(first_core, other, mine)
        return jnp.concatenate([low, high], axis=-1)

    grad_pre = jnp.where(pre_act > 0, cotan, jnp.zeros_like(cotan))
    wn_mine = lax.dynamic_slice_in_dim(w_neigh, core * HALF, HALF)
    wn_other = lax.dynamic_slice_in_dim(w_neigh, (1 - core) * HALF, HALF)
    agg_other = lax.dot_general(grad_pre, wn_other, cols, preferred_element_type=f32).astype(bf16)
    agg_sib = shift(agg_other, "core", 1)
    agg_own = lax.dot_general(grad_pre, wn_mine, cols, preferred_element_type=f32).astype(bf16)
    head = jnp.concatenate([words, cross_words, jnp.zeros((HEAD - 3, HALF), bf16)])
    chunk = join_chunk(head, agg_own, agg_sib)

    far_own, home_own = far_tiles[0, 0], home_tiles[0, 0]
    mine, other = weight_terms(meta, feats, neigh, grad_pre)

    far_sib, home_sib = shift(far_own, "core", 1), shift(home_own, "core", 1)
    chunk, far_sib, home_sib, mine, other = bar((chunk, far_sib, home_sib, mine, other))
    up1, dn1 = shift(chunk, "z", 1), shift(chunk, "z", -1)
    own3, own1 = shift(far_own, "x", 1), shift(far_own, "x", -1)
    other = shift(other, "core", 1)
    store = deposit(None, chunk0=chunk, tiles0=far_own, tiles1=far_sib, tiles8=home_own, tiles9=home_sib)
    up1, dn1, own1, own3, chunk, row, mine, other, far_sib, store = bar(
        (up1, dn1, own1, own3, chunk, row, mine, other, far_sib, store)
    )
    store = deposit(store, chunk7=up1, chunk1=dn1, tiles2=own1, tiles6=own3)
    weights = (mine + other).reshape(4 * HALF, HALF + BLK)
    weights = lax.psum_scatter(weights, "group", scatter_dimension=0, tiled=True)
    up2, dn2 = shift(up1, "z", 1), shift(dn1, "z", -1)
    sib3, sib1 = shift(far_sib, "x", 1), shift(far_sib, "x", -1)
    y1 = shift(chunk, "group", 1)
    (picked,) = scalars(pick_kernel, (PICKED,), meta, row)
    up2, dn2, sib1, sib3, own3, y1, chunk, picked, store = bar((up2, dn2, sib1, sib3, own3, y1, chunk, picked, store))
    store = deposit(store, chunk6=up2, chunk2=dn2, tiles3=sib1, tiles7=sib3, chunk8=y1)
    up3, dn3 = shift(up2, "z", 1), shift(dn2, "z", -1)
    own2, sib2 = shift(own3, "x", 1), shift(sib1, "x", -1)
    y3 = shift(chunk, "group", 3)
    up3, dn3, own2, sib2, y3, chunk, weights, store = bar((up3, dn3, own2, sib2, y3, chunk, weights, store))
    store = deposit(store, chunk5=up3, chunk3=dn3, tiles4=own2, tiles5=sib2, chunk10=y3)
    weights = lax.psum_scatter(weights, "z", scatter_dimension=0, tiled=True)
    middle = HEAD + 2 * BLK
    up4, dn4 = shift(up3[:middle], "z", 1), shift(dn3[middle:], "z", -1)
    y2 = shift(chunk, "group", 2)
    up4, dn4, y2, store = bar((up4, dn4, y2, store))
    store = deposit(store, chunk4=up4, tail4=dn4, chunk9=y2)
    todo = list_tiles(meta, row, picked, store)

    def weight_stages(w):
        w = yield w
        w = jnp.pad(w, ((0, 16), (0, 0)))
        w = yield lax.all_gather(w, ("group", "x"), axis=0)
        w = jnp.sum(w.reshape(NY, NX, 48, HALF + BLK)[:, :, :32], axis=1)
        yield lax.all_gather(w, "z", axis=0)

    def sums_of(group, arrived):
        *arrived, now = bar((*arrived, todo))
        return *arrived, tile_sums(group, now, store)

    (first,) = sums_of(0, ())
    def rows_of(value):
        return value.transpose(1, 0, 2, 3).reshape(4 * HALF, HALF + BLK)

    def join_weights(mine, other):
        mine, other = rows_of(mine), rows_of(other)
        sums = join(mine[:, :HALF], other[:, :HALF])
        return sums[:512], sums[512:], join(mine[:2, HALF:].reshape(-1), other[:2, HALF:].reshape(-1))

    sum_a, sum_b, joined = return_sums(first, sums_of, weight_stages(weights), join_weights)
    self_grad = lax.dot_general(grad_pre, w_self, cols, preferred_element_type=f32)
    other = shift(sum_b, "core", 1)
    grad_input = self_grad + join(sum_a.reshape(2 * BLK, HALF), other.reshape(2 * BLK, HALF))
    return grad_input.astype(bf16), *joined


def solution(mesh):
    fine = Mesh(mesh.devices.reshape(NY, NZ, NX, 2), AXES)
    rows = P(AXES, None)
    part = lambda extra: P("group", DOM, *([None] * extra))
    return jax.shard_map(
        body,
        mesh=fine,
        in_specs=(rows,) * 4
        + (P(), P())
        + (part(1), part(1), part(2), part(2), part(3), part(1), part(1), part(3), part(1), part(1), part(0)),
        out_specs=(rows, P(), P(), P()),
        check_vma=False,
    )
```

```python
import jax
import jax.numpy as jnp
from jax import lax
from jax.experimental import pallas as pl
from jax.experimental.pallas import tpu as pltpu
from jax.sharding import Mesh
from jax.sharding import PartitionSpec as P

AXES = ("group", "z", "x", "core")
DOM = ("z", "x", "core")
NY, NZ, NX = 4, 8, 4
BLK, HALF = 128, 256
NT = 16
SLOTS = 32
bf16, f32, i32 = jnp.bfloat16, jnp.float32, jnp.int32

SEND, CROSS, HT, HS, FT, FS, FC, INTS = 0, 64, 72, 88, 104, 120, 136, 256
HEAD = 16
ENTRIES = 161
LIST = 1 + 3 * ENTRIES
HEADS, TILES, STORE = 48, 64, 1024
PICKED = 1 + 128

GROUPS = (
    ((0, 8), (8, 8), (16, 4), (20, 4), (24, 8), (32, 8)),
    ((0, 16), (16, 16), (32, 8), (40, 8), (48, 16), (64, 16), (80, 8), (88, 8)),
    ((0, 16), (16, 8), (24, 8), (32, 8)),
)
STARTS, SIZES = (0, 40, 136), (40, 96, 40)
MIB = 2**20

VMEM = pl.BlockSpec(memory_space=pltpu.VMEM)
SMEM = pl.BlockSpec(memory_space=pltpu.SMEM)
ANY = pl.BlockSpec(memory_space=pl.ANY)
HBM = pl.BlockSpec(memory_space=pltpu.HBM)


def shift(value, axis, k):
    n = {"group": NY, "z": NZ, "x": NX, "core": 2}[axis]
    return lax.ppermute(value, axis, [(i, (i + k) % n) for i in range(n)])


def pick_kernel(meta, row, out):
    x = meta[2]
    out[0] = 0
    for dx in range(NX):
        for r in range(2):
            base = (dx * 2 + r) * INTS

            @pl.loop(0, jnp.minimum(row[base + FC], NT))
            def _(t, dx=dx, r=r, base=base):
                slot = row[base + FT + t]
                column = ((slot - 2) >> 1) & 3
                here = jnp.where(slot < 66, column == x, dx == 0)

                @pl.when(here)
                def _():
                    n = out[0]
                    out[0] = n + 1
                    out[1 + n] = (dx * 2 + r) * NT + t


def deposit_kernel(plan, *refs):
    sources, (store, staged, sems) = refs[: len(plan)], refs[-3:]
    copies = []

    def copy(source, target):
        copies.append(pltpu.make_async_copy(source, target, sems.at[len(copies)]))
        copies[-1].start()

    loads = {}
    for source, (kind, i) in zip(sources, plan):
        if kind == "tiles":
            loads[i] = pltpu.make_async_copy(source, staged.at[len(loads)], sems.at[5 * len(plan) + len(loads)])
            loads[i].start()
    slots = {i: j for j, i in enumerate(loads)}
    for source, (kind, i) in sorted(zip(sources, plan), key=lambda pair: pair[1][0]):
        if kind == "tiles":
            loads[i].wait()
            source = staged.at[slots[i]]
            for half in range(2):
                lanes = pl.ds(half * BLK, BLK)
                copy(source.at[pl.ds(8 * half, 8)], store.at[pl.ds(TILES + 8 * i, 8), :, lanes])
            continue
        start, first = (0, 2) if kind == "tail" else (HEAD, 0)
        if kind != "tail":
            copy(source.at[pl.ds(0, HEAD)], store.at[HEADS + i, pl.ds(0, HEAD)])
        for j in range((source.shape[0] - start) // BLK):
            copy(source.at[pl.ds(start + BLK * j, BLK)], store.at[4 * i + first + j])
    for c in copies:
        c.wait()


def deposit(store, **arrived):
    plan = [(name.rstrip("0123456789"), int(name.strip("abcdefghijklmnopqrstuvwxyz"))) for name in arrived]
    old = [] if store is None else [store]
    return pl.pallas_call(
        lambda *refs: deposit_kernel(plan, *refs),
        out_shape=jax.ShapeDtypeStruct((STORE, BLK, HALF), bf16),
        in_specs=[ANY] * (len(plan) + len(old)),
        out_specs=ANY,
        input_output_aliases={len(plan): 0} if old else {},
        scratch_shapes=[
            pltpu.VMEM((4, NT, BLK, BLK), bf16),
            pltpu.SemaphoreType.DMA((5 * len(plan) + 4,)),
        ],
        compiler_params=pltpu.CompilerParams(vmem_limit_bytes=4 * MIB),
    )(*arrived.values(), *old)


def list_kernel(meta, row, picked, store, out, low, wide, words, sems):
    core, z, x, y = (meta[j] for j in range(4))
    heads = [store.at[HEADS + j, pl.ds(0, HEAD)] for j in range(11)]
    copies = [pltpu.make_async_copy(v, low.at[j], sems.at[j]) for j, v in enumerate(heads)]
    for copy in copies:
        copy.start()
    for copy in copies:
        copy.wait()
    wide[...] = low[...].astype(f32).astype(i32)
    copy = pltpu.make_async_copy(wide.at[:, pl.ds(0, 8)], words, sems.at[0])
    copy.start()
    copy.wait()
    for group in range(3):
        out[group * LIST] = 0

    def master(slot, dx, r):
        in_dom = slot < 66
        q = jnp.clip(slot - 2, 0, 63)
        dz = ((q >> 3) - z) & 7
        to_x = (((q >> 1) & 3) - x) & 3
        same = ((q & 1) ^ core)
        me = z * 8 + ((x + dx) & 3) * 2 + (core ^ r)
        v = jnp.clip(slot - 66, 0, 7)
        dy = ((v >> 1) - y) & 3
        word = jnp.where(
            in_dom,
            words[dz, to_x >> 1, ((to_x & 1) * 2 + same) * 64 + me],
            words[jnp.where(dy == 0, 0, 11 - dy), 2, (dx * 2 + r) * 8 + y * 2 + (v & 1)],
        )
        k = word & 1
        dz = jnp.where(in_dom, dz, 0)
        to_x = jnp.where(in_dom, to_x, dx)
        same = jnp.where(in_dom, same, r)
        dy = jnp.where(in_dom, 0, dy)
        return word >= 2, dy, dz, to_x, same, k

    def accumulator(slot, dx, r):
        live, dy, dz, to_x, same, k = master(slot, dx, r)
        own = slot < 2
        live = jnp.logical_or(own, live)
        dy, dz = jnp.where(own, 0, dy), jnp.where(own, 0, dz)
        to_x, same = jnp.where(own, dx, to_x), jnp.where(own, r, same)
        k = jnp.where(own, slot, k)
        a = jnp.where(to_x == 0, 136, jnp.where(to_x == 2, 0, 32 + 8 * to_x)) + dz * 2
        middle = jnp.where(dz == 4, 16, 72 + 4 * (dz - 3))
        outer = jnp.where(dz < 2, 152 + 8 * dz, jnp.where(dz == 7, 168, 116 + 2 * dz))
        b = jnp.where((dz - 4) * (dz - 4) < 2, middle, outer) + to_x * 2
        c = jnp.where(dy == 2, 24, jnp.where(dy == 1, 88, 104)) + r * 8 + dx * 2
        return live, jnp.where(dy > 0, c, jnp.where(same == 0, a, b)) + k

    def append(live, tile, block, place):
        middle, last = place >= STARTS[1], place >= STARTS[2]
        base = jnp.where(last, 2 * LIST, jnp.where(middle, LIST, 0))
        place = place - jnp.where(last, STARTS[2], jnp.where(middle, STARTS[1], 0))
        n = out[base]
        for j, value in enumerate((tile, block, place)):
            out[base + 1 + ENTRIES * j + n] = value
        out[base] = n + live.astype(i32)

    for r in range(2):

        @pl.loop(0, NT, unroll=4)
        def _(t, r=r):
            live, place = accumulator(row[r * INTS + HS + t], 0, r)
            append(live, (8 + r) * NT + t, 2 * r + row[r * INTS + HT + t], place)

    @pl.loop(0, picked[0])
    def _(i):
        which = picked[1 + i]
        dx, r, t = which >> 5, (which >> 4) & 1, which & 15
        base = (which >> 4) * INTS
        target_live, dy, dz, _, same, k = master(row[base + FT + t], dx, r)
        source_live, place = accumulator(row[base + FS + t], dx, r)
        source = jnp.where(dy > 0, 11 - dy, dz)
        append(jnp.logical_and(target_live, source_live), which, 4 * source + 2 * same + k, place)


def list_tiles(meta, row, picked, store):
    return pl.pallas_call(
        list_kernel,
        out_shape=jax.ShapeDtypeStruct((3 * LIST,), i32),
        in_specs=[SMEM] * 3 + [ANY],
        out_specs=SMEM,
        scratch_shapes=[
            pltpu.VMEM((11, HEAD, HALF), bf16),
            pltpu.VMEM((11, HEAD, HALF), i32),
            pltpu.SMEM((11, 8, HALF), i32),
            pltpu.SemaphoreType.DMA((11,)),
        ],
        compiler_params=pltpu.CompilerParams(vmem_limit_bytes=3 * MIB),
    )(meta, row, picked, store)


bar = lax.optimization_barrier


def tile_product(tile, block):
    return lax.dot_general(tile, block, (((0,), (0,)), ((), ())), preferred_element_type=f32)


def tile_kernel(group, todo, store, *refs):
    parts, base = GROUPS[group], group * LIST
    outs, (acc, tiles, blocks, tile_sems, block_sems, out_sems) = refs[: len(parts)], refs[len(parts) :]
    n = todo[base]

    def held(c):
        return jnp.clip(n - c * SLOTS, 0, SLOTS)

    def start(c):
        def one(j, _):
            i = base + 1 + c * SLOTS + j
            which = todo[i]
            row = TILES + ((which >> 4) << 3) + (which & 7)
            lanes = pl.ds(pl.multiple_of(((which >> 3) & 1) * BLK, BLK), BLK)
            pltpu.make_async_copy(store.at[row, :, lanes], tiles.at[j], tile_sems.at[j]).start()
            pltpu.make_async_copy(store.at[todo[i + ENTRIES]], blocks.at[j], block_sems.at[j]).start()
            return 0

        lax.fori_loop(0, held(c), one, 0)

    def finish(c):
        def one(j, _):
            place = todo[base + 1 + 2 * ENTRIES + c * SLOTS + j]
            pltpu.make_async_copy(store.at[0, :, pl.ds(0, BLK)], tiles.at[j], tile_sems.at[j]).wait()
            pltpu.make_async_copy(store.at[0], blocks.at[j], block_sems.at[j]).wait()
            term = tile_product(tiles[j], blocks[j])
            acc[place] = (acc[place].astype(f32) + term).astype(bf16)
            return 0

        lax.fori_loop(0, held(c), one, 0)

    start(0)

    @pl.loop(0, acc.shape[0])
    def _(b):
        acc[b] = jnp.zeros((BLK, HALF), bf16)

    def step(c, _):
        finish(c)
        start(c + 1)
        return 0

    lax.fori_loop(0, (n + SLOTS - 1) // SLOTS, step, 0)
    copies = [
        pltpu.make_async_copy(acc.at[pl.ds(s, m)], out, out_sems.at[j])
        for j, ((s, m), out) in enumerate(zip(parts, outs))
    ]
    for copy in copies:
        copy.start()
    for copy in copies:
        copy.wait()


def tile_sums(group, todo, store):
    parts, size = GROUPS[group], SIZES[group]
    return pl.pallas_call(
        lambda *refs: tile_kernel(group, *refs),
        out_shape=[jax.ShapeDtypeStruct((m, BLK, HALF), bf16) for _, m in parts],
        in_specs=[SMEM, ANY],
        out_specs=[VMEM if group else HBM] * len(parts),
        scratch_shapes=[
            pltpu.VMEM((size, BLK, HALF), bf16),
            pltpu.VMEM((SLOTS, BLK, BLK), bf16),
            pltpu.VMEM((SLOTS, BLK, HALF), bf16),
            pltpu.SemaphoreType.DMA((SLOTS,)),
            pltpu.SemaphoreType.DMA((SLOTS,)),
            pltpu.SemaphoreType.DMA((len(parts),)),
        ],
        compiler_params=pltpu.CompilerParams(vmem_limit_bytes=11 * MIB),
        cost_estimate=pl.CostEstimate(flops=10**9, bytes_accessed=2 * 10**7, transcendentals=0),
    )(todo, store)


def join_kernel(head, own, sib, out):
    out[:HEAD] = head[...]
    out[HEAD : HEAD + HALF] = own[...]
    out[HEAD + HALF :] = sib[...]


def join_chunk(head, own, sib):
    return pl.pallas_call(
        join_kernel,
        out_shape=jax.ShapeDtypeStruct((HEAD + 2 * HALF, HALF), bf16),
        in_specs=[VMEM] * 3,
        out_specs=VMEM,
        compiler_params=pltpu.CompilerParams(vmem_limit_bytes=4 * MIB),
    )(head, own, sib)


def weight_kernel(meta, grad_pre, feats, neigh, mine, other, source, sums, sems):
    loads = [pltpu.make_async_copy(v, source.at[j], sems.at[j]) for j, v in enumerate((feats, neigh))]
    for load in loads:
        load.start()
    core = meta[0]
    low, high = grad_pre[:, :HALF], grad_pre[:, HALF:]
    for load in loads:
        load.wait()
    stores = []
    for j, (out, from_low) in enumerate(((other, core == 1), (mine, core == 0))):
        part = jnp.where(from_low, low, high)
        bias = jnp.sum(part.astype(f32), axis=0, keepdims=True)
        for g in range(NY):
            cols = source[g // 2, :, (g % 2) * HALF : (g % 2 + 1) * HALF]
            sums[j, g, :, :HALF] = tile_product(cols, part)
            sums[j, g, :, HALF:] = jnp.zeros((HALF, BLK), f32)
            if g == 0:
                sums[j, g, 0:1, HALF:] = bias[:, :BLK]
                sums[j, g, 1:2, HALF:] = bias[:, BLK:]
        stores.append(pltpu.make_async_copy(sums.at[j], out, sems.at[2 + j]))
        stores[-1].start()
    for store in stores:
        store.wait()


def weight_terms(meta, feats, neigh, grad_pre):
    shape = (NY, HALF, HALF + BLK)
    return pl.pallas_call(
        weight_kernel,
        out_shape=[jax.ShapeDtypeStruct(shape, f32)] * 2,
        in_specs=[SMEM, VMEM, HBM, HBM],
        out_specs=[HBM] * 2,
        scratch_shapes=[
            pltpu.VMEM((2, *feats.shape), bf16),
            pltpu.VMEM((2, *shape), f32),
            pltpu.SemaphoreType.DMA((4,)),
        ],
        compiler_params=pltpu.CompilerParams(vmem_limit_bytes=8 * MIB),
        cost_estimate=pl.CostEstimate(flops=10**9, bytes_accessed=2 * 10**7, transcendentals=0),
    )(meta, grad_pre, feats, neigh)


def agg_kernel(meta, pre_act, cotan, w_neigh, grad_pre, agg_own, agg_other):
    grad = jnp.where(pre_act[...] > 0, cotan[...], jnp.zeros_like(cotan))
    grad_pre[...] = grad
    for out, half in ((agg_other, 1 - meta[0]), (agg_own, meta[0])):
        weight = w_neigh[pl.ds(pl.multiple_of(half * HALF, HALF), HALF), :]
        product = lax.dot_general(grad, weight, (((1,), (1,)), ((), ())), preferred_element_type=f32)
        out[...] = product.astype(bf16)


def agg_terms(meta, pre_act, cotan, w_neigh):
    half = jax.ShapeDtypeStruct((HALF, HALF), bf16)
    return pl.pallas_call(
        agg_kernel,
        out_shape=[jax.ShapeDtypeStruct(pre_act.shape, bf16), half, half],
        in_specs=[SMEM] + [VMEM] * 3,
        out_specs=[VMEM] * 3,
        compiler_params=pltpu.CompilerParams(vmem_limit_bytes=6 * MIB),
    )(meta, pre_act, cotan, w_neigh)


def join_kernel(head, own, sib, out):
    out[:HEAD] = head[...]
    out[HEAD : HEAD + HALF] = own[...]
    out[HEAD + HALF :] = sib[...]


def join_chunk(head, own, sib):
    return pl.pallas_call(
        join_kernel,
        out_shape=jax.ShapeDtypeStruct((HEAD + 2 * HALF, HALF), bf16),
        in_specs=[VMEM] * 3,
        out_specs=VMEM,
        compiler_params=pltpu.CompilerParams(vmem_limit_bytes=4 * MIB),
    )(head, own, sib)


def weight_kernel(meta, feats, neigh, grad_pre, mine, other):
    core = meta[0]
    low, high = grad_pre[:, :HALF], grad_pre[:, HALF:]
    for out, from_low in ((mine, core == 0), (other, core == 1)):
        part = jnp.where(from_low, low, high)
        bias = jnp.sum(part.astype(f32), axis=0, keepdims=True)
        for g in range(NY):
            source = feats if g < 2 else neigh
            cols = source[:, (g % 2) * HALF : (g % 2 + 1) * HALF]
            out[g, :, :HALF] = tile_product(cols, part)
            out[g, :, HALF:] = jnp.zeros((HALF, BLK), f32)
            if g == 0:
                out[g, 0:1, HALF:] = bias[:, :BLK]
                out[g, 1:2, HALF:] = bias[:, BLK:]


def weight_terms(meta, feats, neigh, grad_pre):
    return pl.pallas_call(
        weight_kernel,
        out_shape=[jax.ShapeDtypeStruct((NY, HALF, HALF + BLK), f32)] * 2,
        in_specs=[SMEM] + [VMEM] * 3,
        out_specs=[VMEM] * 2,
        compiler_params=pltpu.CompilerParams(vmem_limit_bytes=10 * MIB),
    )(meta, feats, neigh, grad_pre)


def scalars(kernel, sizes, *args):
    return pl.pallas_call(
        kernel,
        out_shape=[jax.ShapeDtypeStruct((n,), i32) for n in sizes],
        in_specs=[SMEM] * len(args),
        out_specs=[SMEM] * len(sizes),
        compiler_params=pltpu.CompilerParams(vmem_limit_bytes=3 * MIB),
    )(*args)


def add(*terms):
    total = terms[0].astype(f32)
    for term in terms[1:]:
        total = total + term.astype(f32)
    return total


def add_head(value, head):
    n = head.shape[0]
    return jnp.concatenate([add(value[:n], head).astype(bf16), value[n:].astype(bf16)])


def add_tail(value, tail):
    n = value.shape[0] - tail.shape[0]
    return jnp.concatenate([value[:n].astype(bf16), add(value[n:], tail).astype(bf16)])


def return_sums(first, sums_of, weights, join_weights):
    a2h, a2t, b4h, b4t, y2h, y2t = first
    w = next(weights)
    b4h, b4t, a2h, a2t, y2h, y2t, (a1, a3, b3, b5, y1, y3, b2, b6) = sums_of(1, (b4h, b4t, a2h, a2t, y2h, y2t))
    up, down = shift(b4h, "z", 1), shift(b4t, "z", -1)
    ax_p, ax_m = shift(a2h, "x", 1), shift(a2t, "x", -1)
    y_p = shift(y2h, "group", 1)

    up, down, ax_p, ax_m, y_p, y2t, a1, a3, b3, b5, w = bar((up, down, ax_p, ax_m, y_p, y2t, a1, a3, b3, b5, w))
    w = weights.send(w)
    up, down = shift(add_head(b3, up), "z", 1), shift(add_tail(b5, down), "z", -1)
    ax_p, ax_m = shift(add_head(a1, ax_p), "x", 1), shift(add_tail(a3, ax_m), "x", -1)
    y_p = shift(add_head(y1, y_p), "group", 1)

    up, down, y2t, (a0, b0, b1, b7) = sums_of(2, (up, down, y2t))
    up, down = add(b2, up).astype(bf16), add(b6, down).astype(bf16)
    up, down = shift(up, "z", 1), shift(down, "z", -1)
    y_m = shift(y2t, "group", -1)

    def part_a(dz):
        rows = slice(2 * dz, 2 * dz + 2)
        return add(a0[rows], ax_p[rows], ax_m[rows])

    def part_b(dx):
        rows = slice(2 * dx, 2 * dx + 2)
        cross = slice(8 + 2 * dx, 10 + 2 * dx)
        sums = add(b0[rows], up[rows], down[rows], y_p[cross], y_m[cross])
        return jnp.concatenate([sums, add(y_p[rows], y_m[rows])])

    up, down, ax_p, ax_m, y_p, y_m, a0, b1, b7 = bar((up, down, ax_p, ax_m, y_p, y_m, a0, b1, b7))
    far = part_a(4).astype(bf16)
    up, down = add(b1, up).astype(bf16), add(b7, down).astype(bf16)
    az_p, az_m = shift(far[:1], "z", 1), shift(far[1:], "z", -1)
    up, down = shift(up, "z", 1), shift(down, "z", -1)
    y_m = shift(add_tail(y3, y_m), "group", -1)
    az_p, az_m, w = bar((az_p, az_m, w))
    w = weights.send(w)
    az_p, az_m = add_head(part_a(3), az_p), add_tail(part_a(5), az_m)
    az_p, az_m = shift(az_p, "z", 1), shift(az_m, "z", -1)
    az_p, az_m = add(part_a(2), az_p).astype(bf16), add(part_a(6), az_m).astype(bf16)
    far = part_b(2).astype(bf16)
    az_p, az_m, far = bar((az_p, az_m, far))
    bx_p, bx_m = shift(far[:2], "x", 1), shift(far[2:], "x", -1)
    az_p, az_m = shift(az_p, "z", 1), shift(az_m, "z", -1)
    bx_p, bx_m = add_head(part_b(1), bx_p), add_tail(part_b(3), bx_m)
    az_p, az_m = add(part_a(1), az_p).astype(bf16), add(part_a(7), az_m).astype(bf16)
    az_p, az_m, bx_p, bx_m, w = bar((az_p, az_m, bx_p, bx_m, w))
    w_sib = shift(w, "core", 1)
    bx_p, bx_m = shift(bx_p, "x", 1), shift(bx_m, "x", -1)
    az_p, az_m = shift(az_p, "z", 1), shift(az_m, "z", -1)
    joined = join_weights(w, w_sib)
    az_p, az_m, bx_p, bx_m, *joined = bar((az_p, az_m, bx_p, bx_m, *joined))
    sum_b = add(part_b(0), bx_p, bx_m)
    return add(part_a(0), az_p, az_m, sum_b[2:]), sum_b[:2], joined


def body(
    feats,
    neigh,
    pre_act,
    cotan,
    w_self,
    w_neigh,
    send_list,
    send_live,
    cross_list,
    cross_live,
    home_tiles,
    home_target,
    home_source,
    far_tiles,
    far_target,
    far_source,
    far_count,
):
    y, z, x, core = (lax.axis_index(name) for name in AXES)
    meta = jnp.stack([core, z, x, y]).astype(i32)
    first_core = core == 0
    cols = (((1,), (1,)), ((), ()))
    ints = jnp.concatenate(
        [
            (send_live * 2 + send_list).reshape(-1),
            (cross_live * 2 + cross_list).reshape(-1),
            home_target[0, 0],
            home_source[0, 0],
            far_target[0, 0],
            far_source[0, 0],
            far_count[0],
            jnp.zeros((INTS - FC - 1,), i32),
        ]
    )
    row = jnp.stack([ints, shift(ints, "x", -1), shift(ints, "x", 2), shift(ints, "x", 1)])
    row = jnp.stack([row, shift(row, "core", 1)], axis=1)
    words = row[:, :, :CROSS].reshape(2, HALF).astype(bf16)
    cross_words = jnp.pad(row[:, :, CROSS:HT].reshape(1, BLK // 2).astype(bf16), ((0, 0), (0, HALF - BLK // 2)))
    row = row.reshape(-1)

    def join(mine, other):
        low, high = jnp.where(first_core, mine, other), jnp.where(first_core, other, mine)
        return jnp.concatenate([low, high], axis=-1)

    grad_pre = jnp.where(pre_act > 0, cotan, jnp.zeros_like(cotan))
    wn_mine = lax.dynamic_slice_in_dim(w_neigh, core * HALF, HALF)
    wn_other = lax.dynamic_slice_in_dim(w_neigh, (1 - core) * HALF, HALF)
    agg_other = lax.dot_general(grad_pre, wn_other, cols, preferred_element_type=f32).astype(bf16)
    agg_sib = shift(agg_other, "core", 1)
    agg_own = lax.dot_general(grad_pre, wn_mine, cols, preferred_element_type=f32).astype(bf16)
    head = jnp.concatenate([words, cross_words, jnp.zeros((HEAD - 3, HALF), bf16)])
    chunk = join_chunk(head, agg_own, agg_sib)

    far_own, home_own = far_tiles[0, 0], home_tiles[0, 0]
    far_sib, home_sib = shift(far_own, "core", 1), shift(home_own, "core", 1)
    chunk, far_sib, home_sib, grad_pre = bar((chunk, far_sib, home_sib, grad_pre))
    up1, dn1 = shift(chunk, "z", 1), shift(chunk, "z", -1)
    own3, own1 = shift(far_own, "x", 1), shift(far_own, "x", -1)
    mine, other = weight_terms(meta, feats, neigh, grad_pre)
    other = shift(other, "core", 1)
    store = deposit(None, chunk0=chunk, tiles0=far_own, tiles1=far_sib, tiles8=home_own, tiles9=home_sib)
    up1, dn1, own1, own3, chunk, row, mine, other, far_sib, store = bar(
        (up1, dn1, own1, own3, chunk, row, mine, other, far_sib, store)
    )
    store = deposit(store, chunk7=up1, chunk1=dn1, tiles2=own1, tiles6=own3)
    weights = (mine + other).reshape(4 * HALF, HALF + BLK)
    weights = lax.psum_scatter(weights, "group", scatter_dimension=0, tiled=True)
    up2, dn2 = shift(up1, "z", 1), shift(dn1, "z", -1)
    sib3, sib1 = shift(far_sib, "x", 1), shift(far_sib, "x", -1)
    y1 = shift(chunk, "group", 1)
    (picked,) = scalars(pick_kernel, (PICKED,), meta, row)
    up2, dn2, sib1, sib3, own3, chunk, picked, store = bar((up2, dn2, sib1, sib3, own3, chunk, picked, store))
    store = deposit(store, chunk6=up2, chunk2=dn2, tiles3=sib1, tiles7=sib3)
    up3, dn3 = shift(up2, "z", 1), shift(dn2, "z", -1)
    own2, sib2 = shift(own3, "x", 1), shift(sib1, "x", -1)
    y3 = shift(chunk, "group", 3)
    up3, dn3, own2, sib2, y1, chunk, weights, store = bar((up3, dn3, own2, sib2, y1, chunk, weights, store))
    store = deposit(store, chunk5=up3, chunk3=dn3, tiles4=own2, tiles5=sib2, chunk8=y1)
    weights = lax.psum_scatter(weights, "z", scatter_dimension=0, tiled=True)
    middle = HEAD + 2 * BLK
    up4, dn4 = shift(up3[:middle], "z", 1), shift(dn3[middle:], "z", -1)
    y2 = shift(chunk, "group", 2)
    up4, dn4, y2, y3, store = bar((up4, dn4, y2, y3, store))
    store = deposit(store, chunk4=up4, tail4=dn4, chunk9=y2, chunk10=y3)
    todo = list_tiles(meta, row, picked, store)

    def weight_stages(w):
        w = yield w
        w = jnp.pad(w, ((0, 16), (0, 0)))
        w = yield lax.all_gather(w, ("group", "x"), axis=0)
        w = jnp.sum(w.reshape(NY, NX, 48, HALF + BLK)[:, :, :32], axis=1)
        yield lax.all_gather(w, "z", axis=0)

    def sums_of(group, arrived):
        *arrived, now = bar((*arrived, todo))
        return *arrived, tile_sums(group, now, store)

    (first,) = sums_of(0, ())
    def rows_of(value):
        return value.transpose(1, 0, 2, 3).reshape(4 * HALF, HALF + BLK)

    def join_weights(mine, other):
        mine, other = rows_of(mine), rows_of(other)
        sums = join(mine[:, :HALF], other[:, :HALF])
        return sums[:512], sums[512:], join(mine[:2, HALF:].reshape(-1), other[:2, HALF:].reshape(-1))

    sum_a, sum_b, joined = return_sums(first, sums_of, weight_stages(weights), join_weights)
    self_grad = lax.dot_general(grad_pre, w_self, cols, preferred_element_type=f32)
    other = shift(sum_b, "core", 1)
    grad_input = self_grad + join(sum_a.reshape(2 * BLK, HALF), other.reshape(2 * BLK, HALF))
    return grad_input.astype(bf16), *joined


def solution(mesh):
    fine = Mesh(mesh.devices.reshape(NY, NZ, NX, 2), AXES)
    rows = P(AXES, None)
    part = lambda extra: P("group", DOM, *([None] * extra))
    return jax.shard_map(
        body,
        mesh=fine,
        in_specs=(rows,) * 4
        + (P(), P())
        + (part(1), part(1), part(2), part(2), part(3), part(1), part(1), part(3), part(1), part(1), part(0)),
        out_specs=(rows, P(), P(), P()),
        check_vma=False,
    )
```

```python
import jax
import jax.numpy as jnp
from jax import lax
from jax.experimental import pallas as pl
from jax.experimental.pallas import tpu as pltpu
from jax.sharding import Mesh
from jax.sharding import PartitionSpec as P

AXES = ("group", "z", "x", "core")
DOM = ("z", "x", "core")
NY, NZ, NX = 4, 8, 4
BLK, HALF = 128, 256
NT = 16
SLOTS = 32
bf16, f32, i32 = jnp.bfloat16, jnp.float32, jnp.int32

SEND, CROSS, HT, HS, FT, FS, FC, INTS = 0, 64, 72, 88, 104, 120, 136, 256
HEAD = 16
ENTRIES = 161
LIST = 1 + 3 * ENTRIES
HEADS, TILES, STORE = 48, 64, 1024
PICKED = 1 + 128

GROUPS = (
    ((0, 8), (8, 8), (16, 4), (20, 4), (24, 8), (32, 8)),
    ((0, 16), (16, 16), (32, 8), (40, 8), (48, 16), (64, 16), (80, 8), (88, 8)),
    ((0, 16), (16, 8), (24, 8), (32, 8)),
)
STARTS, SIZES = (0, 40, 136), (40, 96, 40)
MIB = 2**20

VMEM = pl.BlockSpec(memory_space=pltpu.VMEM)
SMEM = pl.BlockSpec(memory_space=pltpu.SMEM)
ANY = pl.BlockSpec(memory_space=pl.ANY)
HBM = pl.BlockSpec(memory_space=pltpu.HBM)


def shift(value, axis, k):
    n = {"group": NY, "z": NZ, "x": NX, "core": 2}[axis]
    return lax.ppermute(value, axis, [(i, (i + k) % n) for i in range(n)])


def pick_kernel(meta, row, out):
    x = meta[2]
    out[0] = 0
    for dx in range(NX):
        for r in range(2):
            base = (dx * 2 + r) * INTS

            @pl.loop(0, jnp.minimum(row[base + FC], NT))
            def _(t, dx=dx, r=r, base=base):
                slot = row[base + FT + t]
                column = ((slot - 2) >> 1) & 3
                here = jnp.where(slot < 66, column == x, dx == 0)

                @pl.when(here)
                def _():
                    n = out[0]
                    out[0] = n + 1
                    out[1 + n] = (dx * 2 + r) * NT + t


def deposit_kernel(plan, *refs):
    sources, (store, staged, sems) = refs[: len(plan)], refs[-3:]
    copies = []

    def copy(source, target):
        copies.append(pltpu.make_async_copy(source, target, sems.at[len(copies)]))
        copies[-1].start()

    loads = {}
    for source, (kind, i) in zip(sources, plan):
        if kind == "tiles":
            loads[i] = pltpu.make_async_copy(source, staged.at[len(loads)], sems.at[5 * len(plan) + len(loads)])
            loads[i].start()
    slots = {i: j for j, i in enumerate(loads)}
    for source, (kind, i) in sorted(zip(sources, plan), key=lambda pair: pair[1][0]):
        if kind == "tiles":
            loads[i].wait()
            source = staged.at[slots[i]]
            for half in range(2):
                lanes = pl.ds(half * BLK, BLK)
                copy(source.at[pl.ds(8 * half, 8)], store.at[pl.ds(TILES + 8 * i, 8), :, lanes])
            continue
        start, first = (0, 2) if kind == "tail" else (HEAD, 0)
        if kind != "tail":
            copy(source.at[pl.ds(0, HEAD)], store.at[HEADS + i, pl.ds(0, HEAD)])
        for j in range((source.shape[0] - start) // BLK):
            copy(source.at[pl.ds(start + BLK * j, BLK)], store.at[4 * i + first + j])
    for c in copies:
        c.wait()


def deposit(store, **arrived):
    plan = [(name.rstrip("0123456789"), int(name.strip("abcdefghijklmnopqrstuvwxyz"))) for name in arrived]
    old = [] if store is None else [store]
    return pl.pallas_call(
        lambda *refs: deposit_kernel(plan, *refs),
        out_shape=jax.ShapeDtypeStruct((STORE, BLK, HALF), bf16),
        in_specs=[ANY] * (len(plan) + len(old)),
        out_specs=ANY,
        input_output_aliases={len(plan): 0} if old else {},
        scratch_shapes=[
            pltpu.VMEM((4, NT, BLK, BLK), bf16),
            pltpu.SemaphoreType.DMA((5 * len(plan) + 4,)),
        ],
        compiler_params=pltpu.CompilerParams(vmem_limit_bytes=4 * MIB),
    )(*arrived.values(), *old)


def list_kernel(meta, row, picked, store, out, low, wide, words, sems):
    core, z, x, y = (meta[j] for j in range(4))
    heads = [store.at[HEADS + j, pl.ds(0, HEAD)] for j in range(11)]
    copies = [pltpu.make_async_copy(v, low.at[j], sems.at[j]) for j, v in enumerate(heads)]
    for copy in copies:
        copy.start()
    for copy in copies:
        copy.wait()
    wide[...] = low[...].astype(f32).astype(i32)
    copy = pltpu.make_async_copy(wide.at[:, pl.ds(0, 8)], words, sems.at[0])
    copy.start()
    copy.wait()
    for group in range(3):
        out[group * LIST] = 0

    def master(slot, dx, r):
        in_dom = slot < 66
        q = jnp.clip(slot - 2, 0, 63)
        dz = ((q >> 3) - z) & 7
        to_x = (((q >> 1) & 3) - x) & 3
        same = ((q & 1) ^ core)
        me = z * 8 + ((x + dx) & 3) * 2 + (core ^ r)
        v = jnp.clip(slot - 66, 0, 7)
        dy = ((v >> 1) - y) & 3
        word = jnp.where(
            in_dom,
            words[dz, to_x >> 1, ((to_x & 1) * 2 + same) * 64 + me],
            words[jnp.where(dy == 0, 0, 11 - dy), 2, (dx * 2 + r) * 8 + y * 2 + (v & 1)],
        )
        k = word & 1
        dz = jnp.where(in_dom, dz, 0)
        to_x = jnp.where(in_dom, to_x, dx)
        same = jnp.where(in_dom, same, r)
        dy = jnp.where(in_dom, 0, dy)
        return word >= 2, dy, dz, to_x, same, k

    def accumulator(slot, dx, r):
        live, dy, dz, to_x, same, k = master(slot, dx, r)
        own = slot < 2
        live = jnp.logical_or(own, live)
        dy, dz = jnp.where(own, 0, dy), jnp.where(own, 0, dz)
        to_x, same = jnp.where(own, dx, to_x), jnp.where(own, r, same)
        k = jnp.where(own, slot, k)
        a = jnp.where(to_x == 0, 136, jnp.where(to_x == 2, 0, 32 + 8 * to_x)) + dz * 2
        middle = jnp.where(dz == 4, 16, 72 + 4 * (dz - 3))
        outer = jnp.where(dz < 2, 152 + 8 * dz, jnp.where(dz == 7, 168, 116 + 2 * dz))
        b = jnp.where((dz - 4) * (dz - 4) < 2, middle, outer) + to_x * 2
        c = jnp.where(dy == 2, 24, jnp.where(dy == 1, 88, 104)) + r * 8 + dx * 2
        return live, jnp.where(dy > 0, c, jnp.where(same == 0, a, b)) + k

    def append(live, tile, block, place):
        middle, last = place >= STARTS[1], place >= STARTS[2]
        base = jnp.where(last, 2 * LIST, jnp.where(middle, LIST, 0))
        place = place - jnp.where(last, STARTS[2], jnp.where(middle, STARTS[1], 0))
        n = out[base]
        for j, value in enumerate((tile, block, place)):
            out[base + 1 + ENTRIES * j + n] = value
        out[base] = n + live.astype(i32)

    for r in range(2):

        @pl.loop(0, NT, unroll=4)
        def _(t, r=r):
            live, place = accumulator(row[r * INTS + HS + t], 0, r)
            append(live, (8 + r) * NT + t, 2 * r + row[r * INTS + HT + t], place)

    @pl.loop(0, picked[0])
    def _(i):
        which = picked[1 + i]
        dx, r, t = which >> 5, (which >> 4) & 1, which & 15
        base = (which >> 4) * INTS
        target_live, dy, dz, _, same, k = master(row[base + FT + t], dx, r)
        source_live, place = accumulator(row[base + FS + t], dx, r)
        source = jnp.where(dy > 0, 11 - dy, dz)
        append(jnp.logical_and(target_live, source_live), which, 4 * source + 2 * same + k, place)


def list_tiles(meta, row, picked, store):
    return pl.pallas_call(
        list_kernel,
        out_shape=jax.ShapeDtypeStruct((3 * LIST,), i32),
        in_specs=[SMEM] * 3 + [ANY],
        out_specs=SMEM,
        scratch_shapes=[
            pltpu.VMEM((11, HEAD, HALF), bf16),
            pltpu.VMEM((11, HEAD, HALF), i32),
            pltpu.SMEM((11, 8, HALF), i32),
            pltpu.SemaphoreType.DMA((11,)),
        ],
        compiler_params=pltpu.CompilerParams(vmem_limit_bytes=3 * MIB),
    )(meta, row, picked, store)


bar = lax.optimization_barrier


def tile_product(tile, block):
    return lax.dot_general(tile, block, (((0,), (0,)), ((), ())), preferred_element_type=f32)


def tile_kernel(group, todo, store, *refs):
    parts, base = GROUPS[group], group * LIST
    outs, (acc, tiles, blocks, tile_sems, block_sems, out_sems) = refs[: len(parts)], refs[len(parts) :]
    n = todo[base]

    def held(c):
        return jnp.clip(n - c * SLOTS, 0, SLOTS)

    def start(c):
        def one(j, _):
            i = base + 1 + c * SLOTS + j
            which = todo[i]
            row = TILES + ((which >> 4) << 3) + (which & 7)
            lanes = pl.ds(pl.multiple_of(((which >> 3) & 1) * BLK, BLK), BLK)
            pltpu.make_async_copy(store.at[row, :, lanes], tiles.at[j], tile_sems.at[j]).start()
            pltpu.make_async_copy(store.at[todo[i + ENTRIES]], blocks.at[j], block_sems.at[j]).start()
            return 0

        lax.fori_loop(0, held(c), one, 0)

    def finish(c):
        def one(j, _):
            place = todo[base + 1 + 2 * ENTRIES + c * SLOTS + j]
            pltpu.make_async_copy(store.at[0, :, pl.ds(0, BLK)], tiles.at[j], tile_sems.at[j]).wait()
            pltpu.make_async_copy(store.at[0], blocks.at[j], block_sems.at[j]).wait()
            term = tile_product(tiles[j], blocks[j])
            acc[place] = (acc[place].astype(f32) + term).astype(bf16)
            return 0

        lax.fori_loop(0, held(c), one, 0)

    start(0)

    @pl.loop(0, acc.shape[0])
    def _(b):
        acc[b] = jnp.zeros((BLK, HALF), bf16)

    def step(c, _):
        finish(c)
        start(c + 1)
        return 0

    lax.fori_loop(0, (n + SLOTS - 1) // SLOTS, step, 0)
    copies = [
        pltpu.make_async_copy(acc.at[pl.ds(s, m)], out, out_sems.at[j])
        for j, ((s, m), out) in enumerate(zip(parts, outs))
    ]
    for copy in copies:
        copy.start()
    for copy in copies:
        copy.wait()


def tile_sums(group, todo, store):
    parts, size = GROUPS[group], SIZES[group]
    return pl.pallas_call(
        lambda *refs: tile_kernel(group, *refs),
        out_shape=[jax.ShapeDtypeStruct((m, BLK, HALF), bf16) for _, m in parts],
        in_specs=[SMEM, ANY],
        out_specs=[VMEM if group else HBM] * len(parts),
        scratch_shapes=[
            pltpu.VMEM((size, BLK, HALF), bf16),
            pltpu.VMEM((SLOTS, BLK, BLK), bf16),
            pltpu.VMEM((SLOTS, BLK, HALF), bf16),
            pltpu.SemaphoreType.DMA((SLOTS,)),
            pltpu.SemaphoreType.DMA((SLOTS,)),
            pltpu.SemaphoreType.DMA((len(parts),)),
        ],
        compiler_params=pltpu.CompilerParams(vmem_limit_bytes=11 * MIB),
        cost_estimate=pl.CostEstimate(flops=10**9, bytes_accessed=2 * 10**7, transcendentals=0),
    )(todo, store)


def join_kernel(head, own, sib, out):
    out[:HEAD] = head[...]
    out[HEAD : HEAD + HALF] = own[...]
    out[HEAD + HALF :] = sib[...]


def join_chunk(head, own, sib):
    return pl.pallas_call(
        join_kernel,
        out_shape=jax.ShapeDtypeStruct((HEAD + 2 * HALF, HALF), bf16),
        in_specs=[VMEM] * 3,
        out_specs=VMEM,
        compiler_params=pltpu.CompilerParams(vmem_limit_bytes=4 * MIB),
    )(head, own, sib)


def weight_kernel(meta, grad_pre, feats, neigh, mine, other, source, sums, sems):
    loads = [pltpu.make_async_copy(v, source.at[j], sems.at[j]) for j, v in enumerate((feats, neigh))]
    for load in loads:
        load.start()
    core = meta[0]
    low, high = grad_pre[:, :HALF], grad_pre[:, HALF:]
    for load in loads:
        load.wait()
    stores = []
    for j, (out, from_low) in enumerate(((other, core == 1), (mine, core == 0))):
        part = jnp.where(from_low, low, high)
        bias = jnp.sum(part.astype(f32), axis=0, keepdims=True)
        for g in range(NY):
            cols = source[g // 2, :, (g % 2) * HALF : (g % 2 + 1) * HALF]
            sums[j, g, :, :HALF] = tile_product(cols, part)
            sums[j, g, :, HALF:] = jnp.zeros((HALF, BLK), f32)
            if g == 0:
                sums[j, g, 0:1, HALF:] = bias[:, :BLK]
                sums[j, g, 1:2, HALF:] = bias[:, BLK:]
        stores.append(pltpu.make_async_copy(sums.at[j], out, sems.at[2 + j]))
        stores[-1].start()
    for store in stores:
        store.wait()


def weight_terms(meta, feats, neigh, grad_pre):
    shape = (NY, HALF, HALF + BLK)
    return pl.pallas_call(
        weight_kernel,
        out_shape=[jax.ShapeDtypeStruct(shape, f32)] * 2,
        in_specs=[SMEM, VMEM, HBM, HBM],
        out_specs=[HBM] * 2,
        scratch_shapes=[
            pltpu.VMEM((2, *feats.shape), bf16),
            pltpu.VMEM((2, *shape), f32),
            pltpu.SemaphoreType.DMA((4,)),
        ],
        compiler_params=pltpu.CompilerParams(vmem_limit_bytes=8 * MIB),
        cost_estimate=pl.CostEstimate(flops=10**9, bytes_accessed=2 * 10**7, transcendentals=0),
    )(meta, grad_pre, feats, neigh)


def agg_kernel(meta, pre_act, cotan, w_neigh, grad_pre, agg_own, agg_other):
    grad = jnp.where(pre_act[...] > 0, cotan[...], jnp.zeros_like(cotan))
    grad_pre[...] = grad
    for out, half in ((agg_other, 1 - meta[0]), (agg_own, meta[0])):
        weight = w_neigh[pl.ds(pl.multiple_of(half * HALF, HALF), HALF), :]
        product = lax.dot_general(grad, weight, (((1,), (1,)), ((), ())), preferred_element_type=f32)
        out[...] = product.astype(bf16)


def agg_terms(meta, pre_act, cotan, w_neigh):
    half = jax.ShapeDtypeStruct((HALF, HALF), bf16)
    return pl.pallas_call(
        agg_kernel,
        out_shape=[jax.ShapeDtypeStruct(pre_act.shape, bf16), half, half],
        in_specs=[SMEM] + [VMEM] * 3,
        out_specs=[VMEM] * 3,
        compiler_params=pltpu.CompilerParams(vmem_limit_bytes=6 * MIB),
    )(meta, pre_act, cotan, w_neigh)


def join_kernel(head, own, sib, out):
    out[:HEAD] = head[...]
    out[HEAD : HEAD + HALF] = own[...]
    out[HEAD + HALF :] = sib[...]


def join_chunk(head, own, sib):
    return pl.pallas_call(
        join_kernel,
        out_shape=jax.ShapeDtypeStruct((HEAD + 2 * HALF, HALF), bf16),
        in_specs=[VMEM] * 3,
        out_specs=VMEM,
        compiler_params=pltpu.CompilerParams(vmem_limit_bytes=4 * MIB),
    )(head, own, sib)


def weight_kernel(meta, feats, neigh, grad_pre, mine, other):
    core = meta[0]
    low, high = grad_pre[:, :HALF], grad_pre[:, HALF:]
    for out, from_low in ((mine, core == 0), (other, core == 1)):
        part = jnp.where(from_low, low, high)
        bias = jnp.sum(part.astype(f32), axis=0, keepdims=True)
        for g in range(NY):
            source = feats if g < 2 else neigh
            cols = source[:, (g % 2) * HALF : (g % 2 + 1) * HALF]
            out[g, :, :HALF] = tile_product(cols, part)
            out[g, :, HALF:] = jnp.zeros((HALF, BLK), f32)
            if g == 0:
                out[g, 0:1, HALF:] = bias[:, :BLK]
                out[g, 1:2, HALF:] = bias[:, BLK:]


def weight_terms(meta, feats, neigh, grad_pre):
    return pl.pallas_call(
        weight_kernel,
        out_shape=[jax.ShapeDtypeStruct((NY, HALF, HALF + BLK), f32)] * 2,
        in_specs=[SMEM] + [VMEM] * 3,
        out_specs=[VMEM] * 2,
        compiler_params=pltpu.CompilerParams(vmem_limit_bytes=10 * MIB),
    )(meta, feats, neigh, grad_pre)


def scalars(kernel, sizes, *args):
    return pl.pallas_call(
        kernel,
        out_shape=[jax.ShapeDtypeStruct((n,), i32) for n in sizes],
        in_specs=[SMEM] * len(args),
        out_specs=[SMEM] * len(sizes),
        compiler_params=pltpu.CompilerParams(vmem_limit_bytes=3 * MIB),
    )(*args)


def add(*terms):
    total = terms[0].astype(f32)
    for term in terms[1:]:
        total = total + term.astype(f32)
    return total


def add_head(value, head):
    n = head.shape[0]
    return jnp.concatenate([add(value[:n], head).astype(bf16), value[n:].astype(bf16)])


def add_tail(value, tail):
    n = value.shape[0] - tail.shape[0]
    return jnp.concatenate([value[:n].astype(bf16), add(value[n:], tail).astype(bf16)])


def return_sums(first, sums_of, weights, join_weights):
    a2h, a2t, b4h, b4t, y2h, y2t = first
    w = next(weights)
    b4h, b4t, a2h, a2t, y2h, y2t, (a1, a3, b3, b5, y1, y3, b2, b6) = sums_of(1, (b4h, b4t, a2h, a2t, y2h, y2t))
    up, down = shift(b4h, "z", 1), shift(b4t, "z", -1)
    ax_p, ax_m = shift(a2h, "x", 1), shift(a2t, "x", -1)
    y_p = shift(y2h, "group", 1)

    up, down, ax_p, ax_m, y_p, y2t, a1, a3, b3, b5, w = bar((up, down, ax_p, ax_m, y_p, y2t, a1, a3, b3, b5, w))
    w = weights.send(w)
    up, down = shift(add_head(b3, up), "z", 1), shift(add_tail(b5, down), "z", -1)
    ax_p, ax_m = shift(add_head(a1, ax_p), "x", 1), shift(add_tail(a3, ax_m), "x", -1)
    y_m = shift(y2t, "group", -1)

    up, down, y_p, y_m, (a0, b0, b1, b7) = sums_of(2, (up, down, y_p, y_m))
    up, down = add(b2, up).astype(bf16), add(b6, down).astype(bf16)
    up, down = shift(up, "z", 1), shift(down, "z", -1)
    y_p = shift(add_head(y1, y_p), "group", 1)

    def part_a(dz):
        rows = slice(2 * dz, 2 * dz + 2)
        return add(a0[rows], ax_p[rows], ax_m[rows])

    def part_b(dx):
        rows = slice(2 * dx, 2 * dx + 2)
        cross = slice(8 + 2 * dx, 10 + 2 * dx)
        sums = add(b0[rows], up[rows], down[rows], y_p[cross], y_m[cross])
        return jnp.concatenate([sums, add(y_p[rows], y_m[rows])])

    up, down, ax_p, ax_m, y_m, a0, b1, b7 = bar((up, down, ax_p, ax_m, y_m, a0, b1, b7))
    far = part_a(4).astype(bf16)
    up, down = add(b1, up).astype(bf16), add(b7, down).astype(bf16)
    az_p, az_m = shift(far[:1], "z", 1), shift(far[1:], "z", -1)
    up, down = shift(up, "z", 1), shift(down, "z", -1)
    az_p, az_m, w, y_m = bar((az_p, az_m, w, y_m))
    w = weights.send(w)
    y_m = shift(add_tail(y3, y_m), "group", -1)
    az_p, az_m = add_head(part_a(3), az_p), add_tail(part_a(5), az_m)
    az_p, az_m = shift(az_p, "z", 1), shift(az_m, "z", -1)
    az_p, az_m = add(part_a(2), az_p).astype(bf16), add(part_a(6), az_m).astype(bf16)
    az_p, az_m = shift(az_p, "z", 1), shift(az_m, "z", -1)
    az_p, az_m, up, down, y_p, y_m = bar((az_p, az_m, up, down, y_p, y_m))
    far = part_b(2).astype(bf16)
    bx_p, bx_m = shift(far[:2], "x", 1), shift(far[2:], "x", -1)
    az_p, az_m = add(part_a(1), az_p).astype(bf16), add(part_a(7), az_m).astype(bf16)
    az_p, az_m = shift(az_p, "z", 1), shift(az_m, "z", -1)
    bx_p, bx_m = add_head(part_b(1), bx_p), add_tail(part_b(3), bx_m)
    az_p, az_m, bx_p, bx_m, w = bar((az_p, az_m, bx_p, bx_m, w))
    w_sib = shift(w, "core", 1)
    bx_p, bx_m = shift(bx_p, "x", 1), shift(bx_m, "x", -1)
    joined = join_weights(w, w_sib)
    bx_p, bx_m, *joined = bar((bx_p, bx_m, *joined))
    sum_b = add(part_b(0), bx_p, bx_m)
    return add(part_a(0), az_p, az_m, sum_b[2:]), sum_b[:2], joined


def body(
    feats,
    neigh,
    pre_act,
    cotan,
    w_self,
    w_neigh,
    send_list,
    send_live,
    cross_list,
    cross_live,
    home_tiles,
    home_target,
    home_source,
    far_tiles,
    far_target,
    far_source,
    far_count,
):
    y, z, x, core = (lax.axis_index(name) for name in AXES)
    meta = jnp.stack([core, z, x, y]).astype(i32)
    first_core = core == 0
    cols = (((1,), (1,)), ((), ()))
    ints = jnp.concatenate(
        [
            (send_live * 2 + send_list).reshape(-1),
            (cross_live * 2 + cross_list).reshape(-1),
            home_target[0, 0],
            home_source[0, 0],
            far_target[0, 0],
            far_source[0, 0],
            far_count[0],
            jnp.zeros((INTS - FC - 1,), i32),
        ]
    )
    row = jnp.stack([ints, shift(ints, "x", -1), shift(ints, "x", 2), shift(ints, "x", 1)])
    row = jnp.stack([row, shift(row, "core", 1)], axis=1)
    words = row[:, :, :CROSS].reshape(2, HALF).astype(bf16)
    cross_words = jnp.pad(row[:, :, CROSS:HT].reshape(1, BLK // 2).astype(bf16), ((0, 0), (0, HALF - BLK // 2)))
    row = row.reshape(-1)

    def join(mine, other):
        low, high = jnp.where(first_core, mine, other), jnp.where(first_core, other, mine)
        return jnp.concatenate([low, high], axis=-1)

    grad_pre = jnp.where(pre_act > 0, cotan, jnp.zeros_like(cotan))
    wn_mine = lax.dynamic_slice_in_dim(w_neigh, core * HALF, HALF)
    wn_other = lax.dynamic_slice_in_dim(w_neigh, (1 - core) * HALF, HALF)
    agg_other = lax.dot_general(grad_pre, wn_other, cols, preferred_element_type=f32).astype(bf16)
    agg_sib = shift(agg_other, "core", 1)
    agg_own = lax.dot_general(grad_pre, wn_mine, cols, preferred_element_type=f32).astype(bf16)
    head = jnp.concatenate([words, cross_words, jnp.zeros((HEAD - 3, HALF), bf16)])
    chunk = join_chunk(head, agg_own, agg_sib)

    far_own, home_own = far_tiles[0, 0], home_tiles[0, 0]
    far_sib, home_sib = shift(far_own, "core", 1), shift(home_own, "core", 1)
    chunk, far_sib, home_sib, grad_pre = bar((chunk, far_sib, home_sib, grad_pre))
    up1, dn1 = shift(chunk, "z", 1), shift(chunk, "z", -1)
    own3, own1 = shift(far_own, "x", 1), shift(far_own, "x", -1)
    mine, other = weight_terms(meta, feats, neigh, grad_pre)
    other = shift(other, "core", 1)
    store = deposit(None, chunk0=chunk, tiles0=far_own, tiles1=far_sib, tiles8=home_own, tiles9=home_sib)
    up1, dn1, own1, own3, chunk, row, mine, other, far_sib, store = bar(
        (up1, dn1, own1, own3, chunk, row, mine, other, far_sib, store)
    )
    store = deposit(store, chunk7=up1, chunk1=dn1, tiles2=own1, tiles6=own3)
    weights = (mine + other).reshape(4 * HALF, HALF + BLK)
    weights = lax.psum_scatter(weights, "group", scatter_dimension=0, tiled=True)
    up2, dn2 = shift(up1, "z", 1), shift(dn1, "z", -1)
    sib3, sib1 = shift(far_sib, "x", 1), shift(far_sib, "x", -1)
    y1 = shift(chunk, "group", 1)
    (picked,) = scalars(pick_kernel, (PICKED,), meta, row)
    up2, dn2, sib1, sib3, own3, chunk, picked, store = bar((up2, dn2, sib1, sib3, own3, chunk, picked, store))
    store = deposit(store, chunk6=up2, chunk2=dn2, tiles3=sib1, tiles7=sib3)
    up3, dn3 = shift(up2, "z", 1), shift(dn2, "z", -1)
    own2, sib2 = shift(own3, "x", 1), shift(sib1, "x", -1)
    y3 = shift(chunk, "group", 3)
    up3, dn3, own2, sib2, y1, chunk, weights, store = bar((up3, dn3, own2, sib2, y1, chunk, weights, store))
    store = deposit(store, chunk5=up3, chunk3=dn3, tiles4=own2, tiles5=sib2, chunk8=y1)
    weights = lax.psum_scatter(weights, "z", scatter_dimension=0, tiled=True)
    middle = HEAD + 2 * BLK
    up4, dn4 = shift(up3[:middle], "z", 1), shift(dn3[middle:], "z", -1)
    y2 = shift(chunk, "group", 2)
    up4, dn4, y2, y3, store = bar((up4, dn4, y2, y3, store))
    store = deposit(store, chunk4=up4, tail4=dn4, chunk9=y2, chunk10=y3)
    todo = list_tiles(meta, row, picked, store)

    def weight_stages(w):
        w = yield w
        w = jnp.pad(w, ((0, 16), (0, 0)))
        w = yield lax.all_gather(w, ("group", "x"), axis=0)
        w = jnp.sum(w.reshape(NY, NX, 48, HALF + BLK)[:, :, :32], axis=1)
        yield lax.all_gather(w, "z", axis=0)

    def sums_of(group, arrived):
        *arrived, now = bar((*arrived, todo))
        return *arrived, tile_sums(group, now, store)

    (first,) = sums_of(0, ())
    def rows_of(value):
        return value.transpose(1, 0, 2, 3).reshape(4 * HALF, HALF + BLK)

    def join_weights(mine, other):
        mine, other = rows_of(mine), rows_of(other)
        sums = join(mine[:, :HALF], other[:, :HALF])
        return sums[:512], sums[512:], join(mine[:2, HALF:].reshape(-1), other[:2, HALF:].reshape(-1))

    sum_a, sum_b, joined = return_sums(first, sums_of, weight_stages(weights), join_weights)
    self_grad = lax.dot_general(grad_pre, w_self, cols, preferred_element_type=f32)
    other = shift(sum_b, "core", 1)
    grad_input = self_grad + join(sum_a.reshape(2 * BLK, HALF), other.reshape(2 * BLK, HALF))
    return grad_input.astype(bf16), *joined


def solution(mesh):
    fine = Mesh(mesh.devices.reshape(NY, NZ, NX, 2), AXES)
    rows = P(AXES, None)
    part = lambda extra: P("group", DOM, *([None] * extra))
    return jax.shard_map(
        body,
        mesh=fine,
        in_specs=(rows,) * 4
        + (P(), P())
        + (part(1), part(1), part(2), part(2), part(3), part(1), part(1), part(3), part(1), part(1), part(0)),
        out_specs=(rows, P(), P(), P()),
        check_vma=False,
    )
```

```python
import jax
import jax.numpy as jnp
from jax import lax
from jax.experimental import pallas as pl
from jax.experimental.pallas import tpu as pltpu
from jax.sharding import Mesh
from jax.sharding import PartitionSpec as P

AXES = ("group", "z", "x", "core")
DOM = ("z", "x", "core")
NY, NZ, NX = 4, 8, 4
BLK, HALF = 128, 256
NT = 16
SLOTS = 32
bf16, f32, i32 = jnp.bfloat16, jnp.float32, jnp.int32

SEND, CROSS, HT, HS, FT, FS, FC, INTS = 0, 64, 72, 88, 104, 120, 136, 256
HEAD = 16
ENTRIES = 161
LIST = 1 + 3 * ENTRIES
HEADS, TILES, STORE = 48, 64, 1024
PICKED = 1 + 128

GROUPS = (
    ((0, 8), (8, 8), (16, 4), (20, 4), (24, 8), (32, 8)),
    ((0, 16), (16, 16), (32, 8), (40, 8), (48, 16), (64, 16), (80, 8), (88, 8)),
    ((0, 16), (16, 8), (24, 8), (32, 8)),
)
STARTS, SIZES = (0, 40, 136), (40, 96, 40)
MIB = 2**20

VMEM = pl.BlockSpec(memory_space=pltpu.VMEM)
SMEM = pl.BlockSpec(memory_space=pltpu.SMEM)
ANY = pl.BlockSpec(memory_space=pl.ANY)
HBM = pl.BlockSpec(memory_space=pltpu.HBM)


def shift(value, axis, k):
    n = {"group": NY, "z": NZ, "x": NX, "core": 2}[axis]
    return lax.ppermute(value, axis, [(i, (i + k) % n) for i in range(n)])


def pick_kernel(meta, row, out):
    x = meta[2]
    out[0] = 0
    for dx in range(NX):
        for r in range(2):
            base = (dx * 2 + r) * INTS

            @pl.loop(0, jnp.minimum(row[base + FC], NT))
            def _(t, dx=dx, r=r, base=base):
                slot = row[base + FT + t]
                column = ((slot - 2) >> 1) & 3
                here = jnp.where(slot < 66, column == x, dx == 0)

                @pl.when(here)
                def _():
                    n = out[0]
                    out[0] = n + 1
                    out[1 + n] = (dx * 2 + r) * NT + t


def deposit_kernel(plan, *refs):
    sources, (store, staged, sems) = refs[: len(plan)], refs[-3:]
    copies = []

    def copy(source, target):
        copies.append(pltpu.make_async_copy(source, target, sems.at[len(copies)]))
        copies[-1].start()

    loads = {}
    for source, (kind, i) in zip(sources, plan):
        if kind == "tiles":
            loads[i] = pltpu.make_async_copy(source, staged.at[len(loads)], sems.at[5 * len(plan) + len(loads)])
            loads[i].start()
    slots = {i: j for j, i in enumerate(loads)}
    for source, (kind, i) in sorted(zip(sources, plan), key=lambda pair: pair[1][0]):
        if kind == "tiles":
            loads[i].wait()
            source = staged.at[slots[i]]
            for half in range(2):
                lanes = pl.ds(half * BLK, BLK)
                copy(source.at[pl.ds(8 * half, 8)], store.at[pl.ds(TILES + 8 * i, 8), :, lanes])
            continue
        start, first = (0, 2) if kind == "tail" else (HEAD, 0)
        if kind != "tail":
            copy(source.at[pl.ds(0, HEAD)], store.at[HEADS + i, pl.ds(0, HEAD)])
        for j in range((source.shape[0] - start) // BLK):
            copy(source.at[pl.ds(start + BLK * j, BLK)], store.at[4 * i + first + j])
    for c in copies:
        c.wait()


def deposit(store, **arrived):
    plan = [(name.rstrip("0123456789"), int(name.strip("abcdefghijklmnopqrstuvwxyz"))) for name in arrived]
    old = [] if store is None else [store]
    return pl.pallas_call(
        lambda *refs: deposit_kernel(plan, *refs),
        out_shape=jax.ShapeDtypeStruct((STORE, BLK, HALF), bf16),
        in_specs=[ANY] * (len(plan) + len(old)),
        out_specs=ANY,
        input_output_aliases={len(plan): 0} if old else {},
        scratch_shapes=[
            pltpu.VMEM((4, NT, BLK, BLK), bf16),
            pltpu.SemaphoreType.DMA((5 * len(plan) + 4,)),
        ],
        compiler_params=pltpu.CompilerParams(vmem_limit_bytes=4 * MIB),
    )(*arrived.values(), *old)


def list_kernel(meta, row, picked, store, out, low, wide, words, sems):
    core, z, x, y = (meta[j] for j in range(4))
    heads = [store.at[HEADS + j, pl.ds(0, HEAD)] for j in range(11)]
    copies = [pltpu.make_async_copy(v, low.at[j], sems.at[j]) for j, v in enumerate(heads)]
    for copy in copies:
        copy.start()
    for copy in copies:
        copy.wait()
    wide[...] = low[...].astype(f32).astype(i32)
    copy = pltpu.make_async_copy(wide.at[:, pl.ds(0, 8)], words, sems.at[0])
    copy.start()
    copy.wait()
    for group in range(3):
        out[group * LIST] = 0

    def master(slot, dx, r):
        in_dom = slot < 66
        q = jnp.clip(slot - 2, 0, 63)
        dz = ((q >> 3) - z) & 7
        to_x = (((q >> 1) & 3) - x) & 3
        same = ((q & 1) ^ core)
        me = z * 8 + ((x + dx) & 3) * 2 + (core ^ r)
        v = jnp.clip(slot - 66, 0, 7)
        dy = ((v >> 1) - y) & 3
        word = jnp.where(
            in_dom,
            words[dz, to_x >> 1, ((to_x & 1) * 2 + same) * 64 + me],
            words[jnp.where(dy == 0, 0, 11 - dy), 2, (dx * 2 + r) * 8 + y * 2 + (v & 1)],
        )
        k = word & 1
        dz = jnp.where(in_dom, dz, 0)
        to_x = jnp.where(in_dom, to_x, dx)
        same = jnp.where(in_dom, same, r)
        dy = jnp.where(in_dom, 0, dy)
        return word >= 2, dy, dz, to_x, same, k

    def accumulator(slot, dx, r):
        live, dy, dz, to_x, same, k = master(slot, dx, r)
        own = slot < 2
        live = jnp.logical_or(own, live)
        dy, dz = jnp.where(own, 0, dy), jnp.where(own, 0, dz)
        to_x, same = jnp.where(own, dx, to_x), jnp.where(own, r, same)
        k = jnp.where(own, slot, k)
        a = jnp.where(to_x == 0, 136, jnp.where(to_x == 2, 0, 32 + 8 * to_x)) + dz * 2
        middle = jnp.where(dz == 4, 16, 72 + 4 * (dz - 3))
        outer = jnp.where(dz < 2, 152 + 8 * dz, jnp.where(dz == 7, 168, 116 + 2 * dz))
        b = jnp.where((dz - 4) * (dz - 4) < 2, middle, outer) + to_x * 2
        c = jnp.where(dy == 2, 24, jnp.where(dy == 1, 88, 104)) + r * 8 + dx * 2
        return live, jnp.where(dy > 0, c, jnp.where(same == 0, a, b)) + k

    def append(live, tile, block, place):
        middle, last = place >= STARTS[1], place >= STARTS[2]
        base = jnp.where(last, 2 * LIST, jnp.where(middle, LIST, 0))
        place = place - jnp.where(last, STARTS[2], jnp.where(middle, STARTS[1], 0))
        n = out[base]
        for j, value in enumerate((tile, block, place)):
            out[base + 1 + ENTRIES * j + n] = value
        out[base] = n + live.astype(i32)

    for r in range(2):

        @pl.loop(0, NT, unroll=4)
        def _(t, r=r):
            live, place = accumulator(row[r * INTS + HS + t], 0, r)
            append(live, (8 + r) * NT + t, 2 * r + row[r * INTS + HT + t], place)

    @pl.loop(0, picked[0])
    def _(i):
        which = picked[1 + i]
        dx, r, t = which >> 5, (which >> 4) & 1, which & 15
        base = (which >> 4) * INTS
        target_live, dy, dz, _, same, k = master(row[base + FT + t], dx, r)
        source_live, place = accumulator(row[base + FS + t], dx, r)
        source = jnp.where(dy > 0, 11 - dy, dz)
        append(jnp.logical_and(target_live, source_live), which, 4 * source + 2 * same + k, place)


def list_tiles(meta, row, picked, store):
    return pl.pallas_call(
        list_kernel,
        out_shape=jax.ShapeDtypeStruct((3 * LIST,), i32),
        in_specs=[SMEM] * 3 + [ANY],
        out_specs=SMEM,
        scratch_shapes=[
            pltpu.VMEM((11, HEAD, HALF), bf16),
            pltpu.VMEM((11, HEAD, HALF), i32),
            pltpu.SMEM((11, 8, HALF), i32),
            pltpu.SemaphoreType.DMA((11,)),
        ],
        compiler_params=pltpu.CompilerParams(vmem_limit_bytes=3 * MIB),
    )(meta, row, picked, store)


bar = lax.optimization_barrier


def tile_product(tile, block):
    return lax.dot_general(tile, block, (((0,), (0,)), ((), ())), preferred_element_type=f32)


def tile_kernel(group, todo, store, *refs):
    parts, base = GROUPS[group], group * LIST
    outs, (acc, tiles, blocks, tile_sems, block_sems, out_sems) = refs[: len(parts)], refs[len(parts) :]
    n = todo[base]

    def held(c):
        return jnp.clip(n - c * SLOTS, 0, SLOTS)

    def start(c):
        def one(j, _):
            i = base + 1 + c * SLOTS + j
            which = todo[i]
            row = TILES + ((which >> 4) << 3) + (which & 7)
            lanes = pl.ds(pl.multiple_of(((which >> 3) & 1) * BLK, BLK), BLK)
            pltpu.make_async_copy(store.at[row, :, lanes], tiles.at[j], tile_sems.at[j]).start()
            pltpu.make_async_copy(store.at[todo[i + ENTRIES]], blocks.at[j], block_sems.at[j]).start()
            return 0

        lax.fori_loop(0, held(c), one, 0)

    def finish(c):
        def one(j, _):
            place = todo[base + 1 + 2 * ENTRIES + c * SLOTS + j]
            pltpu.make_async_copy(store.at[0, :, pl.ds(0, BLK)], tiles.at[j], tile_sems.at[j]).wait()
            pltpu.make_async_copy(store.at[0], blocks.at[j], block_sems.at[j]).wait()
            term = tile_product(tiles[j], blocks[j])
            acc[place] = (acc[place].astype(f32) + term).astype(bf16)
            return 0

        lax.fori_loop(0, held(c), one, 0)

    start(0)

    @pl.loop(0, acc.shape[0])
    def _(b):
        acc[b] = jnp.zeros((BLK, HALF), bf16)

    def step(c, _):
        finish(c)
        start(c + 1)
        return 0

    lax.fori_loop(0, (n + SLOTS - 1) // SLOTS, step, 0)
    copies = [
        pltpu.make_async_copy(acc.at[pl.ds(s, m)], out, out_sems.at[j])
        for j, ((s, m), out) in enumerate(zip(parts, outs))
    ]
    for copy in copies:
        copy.start()
    for copy in copies:
        copy.wait()


def tile_sums(group, todo, store):
    parts, size = GROUPS[group], SIZES[group]
    return pl.pallas_call(
        lambda *refs: tile_kernel(group, *refs),
        out_shape=[jax.ShapeDtypeStruct((m, BLK, HALF), bf16) for _, m in parts],
        in_specs=[SMEM, ANY],
        out_specs=[VMEM if group else HBM] * len(parts),
        scratch_shapes=[
            pltpu.VMEM((size, BLK, HALF), bf16),
            pltpu.VMEM((SLOTS, BLK, BLK), bf16),
            pltpu.VMEM((SLOTS, BLK, HALF), bf16),
            pltpu.SemaphoreType.DMA((SLOTS,)),
            pltpu.SemaphoreType.DMA((SLOTS,)),
            pltpu.SemaphoreType.DMA((len(parts),)),
        ],
        compiler_params=pltpu.CompilerParams(vmem_limit_bytes=11 * MIB),
        cost_estimate=pl.CostEstimate(flops=10**9, bytes_accessed=2 * 10**7, transcendentals=0),
    )(todo, store)


def join_kernel(head, own, sib, out):
    out[:HEAD] = head[...]
    out[HEAD : HEAD + HALF] = own[...]
    out[HEAD + HALF :] = sib[...]


def join_chunk(head, own, sib):
    return pl.pallas_call(
        join_kernel,
        out_shape=jax.ShapeDtypeStruct((HEAD + 2 * HALF, HALF), bf16),
        in_specs=[VMEM] * 3,
        out_specs=VMEM,
        compiler_params=pltpu.CompilerParams(vmem_limit_bytes=4 * MIB),
    )(head, own, sib)


def weight_kernel(meta, feats, neigh, grad_pre, mine, other):
    core = meta[0]
    low, high = grad_pre[:, :HALF], grad_pre[:, HALF:]
    for out, from_low in ((mine, core == 0), (other, core == 1)):
        part = jnp.where(from_low, low, high)
        bias = jnp.sum(part.astype(f32), axis=0, keepdims=True)
        for g in range(NY):
            source = feats if g < 2 else neigh
            cols = source[:, (g % 2) * HALF : (g % 2 + 1) * HALF]
            out[g, :, :HALF] = tile_product(cols, part)
            out[g, :, HALF:] = jnp.zeros((HALF, BLK), f32)
            if g == 0:
                out[g, 0:1, HALF:] = bias[:, :BLK]
                out[g, 1:2, HALF:] = bias[:, BLK:]


def weight_terms(meta, feats, neigh, grad_pre):
    return pl.pallas_call(
        weight_kernel,
        out_shape=[jax.ShapeDtypeStruct((NY, HALF, HALF + BLK), f32)] * 2,
        in_specs=[SMEM] + [VMEM] * 3,
        out_specs=[VMEM] * 2,
        compiler_params=pltpu.CompilerParams(vmem_limit_bytes=10 * MIB),
    )(meta, feats, neigh, grad_pre)


def scalars(kernel, sizes, *args):
    return pl.pallas_call(
        kernel,
        out_shape=[jax.ShapeDtypeStruct((n,), i32) for n in sizes],
        in_specs=[SMEM] * len(args),
        out_specs=[SMEM] * len(sizes),
        compiler_params=pltpu.CompilerParams(vmem_limit_bytes=3 * MIB),
    )(*args)


def add(*terms):
    total = terms[0].astype(f32)
    for term in terms[1:]:
        total = total + term.astype(f32)
    return total


def add_head(value, head):
    n = head.shape[0]
    return jnp.concatenate([add(value[:n], head).astype(bf16), value[n:].astype(bf16)])


def add_tail(value, tail):
    n = value.shape[0] - tail.shape[0]
    return jnp.concatenate([value[:n].astype(bf16), add(value[n:], tail).astype(bf16)])


def return_sums(first, sums_of, weights, join_weights):
    a2h, a2t, b4h, b4t, y2h, y2t = first
    w = next(weights)
    b4h, b4t, a2h, a2t, y2h, y2t, (a1, a3, b3, b5, y1, y3, b2, b6) = sums_of(1, (b4h, b4t, a2h, a2t, y2h, y2t))
    up, down = shift(b4h, "z", 1), shift(b4t, "z", -1)
    ax_p, ax_m = shift(a2h, "x", 1), shift(a2t, "x", -1)
    y_p = shift(y2h, "group", 1)

    up, down, ax_p, ax_m, y_p, y2t, a1, a3, b3, b5, w = bar((up, down, ax_p, ax_m, y_p, y2t, a1, a3, b3, b5, w))
    w = weights.send(w)
    up, down = shift(add_head(b3, up), "z", 1), shift(add_tail(b5, down), "z", -1)
    ax_p, ax_m = shift(add_head(a1, ax_p), "x", 1), shift(add_tail(a3, ax_m), "x", -1)
    y_m = shift(y2t, "group", -1)

    up, down, y_p, y_m, (a0, b0, b1, b7) = sums_of(2, (up, down, y_p, y_m))
    up, down = add(b2, up).astype(bf16), add(b6, down).astype(bf16)
    up, down = shift(up, "z", 1), shift(down, "z", -1)
    y_p = shift(add_head(y1, y_p), "group", 1)

    def part_a(dz):
        rows = slice(2 * dz, 2 * dz + 2)
        return add(a0[rows], ax_p[rows], ax_m[rows])

    def part_b(dx):
        rows = slice(2 * dx, 2 * dx + 2)
        cross = slice(8 + 2 * dx, 10 + 2 * dx)
        sums = add(b0[rows], up[rows], down[rows], y_p[cross], y_m[cross])
        return jnp.concatenate([sums, add(y_p[rows], y_m[rows])])

    up, down, ax_p, ax_m, y_m, a0, b1, b7 = bar((up, down, ax_p, ax_m, y_m, a0, b1, b7))
    up, down, minus = add(b1, up).astype(bf16), add(b7, down).astype(bf16), add_tail(y3, y_m)
    up, down, minus = bar((up, down, minus))
    up, down = shift(up, "z", 1), shift(down, "z", -1)
    y_m = shift(minus, "group", -1)
    far, y_p, w = bar((part_a(4).astype(bf16), y_p, w))
    w = weights.send(w)
    az_p, az_m = shift(far[:1], "z", 1), shift(far[1:], "z", -1)
    az_p, az_m = add_head(part_a(3), az_p), add_tail(part_a(5), az_m)
    az_p, az_m = shift(az_p, "z", 1), shift(az_m, "z", -1)
    az_p, az_m = add(part_a(2), az_p).astype(bf16), add(part_a(6), az_m).astype(bf16)
    az_p, az_m = shift(az_p, "z", 1), shift(az_m, "z", -1)
    az_p, az_m, up, down, y_p, y_m = bar((az_p, az_m, up, down, y_p, y_m))
    far = part_b(2).astype(bf16)
    bx_p, bx_m = shift(far[:2], "x", 1), shift(far[2:], "x", -1)
    az_p, az_m = add(part_a(1), az_p).astype(bf16), add(part_a(7), az_m).astype(bf16)
    az_p, az_m = shift(az_p, "z", 1), shift(az_m, "z", -1)
    bx_p, bx_m = add_head(part_b(1), bx_p), add_tail(part_b(3), bx_m)
    az_p, az_m, bx_p, bx_m, w = bar((az_p, az_m, bx_p, bx_m, w))
    w_sib = shift(w, "core", 1)
    bx_p, bx_m = shift(bx_p, "x", 1), shift(bx_m, "x", -1)
    joined = join_weights(w, w_sib)
    bx_p, bx_m, *joined = bar((bx_p, bx_m, *joined))
    sum_b = add(part_b(0), bx_p, bx_m)
    return add(part_a(0), az_p, az_m, sum_b[2:]), sum_b[:2], joined


def body(
    feats,
    neigh,
    pre_act,
    cotan,
    w_self,
    w_neigh,
    send_list,
    send_live,
    cross_list,
    cross_live,
    home_tiles,
    home_target,
    home_source,
    far_tiles,
    far_target,
    far_source,
    far_count,
):
    y, z, x, core = (lax.axis_index(name) for name in AXES)
    meta = jnp.stack([core, z, x, y]).astype(i32)
    first_core = core == 0
    cols = (((1,), (1,)), ((), ()))
    ints = jnp.concatenate(
        [
            (send_live * 2 + send_list).reshape(-1),
            (cross_live * 2 + cross_list).reshape(-1),
            home_target[0, 0],
            home_source[0, 0],
            far_target[0, 0],
            far_source[0, 0],
            far_count[0],
            jnp.zeros((INTS - FC - 1,), i32),
        ]
    )
    row = jnp.stack([ints, shift(ints, "x", -1), shift(ints, "x", 2), shift(ints, "x", 1)])
    row = jnp.stack([row, shift(row, "core", 1)], axis=1)
    words = row[:, :, :CROSS].reshape(2, HALF).astype(bf16)
    cross_words = jnp.pad(row[:, :, CROSS:HT].reshape(1, BLK // 2).astype(bf16), ((0, 0), (0, HALF - BLK // 2)))
    row = row.reshape(-1)

    def join(mine, other):
        low, high = jnp.where(first_core, mine, other), jnp.where(first_core, other, mine)
        return jnp.concatenate([low, high], axis=-1)

    grad_pre = jnp.where(pre_act > 0, cotan, jnp.zeros_like(cotan))
    wn_mine = lax.dynamic_slice_in_dim(w_neigh, core * HALF, HALF)
    wn_other = lax.dynamic_slice_in_dim(w_neigh, (1 - core) * HALF, HALF)
    agg_other = lax.dot_general(grad_pre, wn_other, cols, preferred_element_type=f32).astype(bf16)
    agg_sib = shift(agg_other, "core", 1)
    agg_own = lax.dot_general(grad_pre, wn_mine, cols, preferred_element_type=f32).astype(bf16)
    head = jnp.concatenate([words, cross_words, jnp.zeros((HEAD - 3, HALF), bf16)])
    chunk = join_chunk(head, agg_own, agg_sib)

    far_own, home_own = far_tiles[0, 0], home_tiles[0, 0]
    far_sib, home_sib = shift(far_own, "core", 1), shift(home_own, "core", 1)
    chunk, far_sib, home_sib, grad_pre = bar((chunk, far_sib, home_sib, grad_pre))
    up1, dn1 = shift(chunk, "z", 1), shift(chunk, "z", -1)
    own3, own1 = shift(far_own, "x", 1), shift(far_own, "x", -1)
    mine, other = weight_terms(meta, feats, neigh, grad_pre)
    other = shift(other, "core", 1)
    store = deposit(None, chunk0=chunk, tiles0=far_own, tiles1=far_sib, tiles8=home_own, tiles9=home_sib)
    up1, dn1, own1, own3, chunk, row, mine, other, far_sib, store = bar(
        (up1, dn1, own1, own3, chunk, row, mine, other, far_sib, store)
    )
    store = deposit(store, chunk7=up1, chunk1=dn1, tiles2=own1, tiles6=own3)
    weights = (mine + other).reshape(4 * HALF, HALF + BLK)
    weights = lax.psum_scatter(weights, "group", scatter_dimension=0, tiled=True)
    up2, dn2 = shift(up1, "z", 1), shift(dn1, "z", -1)
    sib3, sib1 = shift(far_sib, "x", 1), shift(far_sib, "x", -1)
    y1 = shift(chunk, "group", 1)
    (picked,) = scalars(pick_kernel, (PICKED,), meta, row)
    up2, dn2, sib1, sib3, own3, chunk, picked, store = bar((up2, dn2, sib1, sib3, own3, chunk, picked, store))
    store = deposit(store, chunk6=up2, chunk2=dn2, tiles3=sib1, tiles7=sib3)
    up3, dn3 = shift(up2, "z", 1), shift(dn2, "z", -1)
    own2, sib2 = shift(own3, "x", 1), shift(sib1, "x", -1)
    y3 = shift(chunk, "group", 3)
    up3, dn3, own2, sib2, y1, chunk, weights, store = bar((up3, dn3, own2, sib2, y1, chunk, weights, store))
    store = deposit(store, chunk5=up3, chunk3=dn3, tiles4=own2, tiles5=sib2, chunk8=y1)
    weights = lax.psum_scatter(weights, "z", scatter_dimension=0, tiled=True)
    middle = HEAD + 2 * BLK
    up4, dn4 = shift(up3[:middle], "z", 1), shift(dn3[middle:], "z", -1)
    y2 = shift(chunk, "group", 2)
    up4, dn4, y2, y3, store = bar((up4, dn4, y2, y3, store))
    store = deposit(store, chunk4=up4, tail4=dn4, chunk9=y2, chunk10=y3)
    todo = list_tiles(meta, row, picked, store)

    def weight_stages(w):
        w = yield w
        w = jnp.pad(w, ((0, 16), (0, 0)))
        w = yield lax.all_gather(w, ("group", "x"), axis=0)
        w = jnp.sum(w.reshape(NY, NX, 48, HALF + BLK)[:, :, :32], axis=1)
        yield lax.all_gather(w, "z", axis=0)

    def sums_of(group, arrived):
        *arrived, now = bar((*arrived, todo))
        return *arrived, tile_sums(group, now, store)

    (first,) = sums_of(0, ())
    def rows_of(value):
        return value.transpose(1, 0, 2, 3).reshape(4 * HALF, HALF + BLK)

    def join_weights(mine, other):
        mine, other = rows_of(mine), rows_of(other)
        sums = join(mine[:, :HALF], other[:, :HALF])
        return sums[:512], sums[512:], join(mine[:2, HALF:].reshape(-1), other[:2, HALF:].reshape(-1))

    sum_a, sum_b, joined = return_sums(first, sums_of, weight_stages(weights), join_weights)
    self_grad = lax.dot_general(grad_pre, w_self, cols, preferred_element_type=f32)
    other = shift(sum_b, "core", 1)
    grad_input = self_grad + join(sum_a.reshape(2 * BLK, HALF), other.reshape(2 * BLK, HALF))
    return grad_input.astype(bf16), *joined


def solution(mesh):
    fine = Mesh(mesh.devices.reshape(NY, NZ, NX, 2), AXES)
    rows = P(AXES, None)
    part = lambda extra: P("group", DOM, *([None] * extra))
    return jax.shard_map(
        body,
        mesh=fine,
        in_specs=(rows,) * 4
        + (P(), P())
        + (part(1), part(1), part(2), part(2), part(3), part(1), part(1), part(3), part(1), part(1), part(0)),
        out_specs=(rows, P(), P(), P()),
        check_vma=False,
    )
```

```python
import jax
import jax.numpy as jnp
from jax import lax
from jax.experimental import pallas as pl
from jax.experimental.pallas import tpu as pltpu
from jax.sharding import Mesh
from jax.sharding import PartitionSpec as P

AXES = ("group", "z", "x", "core")
DOM = ("z", "x", "core")
NY, NZ, NX = 4, 8, 4
BLK, HALF = 128, 256
NT = 16
SLOTS = 32
bf16, f32, i32 = jnp.bfloat16, jnp.float32, jnp.int32

SEND, CROSS, HT, HS, FT, FS, FC, INTS = 0, 64, 72, 88, 104, 120, 136, 256
HEAD = 16
ENTRIES = 161
LIST = 1 + 3 * ENTRIES
HEADS, TILES, STORE = 48, 64, 1024
PICKED = 1 + 128

GROUPS = (
    ((0, 8), (8, 8), (16, 4), (20, 4), (24, 8), (32, 8)),
    ((0, 16), (16, 16), (32, 8), (40, 8), (48, 16), (64, 16), (80, 8), (88, 8)),
    ((0, 16), (16, 8), (24, 8), (32, 8)),
)
STARTS, SIZES = (0, 40, 136), (40, 96, 40)
MIB = 2**20

VMEM = pl.BlockSpec(memory_space=pltpu.VMEM)
SMEM = pl.BlockSpec(memory_space=pltpu.SMEM)
ANY = pl.BlockSpec(memory_space=pl.ANY)
HBM = pl.BlockSpec(memory_space=pltpu.HBM)


def shift(value, axis, k):
    n = {"group": NY, "z": NZ, "x": NX, "core": 2}[axis]
    return lax.ppermute(value, axis, [(i, (i + k) % n) for i in range(n)])


def pick_kernel(meta, row, out):
    x = meta[2]
    out[0] = 0
    for dx in range(NX):
        for r in range(2):
            base = (dx * 2 + r) * INTS

            @pl.loop(0, jnp.minimum(row[base + FC], NT))
            def _(t, dx=dx, r=r, base=base):
                slot = row[base + FT + t]
                column = ((slot - 2) >> 1) & 3
                here = jnp.where(slot < 66, column == x, dx == 0)

                @pl.when(here)
                def _():
                    n = out[0]
                    out[0] = n + 1
                    out[1 + n] = (dx * 2 + r) * NT + t


def deposit_kernel(plan, *refs):
    sources, (store, staged, sems) = refs[: len(plan)], refs[-3:]
    copies = []

    def copy(source, target):
        copies.append(pltpu.make_async_copy(source, target, sems.at[len(copies)]))
        copies[-1].start()

    loads = {}
    for source, (kind, i) in zip(sources, plan):
        if kind == "tiles":
            loads[i] = pltpu.make_async_copy(source, staged.at[len(loads)], sems.at[5 * len(plan) + len(loads)])
            loads[i].start()
    slots = {i: j for j, i in enumerate(loads)}
    for source, (kind, i) in sorted(zip(sources, plan), key=lambda pair: pair[1][0]):
        if kind == "tiles":
            loads[i].wait()
            source = staged.at[slots[i]]
            for half in range(2):
                lanes = pl.ds(half * BLK, BLK)
                copy(source.at[pl.ds(8 * half, 8)], store.at[pl.ds(TILES + 8 * i, 8), :, lanes])
            continue
        start, first = (0, 2) if kind == "tail" else (HEAD, 0)
        if kind != "tail":
            copy(source.at[pl.ds(0, HEAD)], store.at[HEADS + i, pl.ds(0, HEAD)])
        for j in range((source.shape[0] - start) // BLK):
            copy(source.at[pl.ds(start + BLK * j, BLK)], store.at[4 * i + first + j])
    for c in copies:
        c.wait()


def deposit(store, **arrived):
    plan = [(name.rstrip("0123456789"), int(name.strip("abcdefghijklmnopqrstuvwxyz"))) for name in arrived]
    old = [] if store is None else [store]
    return pl.pallas_call(
        lambda *refs: deposit_kernel(plan, *refs),
        out_shape=jax.ShapeDtypeStruct((STORE, BLK, HALF), bf16),
        in_specs=[ANY] * (len(plan) + len(old)),
        out_specs=ANY,
        input_output_aliases={len(plan): 0} if old else {},
        scratch_shapes=[
            pltpu.VMEM((4, NT, BLK, BLK), bf16),
            pltpu.SemaphoreType.DMA((5 * len(plan) + 4,)),
        ],
        compiler_params=pltpu.CompilerParams(vmem_limit_bytes=4 * MIB),
    )(*arrived.values(), *old)


def list_kernel(meta, row, picked, store, out, low, wide, words, sems):
    core, z, x, y = (meta[j] for j in range(4))
    heads = [store.at[HEADS + j, pl.ds(0, HEAD)] for j in range(11)]
    copies = [pltpu.make_async_copy(v, low.at[j], sems.at[j]) for j, v in enumerate(heads)]
    for copy in copies:
        copy.start()
    for copy in copies:
        copy.wait()
    wide[...] = low[...].astype(f32).astype(i32)
    copy = pltpu.make_async_copy(wide.at[:, pl.ds(0, 8)], words, sems.at[0])
    copy.start()
    copy.wait()
    for group in range(3):
        out[group * LIST] = 0

    def master(slot, dx, r):
        in_dom = slot < 66
        q = jnp.clip(slot - 2, 0, 63)
        dz = ((q >> 3) - z) & 7
        to_x = (((q >> 1) & 3) - x) & 3
        same = ((q & 1) ^ core)
        me = z * 8 + ((x + dx) & 3) * 2 + (core ^ r)
        v = jnp.clip(slot - 66, 0, 7)
        dy = ((v >> 1) - y) & 3
        word = jnp.where(
            in_dom,
            words[dz, to_x >> 1, ((to_x & 1) * 2 + same) * 64 + me],
            words[jnp.where(dy == 0, 0, 11 - dy), 2, (dx * 2 + r) * 8 + y * 2 + (v & 1)],
        )
        k = word & 1
        dz = jnp.where(in_dom, dz, 0)
        to_x = jnp.where(in_dom, to_x, dx)
        same = jnp.where(in_dom, same, r)
        dy = jnp.where(in_dom, 0, dy)
        return word >= 2, dy, dz, to_x, same, k

    def accumulator(slot, dx, r):
        live, dy, dz, to_x, same, k = master(slot, dx, r)
        own = slot < 2
        live = jnp.logical_or(own, live)
        dy, dz = jnp.where(own, 0, dy), jnp.where(own, 0, dz)
        to_x, same = jnp.where(own, dx, to_x), jnp.where(own, r, same)
        k = jnp.where(own, slot, k)
        a = jnp.where(to_x == 0, 136, jnp.where(to_x == 2, 0, 32 + 8 * to_x)) + dz * 2
        middle = jnp.where(dz == 4, 16, 72 + 4 * (dz - 3))
        outer = jnp.where(dz < 2, 152 + 8 * dz, jnp.where(dz == 7, 168, 116 + 2 * dz))
        b = jnp.where((dz - 4) * (dz - 4) < 2, middle, outer) + to_x * 2
        c = jnp.where(dy == 2, 24, jnp.where(dy == 1, 88, 104)) + r * 8 + dx * 2
        return live, jnp.where(dy > 0, c, jnp.where(same == 0, a, b)) + k

    def append(live, tile, block, place):
        middle, last = place >= STARTS[1], place >= STARTS[2]
        base = jnp.where(last, 2 * LIST, jnp.where(middle, LIST, 0))
        place = place - jnp.where(last, STARTS[2], jnp.where(middle, STARTS[1], 0))
        n = out[base]
        for j, value in enumerate((tile, block, place)):
            out[base + 1 + ENTRIES * j + n] = value
        out[base] = n + live.astype(i32)

    for r in range(2):

        @pl.loop(0, NT, unroll=4)
        def _(t, r=r):
            live, place = accumulator(row[r * INTS + HS + t], 0, r)
            append(live, (8 + r) * NT + t, 2 * r + row[r * INTS + HT + t], place)

    @pl.loop(0, picked[0])
    def _(i):
        which = picked[1 + i]
        dx, r, t = which >> 5, (which >> 4) & 1, which & 15
        base = (which >> 4) * INTS
        target_live, dy, dz, _, same, k = master(row[base + FT + t], dx, r)
        source_live, place = accumulator(row[base + FS + t], dx, r)
        source = jnp.where(dy > 0, 11 - dy, dz)
        append(jnp.logical_and(target_live, source_live), which, 4 * source + 2 * same + k, place)


def list_tiles(meta, row, picked, store):
    return pl.pallas_call(
        list_kernel,
        out_shape=jax.ShapeDtypeStruct((3 * LIST,), i32),
        in_specs=[SMEM] * 3 + [ANY],
        out_specs=SMEM,
        scratch_shapes=[
            pltpu.VMEM((11, HEAD, HALF), bf16),
            pltpu.VMEM((11, HEAD, HALF), i32),
            pltpu.SMEM((11, 8, HALF), i32),
            pltpu.SemaphoreType.DMA((11,)),
        ],
        compiler_params=pltpu.CompilerParams(vmem_limit_bytes=3 * MIB),
    )(meta, row, picked, store)


bar = lax.optimization_barrier


def tile_product(tile, block):
    return lax.dot_general(tile, block, (((0,), (0,)), ((), ())), preferred_element_type=f32)


def tile_kernel(group, todo, store, *refs):
    parts, base = GROUPS[group], group * LIST
    outs, (acc, tiles, blocks, tile_sems, block_sems, out_sems) = refs[: len(parts)], refs[len(parts) :]
    n = todo[base]

    def held(c):
        return jnp.clip(n - c * SLOTS, 0, SLOTS)

    def start(c):
        def one(j, _):
            i = base + 1 + c * SLOTS + j
            which = todo[i]
            row = TILES + ((which >> 4) << 3) + (which & 7)
            lanes = pl.ds(pl.multiple_of(((which >> 3) & 1) * BLK, BLK), BLK)
            pltpu.make_async_copy(store.at[row, :, lanes], tiles.at[j], tile_sems.at[j]).start()
            pltpu.make_async_copy(store.at[todo[i + ENTRIES]], blocks.at[j], block_sems.at[j]).start()
            return 0

        lax.fori_loop(0, held(c), one, 0)

    def finish(c):
        def one(j, _):
            place = todo[base + 1 + 2 * ENTRIES + c * SLOTS + j]
            pltpu.make_async_copy(store.at[0, :, pl.ds(0, BLK)], tiles.at[j], tile_sems.at[j]).wait()
            pltpu.make_async_copy(store.at[0], blocks.at[j], block_sems.at[j]).wait()
            term = tile_product(tiles[j], blocks[j])
            acc[place] = (acc[place].astype(f32) + term).astype(bf16)
            return 0

        lax.fori_loop(0, held(c), one, 0)

    start(0)

    @pl.loop(0, acc.shape[0])
    def _(b):
        acc[b] = jnp.zeros((BLK, HALF), bf16)

    def step(c, _):
        finish(c)
        start(c + 1)
        return 0

    lax.fori_loop(0, (n + SLOTS - 1) // SLOTS, step, 0)
    copies = [
        pltpu.make_async_copy(acc.at[pl.ds(s, m)], out, out_sems.at[j])
        for j, ((s, m), out) in enumerate(zip(parts, outs))
    ]
    for copy in copies:
        copy.start()
    for copy in copies:
        copy.wait()


def tile_sums(group, todo, store):
    parts, size = GROUPS[group], SIZES[group]
    return pl.pallas_call(
        lambda *refs: tile_kernel(group, *refs),
        out_shape=[jax.ShapeDtypeStruct((m, BLK, HALF), bf16) for _, m in parts],
        in_specs=[SMEM, ANY],
        out_specs=[VMEM if group else HBM] * len(parts),
        scratch_shapes=[
            pltpu.VMEM((size, BLK, HALF), bf16),
            pltpu.VMEM((SLOTS, BLK, BLK), bf16),
            pltpu.VMEM((SLOTS, BLK, HALF), bf16),
            pltpu.SemaphoreType.DMA((SLOTS,)),
            pltpu.SemaphoreType.DMA((SLOTS,)),
            pltpu.SemaphoreType.DMA((len(parts),)),
        ],
        compiler_params=pltpu.CompilerParams(vmem_limit_bytes=11 * MIB),
        cost_estimate=pl.CostEstimate(flops=10**9, bytes_accessed=2 * 10**7, transcendentals=0),
    )(todo, store)


def join_kernel(head, own, sib, out):
    out[:HEAD] = head[...]
    out[HEAD : HEAD + HALF] = own[...]
    out[HEAD + HALF :] = sib[...]


def join_chunk(head, own, sib):
    return pl.pallas_call(
        join_kernel,
        out_shape=jax.ShapeDtypeStruct((HEAD + 2 * HALF, HALF), bf16),
        in_specs=[VMEM] * 3,
        out_specs=VMEM,
        compiler_params=pltpu.CompilerParams(vmem_limit_bytes=4 * MIB),
    )(head, own, sib)


def weight_kernel(meta, grad_pre, feats, neigh, mine, other, source, sums, sems):
    loads = [pltpu.make_async_copy(v, source.at[j], sems.at[j]) for j, v in enumerate((feats, neigh))]
    for load in loads:
        load.start()
    core = meta[0]
    low, high = grad_pre[:, :HALF], grad_pre[:, HALF:]
    for load in loads:
        load.wait()
    stores = []
    for j, (out, from_low) in enumerate(((other, core == 1), (mine, core == 0))):
        part = jnp.where(from_low, low, high)
        bias = jnp.sum(part.astype(f32), axis=0, keepdims=True)
        for g in range(NY):
            cols = source[g // 2, :, (g % 2) * HALF : (g % 2 + 1) * HALF]
            sums[j, g, :, :HALF] = tile_product(cols, part)
            sums[j, g, :, HALF:] = jnp.zeros((HALF, BLK), f32)
            if g == 0:
                sums[j, g, 0:1, HALF:] = bias[:, :BLK]
                sums[j, g, 1:2, HALF:] = bias[:, BLK:]
        stores.append(pltpu.make_async_copy(sums.at[j], out, sems.at[2 + j]))
        stores[-1].start()
    for store in stores:
        store.wait()


def weight_terms(meta, feats, neigh, grad_pre):
    shape = (NY, HALF, HALF + BLK)
    return pl.pallas_call(
        weight_kernel,
        out_shape=[jax.ShapeDtypeStruct(shape, f32)] * 2,
        in_specs=[SMEM, VMEM, HBM, HBM],
        out_specs=[HBM] * 2,
        scratch_shapes=[
            pltpu.VMEM((2, *feats.shape), bf16),
            pltpu.VMEM((2, *shape), f32),
            pltpu.SemaphoreType.DMA((4,)),
        ],
        compiler_params=pltpu.CompilerParams(vmem_limit_bytes=8 * MIB),
    )(meta, grad_pre, feats, neigh)


def agg_kernel(meta, pre_act, cotan, w_neigh, grad_pre, agg_own, agg_other):
    grad = jnp.where(pre_act[...] > 0, cotan[...], jnp.zeros_like(cotan))
    grad_pre[...] = grad
    for out, half in ((agg_other, 1 - meta[0]), (agg_own, meta[0])):
        weight = w_neigh[pl.ds(pl.multiple_of(half * HALF, HALF), HALF), :]
        product = lax.dot_general(grad, weight, (((1,), (1,)), ((), ())), preferred_element_type=f32)
        out[...] = product.astype(bf16)


def agg_terms(meta, pre_act, cotan, w_neigh):
    half = jax.ShapeDtypeStruct((HALF, HALF), bf16)
    return pl.pallas_call(
        agg_kernel,
        out_shape=[jax.ShapeDtypeStruct(pre_act.shape, bf16), half, half],
        in_specs=[SMEM] + [VMEM] * 3,
        out_specs=[VMEM] * 3,
        compiler_params=pltpu.CompilerParams(vmem_limit_bytes=6 * MIB),
    )(meta, pre_act, cotan, w_neigh)


def join_kernel(head, own, sib, out):
    out[:HEAD] = head[...]
    out[HEAD : HEAD + HALF] = own[...]
    out[HEAD + HALF :] = sib[...]


def join_chunk(head, own, sib):
    return pl.pallas_call(
        join_kernel,
        out_shape=jax.ShapeDtypeStruct((HEAD + 2 * HALF, HALF), bf16),
        in_specs=[VMEM] * 3,
        out_specs=VMEM,
        compiler_params=pltpu.CompilerParams(vmem_limit_bytes=4 * MIB),
    )(head, own, sib)


def weight_kernel(meta, feats, neigh, grad_pre, mine, other):
    core = meta[0]
    low, high = grad_pre[:, :HALF], grad_pre[:, HALF:]
    for out, from_low in ((mine, core == 0), (other, core == 1)):
        part = jnp.where(from_low, low, high)
        bias = jnp.sum(part.astype(f32), axis=0, keepdims=True)
        for g in range(NY):
            source = feats if g < 2 else neigh
            cols = source[:, (g % 2) * HALF : (g % 2 + 1) * HALF]
            out[g, :, :HALF] = tile_product(cols, part)
            out[g, :, HALF:] = jnp.zeros((HALF, BLK), f32)
            if g == 0:
                out[g, 0:1, HALF:] = bias[:, :BLK]
                out[g, 1:2, HALF:] = bias[:, BLK:]


def weight_terms(meta, feats, neigh, grad_pre):
    return pl.pallas_call(
        weight_kernel,
        out_shape=[jax.ShapeDtypeStruct((NY, HALF, HALF + BLK), f32)] * 2,
        in_specs=[SMEM] + [VMEM] * 3,
        out_specs=[VMEM] * 2,
        compiler_params=pltpu.CompilerParams(vmem_limit_bytes=10 * MIB),
    )(meta, feats, neigh, grad_pre)


def scalars(kernel, sizes, *args):
    return pl.pallas_call(
        kernel,
        out_shape=[jax.ShapeDtypeStruct((n,), i32) for n in sizes],
        in_specs=[SMEM] * len(args),
        out_specs=[SMEM] * len(sizes),
        compiler_params=pltpu.CompilerParams(vmem_limit_bytes=3 * MIB),
    )(*args)


def add(*terms):
    total = terms[0].astype(f32)
    for term in terms[1:]:
        total = total + term.astype(f32)
    return total


def add_head(value, head):
    n = head.shape[0]
    return jnp.concatenate([add(value[:n], head).astype(bf16), value[n:].astype(bf16)])


def add_tail(value, tail):
    n = value.shape[0] - tail.shape[0]
    return jnp.concatenate([value[:n].astype(bf16), add(value[n:], tail).astype(bf16)])


def return_sums(first, sums_of, weights, join_weights):
    a2h, a2t, b4h, b4t, y2h, y2t = first
    w = next(weights)
    b4h, b4t, a2h, a2t, y2h, y2t, (a1, a3, b3, b5, y1, y3, b2, b6) = sums_of(1, (b4h, b4t, a2h, a2t, y2h, y2t))
    up, down = shift(b4h, "z", 1), shift(b4t, "z", -1)
    ax_p, ax_m = shift(a2h, "x", 1), shift(a2t, "x", -1)
    y_p = shift(y2h, "group", 1)

    up, down, ax_p, ax_m, y_p, y2t, a1, a3, b3, b5, w = bar((up, down, ax_p, ax_m, y_p, y2t, a1, a3, b3, b5, w))
    up, down = add_head(b3, up), add_tail(b5, down)
    up, down, ax_p, ax_m, y2t, w = bar((up, down, ax_p, ax_m, y2t, w))
    w = weights.send(w)
    up, down = shift(up, "z", 1), shift(down, "z", -1)
    ax_p, ax_m = shift(add_head(a1, ax_p), "x", 1), shift(add_tail(a3, ax_m), "x", -1)
    y_m = shift(y2t, "group", -1)

    up, down, y_p, y_m, (a0, b0, b1, b7) = sums_of(2, (up, down, y_p, y_m))
    up, down = add(b2, up).astype(bf16), add(b6, down).astype(bf16)
    up, down = shift(up, "z", 1), shift(down, "z", -1)
    y_p = shift(add_head(y1, y_p), "group", 1)

    def part_a(dz):
        rows = slice(2 * dz, 2 * dz + 2)
        return add(a0[rows], ax_p[rows], ax_m[rows])

    def part_b(dx):
        rows = slice(2 * dx, 2 * dx + 2)
        cross = slice(8 + 2 * dx, 10 + 2 * dx)
        sums = add(b0[rows], up[rows], down[rows], y_p[cross], y_m[cross])
        return jnp.concatenate([sums, add(y_p[rows], y_m[rows])])

    up, down, ax_p, ax_m, y_m, a0, b1, b7 = bar((up, down, ax_p, ax_m, y_m, a0, b1, b7))
    far = part_a(4).astype(bf16)
    up, down = add(b1, up).astype(bf16), add(b7, down).astype(bf16)
    far, up, down, y_m = bar((far, up, down, y_m))
    az_p, az_m = shift(far[:1], "z", 1), shift(far[1:], "z", -1)
    up, down = shift(up, "z", 1), shift(down, "z", -1)
    y_m = shift(add_tail(y3, y_m), "group", -1)
    az_p, az_m, w = bar((az_p, az_m, w))
    w = weights.send(w)
    az_p, az_m = add_head(part_a(3), az_p), add_tail(part_a(5), az_m)
    az_p, az_m = shift(az_p, "z", 1), shift(az_m, "z", -1)
    az_p, az_m = add(part_a(2), az_p).astype(bf16), add(part_a(6), az_m).astype(bf16)
    far = part_b(2).astype(bf16)
    az_p, az_m, far = bar((az_p, az_m, far))
    bx_p, bx_m = shift(far[:2], "x", 1), shift(far[2:], "x", -1)
    az_p, az_m = shift(az_p, "z", 1), shift(az_m, "z", -1)
    bx_p, bx_m = add_head(part_b(1), bx_p), add_tail(part_b(3), bx_m)
    az_p, az_m = add(part_a(1), az_p).astype(bf16), add(part_a(7), az_m).astype(bf16)
    az_p, az_m, bx_p, bx_m, w = bar((az_p, az_m, bx_p, bx_m, w))
    w_sib = shift(w, "core", 1)
    bx_p, bx_m = shift(bx_p, "x", 1), shift(bx_m, "x", -1)
    az_p, az_m = shift(az_p, "z", 1), shift(az_m, "z", -1)
    joined = join_weights(w, w_sib)
    az_p, az_m, bx_p, bx_m, *joined = bar((az_p, az_m, bx_p, bx_m, *joined))
    sum_b = add(part_b(0), bx_p, bx_m)
    return add(part_a(0), az_p, az_m, sum_b[2:]), sum_b[:2], joined


def body(
    feats,
    neigh,
    pre_act,
    cotan,
    w_self,
    w_neigh,
    send_list,
    send_live,
    cross_list,
    cross_live,
    home_tiles,
    home_target,
    home_source,
    far_tiles,
    far_target,
    far_source,
    far_count,
):
    y, z, x, core = (lax.axis_index(name) for name in AXES)
    meta = jnp.stack([core, z, x, y]).astype(i32)
    first_core = core == 0
    cols = (((1,), (1,)), ((), ()))
    ints = jnp.concatenate(
        [
            (send_live * 2 + send_list).reshape(-1),
            (cross_live * 2 + cross_list).reshape(-1),
            home_target[0, 0],
            home_source[0, 0],
            far_target[0, 0],
            far_source[0, 0],
            far_count[0],
            jnp.zeros((INTS - FC - 1,), i32),
        ]
    )
    row = jnp.stack([ints, shift(ints, "x", -1), shift(ints, "x", 2), shift(ints, "x", 1)])
    row = jnp.stack([row, shift(row, "core", 1)], axis=1)
    words = row[:, :, :CROSS].reshape(2, HALF).astype(bf16)
    cross_words = jnp.pad(row[:, :, CROSS:HT].reshape(1, BLK // 2).astype(bf16), ((0, 0), (0, HALF - BLK // 2)))
    row = row.reshape(-1)

    def join(mine, other):
        low, high = jnp.where(first_core, mine, other), jnp.where(first_core, other, mine)
        return jnp.concatenate([low, high], axis=-1)

    grad_pre = jnp.where(pre_act > 0, cotan, jnp.zeros_like(cotan))
    wn_mine = lax.dynamic_slice_in_dim(w_neigh, core * HALF, HALF)
    wn_other = lax.dynamic_slice_in_dim(w_neigh, (1 - core) * HALF, HALF)
    agg_other = lax.dot_general(grad_pre, wn_other, cols, preferred_element_type=f32).astype(bf16)
    agg_sib = shift(agg_other, "core", 1)
    agg_own = lax.dot_general(grad_pre, wn_mine, cols, preferred_element_type=f32).astype(bf16)
    head = jnp.concatenate([words, cross_words, jnp.zeros((HEAD - 3, HALF), bf16)])
    chunk = join_chunk(head, agg_own, agg_sib)

    far_own, home_own = far_tiles[0, 0], home_tiles[0, 0]
    mine, other = weight_terms(meta, feats, neigh, grad_pre)

    far_sib, home_sib = shift(far_own, "core", 1), shift(home_own, "core", 1)
    chunk, far_sib, home_sib, mine, other = bar((chunk, far_sib, home_sib, mine, other))
    up1, dn1 = shift(chunk, "z", 1), shift(chunk, "z", -1)
    own3, own1 = shift(far_own, "x", 1), shift(far_own, "x", -1)
    other = shift(other, "core", 1)
    store = deposit(None, chunk0=chunk, tiles0=far_own, tiles1=far_sib, tiles8=home_own, tiles9=home_sib)
    up1, dn1, own1, own3, chunk, row, mine, other, far_sib, store = bar(
        (up1, dn1, own1, own3, chunk, row, mine, other, far_sib, store)
    )
    store = deposit(store, chunk7=up1, chunk1=dn1, tiles2=own1, tiles6=own3)
    weights = (mine + other).reshape(4 * HALF, HALF + BLK)
    weights = lax.psum_scatter(weights, "group", scatter_dimension=0, tiled=True)
    up2, dn2 = shift(up1, "z", 1), shift(dn1, "z", -1)
    sib3, sib1 = shift(far_sib, "x", 1), shift(far_sib, "x", -1)
    y1 = shift(chunk, "group", 1)
    (picked,) = scalars(pick_kernel, (PICKED,), meta, row)
    up2, dn2, sib1, sib3, own3, y1, chunk, picked, store = bar((up2, dn2, sib1, sib3, own3, y1, chunk, picked, store))
    store = deposit(store, chunk6=up2, chunk2=dn2, tiles3=sib1, tiles7=sib3, chunk8=y1)
    up3, dn3 = shift(up2, "z", 1), shift(dn2, "z", -1)
    own2, sib2 = shift(own3, "x", 1), shift(sib1, "x", -1)
    y3 = shift(chunk, "group", 3)
    up3, dn3, own2, sib2, y3, chunk, weights, store = bar((up3, dn3, own2, sib2, y3, chunk, weights, store))
    store = deposit(store, chunk5=up3, chunk3=dn3, tiles4=own2, tiles5=sib2, chunk10=y3)
    weights = lax.psum_scatter(weights, "z", scatter_dimension=0, tiled=True)
    middle = HEAD + 2 * BLK
    up4, dn4 = shift(up3[:middle], "z", 1), shift(dn3[middle:], "z", -1)
    y2 = shift(chunk, "group", 2)
    up4, dn4, y2, store = bar((up4, dn4, y2, store))
    store = deposit(store, chunk4=up4, tail4=dn4, chunk9=y2)
    todo = list_tiles(meta, row, picked, store)

    def weight_stages(w):
        w = yield w
        w = jnp.pad(w, ((0, 16), (0, 0)))
        w = yield lax.all_gather(w, ("group", "x"), axis=0)
        w = jnp.sum(w.reshape(NY, NX, 48, HALF + BLK)[:, :, :32], axis=1)
        yield lax.all_gather(w, "z", axis=0)

    def sums_of(group, arrived):
        *arrived, now = bar((*arrived, todo))
        return *arrived, tile_sums(group, now, store)

    (first,) = sums_of(0, ())
    def rows_of(value):
        return value.transpose(1, 0, 2, 3).reshape(4 * HALF, HALF + BLK)

    def join_weights(mine, other):
        mine, other = rows_of(mine), rows_of(other)
        sums = join(mine[:, :HALF], other[:, :HALF])
        return sums[:512], sums[512:], join(mine[:2, HALF:].reshape(-1), other[:2, HALF:].reshape(-1))

    sum_a, sum_b, joined = return_sums(first, sums_of, weight_stages(weights), join_weights)
    self_grad = lax.dot_general(grad_pre, w_self, cols, preferred_element_type=f32)
    other = shift(sum_b, "core", 1)
    grad_input = self_grad + join(sum_a.reshape(2 * BLK, HALF), other.reshape(2 * BLK, HALF))
    return grad_input.astype(bf16), *joined


def solution(mesh):
    fine = Mesh(mesh.devices.reshape(NY, NZ, NX, 2), AXES)
    rows = P(AXES, None)
    part = lambda extra: P("group", DOM, *([None] * extra))
    return jax.shard_map(
        body,
        mesh=fine,
        in_specs=(rows,) * 4
        + (P(), P())
        + (part(1), part(1), part(2), part(2), part(3), part(1), part(1), part(3), part(1), part(1), part(0)),
        out_specs=(rows, P(), P(), P()),
        check_vma=False,
    )
```

```python
import jax
import jax.numpy as jnp
from jax import lax
from jax.experimental import pallas as pl
from jax.experimental.pallas import tpu as pltpu
from jax.sharding import Mesh
from jax.sharding import PartitionSpec as P

AXES = ("group", "z", "x", "core")
DOM = ("z", "x", "core")
NY, NZ, NX = 4, 8, 4
BLK, HALF = 128, 256
NT = 16
SLOTS = 32
bf16, f32, i32 = jnp.bfloat16, jnp.float32, jnp.int32

SEND, CROSS, HT, HS, FT, FS, FC, INTS = 0, 64, 72, 88, 104, 120, 136, 256
HEAD = 16
ENTRIES = 161
LIST = 1 + 3 * ENTRIES
HEADS, TILES, STORE = 48, 64, 1024
PICKED = 1 + 128

GROUPS = (
    ((0, 8), (8, 8), (16, 4), (20, 4), (24, 8), (32, 8)),
    ((0, 16), (16, 16), (32, 8), (40, 8), (48, 16), (64, 16), (80, 8), (88, 8)),
    ((0, 16), (16, 8), (24, 8), (32, 8)),
)
STARTS, SIZES = (0, 40, 136), (40, 96, 40)
MIB = 2**20

VMEM = pl.BlockSpec(memory_space=pltpu.VMEM)
SMEM = pl.BlockSpec(memory_space=pltpu.SMEM)
ANY = pl.BlockSpec(memory_space=pl.ANY)
HBM = pl.BlockSpec(memory_space=pltpu.HBM)


def shift(value, axis, k):
    n = {"group": NY, "z": NZ, "x": NX, "core": 2}[axis]
    return lax.ppermute(value, axis, [(i, (i + k) % n) for i in range(n)])


def pick_kernel(meta, row, out):
    x = meta[2]
    out[0] = 0
    for dx in range(NX):
        for r in range(2):
            base = (dx * 2 + r) * INTS

            @pl.loop(0, jnp.minimum(row[base + FC], NT))
            def _(t, dx=dx, r=r, base=base):
                slot = row[base + FT + t]
                column = ((slot - 2) >> 1) & 3
                here = jnp.where(slot < 66, column == x, dx == 0)

                @pl.when(here)
                def _():
                    n = out[0]
                    out[0] = n + 1
                    out[1 + n] = (dx * 2 + r) * NT + t


def deposit_kernel(plan, *refs):
    sources, (store, staged, sems) = refs[: len(plan)], refs[-3:]
    copies = []

    def copy(source, target):
        copies.append(pltpu.make_async_copy(source, target, sems.at[len(copies)]))
        copies[-1].start()

    loads = {}
    for source, (kind, i) in zip(sources, plan):
        if kind == "tiles":
            loads[i] = pltpu.make_async_copy(source, staged.at[len(loads)], sems.at[5 * len(plan) + len(loads)])
            loads[i].start()
    slots = {i: j for j, i in enumerate(loads)}
    for source, (kind, i) in sorted(zip(sources, plan), key=lambda pair: pair[1][0]):
        if kind == "tiles":
            loads[i].wait()
            source = staged.at[slots[i]]
            for half in range(2):
                lanes = pl.ds(half * BLK, BLK)
                copy(source.at[pl.ds(8 * half, 8)], store.at[pl.ds(TILES + 8 * i, 8), :, lanes])
            continue
        start, first = (0, 2) if kind == "tail" else (HEAD, 0)
        if kind != "tail":
            copy(source.at[pl.ds(0, HEAD)], store.at[HEADS + i, pl.ds(0, HEAD)])
        for j in range((source.shape[0] - start) // BLK):
            copy(source.at[pl.ds(start + BLK * j, BLK)], store.at[4 * i + first + j])
    for c in copies:
        c.wait()


def deposit(store, **arrived):
    plan = [(name.rstrip("0123456789"), int(name.strip("abcdefghijklmnopqrstuvwxyz"))) for name in arrived]
    old = [] if store is None else [store]
    return pl.pallas_call(
        lambda *refs: deposit_kernel(plan, *refs),
        out_shape=jax.ShapeDtypeStruct((STORE, BLK, HALF), bf16),
        in_specs=[ANY] * (len(plan) + len(old)),
        out_specs=ANY,
        input_output_aliases={len(plan): 0} if old else {},
        scratch_shapes=[
            pltpu.VMEM((4, NT, BLK, BLK), bf16),
            pltpu.SemaphoreType.DMA((5 * len(plan) + 4,)),
        ],
        compiler_params=pltpu.CompilerParams(vmem_limit_bytes=4 * MIB),
    )(*arrived.values(), *old)


def list_kernel(meta, row, picked, store, out, low, wide, words, sems):
    core, z, x, y = (meta[j] for j in range(4))
    heads = [store.at[HEADS + j, pl.ds(0, HEAD)] for j in range(11)]
    copies = [pltpu.make_async_copy(v, low.at[j], sems.at[j]) for j, v in enumerate(heads)]
    for copy in copies:
        copy.start()
    for copy in copies:
        copy.wait()
    wide[...] = low[...].astype(f32).astype(i32)
    copy = pltpu.make_async_copy(wide.at[:, pl.ds(0, 8)], words, sems.at[0])
    copy.start()
    copy.wait()
    for group in range(3):
        out[group * LIST] = 0

    def master(slot, dx, r):
        in_dom = slot < 66
        q = jnp.clip(slot - 2, 0, 63)
        dz = ((q >> 3) - z) & 7
        to_x = (((q >> 1) & 3) - x) & 3
        same = ((q & 1) ^ core)
        me = z * 8 + ((x + dx) & 3) * 2 + (core ^ r)
        v = jnp.clip(slot - 66, 0, 7)
        dy = ((v >> 1) - y) & 3
        word = jnp.where(
            in_dom,
            words[dz, to_x >> 1, ((to_x & 1) * 2 + same) * 64 + me],
            words[jnp.where(dy == 0, 0, 11 - dy), 2, (dx * 2 + r) * 8 + y * 2 + (v & 1)],
        )
        k = word & 1
        dz = jnp.where(in_dom, dz, 0)
        to_x = jnp.where(in_dom, to_x, dx)
        same = jnp.where(in_dom, same, r)
        dy = jnp.where(in_dom, 0, dy)
        return word >= 2, dy, dz, to_x, same, k

    def accumulator(slot, dx, r):
        live, dy, dz, to_x, same, k = master(slot, dx, r)
        own = slot < 2
        live = jnp.logical_or(own, live)
        dy, dz = jnp.where(own, 0, dy), jnp.where(own, 0, dz)
        to_x, same = jnp.where(own, dx, to_x), jnp.where(own, r, same)
        k = jnp.where(own, slot, k)
        a = jnp.where(to_x == 0, 136, jnp.where(to_x == 2, 0, 32 + 8 * to_x)) + dz * 2
        middle = jnp.where(dz == 4, 16, 72 + 4 * (dz - 3))
        outer = jnp.where(dz < 2, 152 + 8 * dz, jnp.where(dz == 7, 168, 116 + 2 * dz))
        b = jnp.where((dz - 4) * (dz - 4) < 2, middle, outer) + to_x * 2
        c = jnp.where(dy == 2, 24, jnp.where(dy == 1, 88, 104)) + r * 8 + dx * 2
        return live, jnp.where(dy > 0, c, jnp.where(same == 0, a, b)) + k

    def append(live, tile, block, place):
        middle, last = place >= STARTS[1], place >= STARTS[2]
        base = jnp.where(last, 2 * LIST, jnp.where(middle, LIST, 0))
        place = place - jnp.where(last, STARTS[2], jnp.where(middle, STARTS[1], 0))
        n = out[base]
        for j, value in enumerate((tile, block, place)):
            out[base + 1 + ENTRIES * j + n] = value
        out[base] = n + live.astype(i32)

    for r in range(2):

        @pl.loop(0, NT, unroll=4)
        def _(t, r=r):
            live, place = accumulator(row[r * INTS + HS + t], 0, r)
            append(live, (8 + r) * NT + t, 2 * r + row[r * INTS + HT + t], place)

    @pl.loop(0, picked[0])
    def _(i):
        which = picked[1 + i]
        dx, r, t = which >> 5, (which >> 4) & 1, which & 15
        base = (which >> 4) * INTS
        target_live, dy, dz, _, same, k = master(row[base + FT + t], dx, r)
        source_live, place = accumulator(row[base + FS + t], dx, r)
        source = jnp.where(dy > 0, 11 - dy, dz)
        append(jnp.logical_and(target_live, source_live), which, 4 * source + 2 * same + k, place)


def list_tiles(meta, row, picked, store):
    return pl.pallas_call(
        list_kernel,
        out_shape=jax.ShapeDtypeStruct((3 * LIST,), i32),
        in_specs=[SMEM] * 3 + [ANY],
        out_specs=SMEM,
        scratch_shapes=[
            pltpu.VMEM((11, HEAD, HALF), bf16),
            pltpu.VMEM((11, HEAD, HALF), i32),
            pltpu.SMEM((11, 8, HALF), i32),
            pltpu.SemaphoreType.DMA((11,)),
        ],
        compiler_params=pltpu.CompilerParams(vmem_limit_bytes=3 * MIB),
    )(meta, row, picked, store)


bar = lax.optimization_barrier


def tile_product(tile, block):
    return lax.dot_general(tile, block, (((0,), (0,)), ((), ())), preferred_element_type=f32)


def tile_kernel(group, todo, store, *refs):
    parts, base = GROUPS[group], group * LIST
    outs, (acc, tiles, blocks, tile_sems, block_sems, out_sems) = refs[: len(parts)], refs[len(parts) :]
    n = todo[base]

    def held(c):
        return jnp.clip(n - c * SLOTS, 0, SLOTS)

    def start(c):
        def one(j, _):
            i = base + 1 + c * SLOTS + j
            which = todo[i]
            row = TILES + ((which >> 4) << 3) + (which & 7)
            lanes = pl.ds(pl.multiple_of(((which >> 3) & 1) * BLK, BLK), BLK)
            pltpu.make_async_copy(store.at[row, :, lanes], tiles.at[j], tile_sems.at[j]).start()
            pltpu.make_async_copy(store.at[todo[i + ENTRIES]], blocks.at[j], block_sems.at[j]).start()
            return 0

        lax.fori_loop(0, held(c), one, 0)

    def finish(c):
        def one(j, _):
            place = todo[base + 1 + 2 * ENTRIES + c * SLOTS + j]
            pltpu.make_async_copy(store.at[0, :, pl.ds(0, BLK)], tiles.at[j], tile_sems.at[j]).wait()
            pltpu.make_async_copy(store.at[0], blocks.at[j], block_sems.at[j]).wait()
            term = tile_product(tiles[j], blocks[j])
            acc[place] = (acc[place].astype(f32) + term).astype(bf16)
            return 0

        lax.fori_loop(0, held(c), one, 0)

    start(0)

    @pl.loop(0, acc.shape[0])
    def _(b):
        acc[b] = jnp.zeros((BLK, HALF), bf16)

    def step(c, _):
        finish(c)
        start(c + 1)
        return 0

    lax.fori_loop(0, (n + SLOTS - 1) // SLOTS, step, 0)
    copies = [
        pltpu.make_async_copy(acc.at[pl.ds(s, m)], out, out_sems.at[j])
        for j, ((s, m), out) in enumerate(zip(parts, outs))
    ]
    for copy in copies:
        copy.start()
    for copy in copies:
        copy.wait()


def tile_sums(group, todo, store):
    parts, size = GROUPS[group], SIZES[group]
    return pl.pallas_call(
        lambda *refs: tile_kernel(group, *refs),
        out_shape=[jax.ShapeDtypeStruct((m, BLK, HALF), bf16) for _, m in parts],
        in_specs=[SMEM, ANY],
        out_specs=[VMEM if group else HBM] * len(parts),
        scratch_shapes=[
            pltpu.VMEM((size, BLK, HALF), bf16),
            pltpu.VMEM((SLOTS, BLK, BLK), bf16),
            pltpu.VMEM((SLOTS, BLK, HALF), bf16),
            pltpu.SemaphoreType.DMA((SLOTS,)),
            pltpu.SemaphoreType.DMA((SLOTS,)),
            pltpu.SemaphoreType.DMA((len(parts),)),
        ],
        compiler_params=pltpu.CompilerParams(vmem_limit_bytes=11 * MIB),
        cost_estimate=pl.CostEstimate(flops=10**9, bytes_accessed=2 * 10**7, transcendentals=0),
    )(todo, store)


def join_kernel(head, own, sib, out):
    out[:HEAD] = head[...]
    out[HEAD : HEAD + HALF] = own[...]
    out[HEAD + HALF :] = sib[...]


def join_chunk(head, own, sib):
    return pl.pallas_call(
        join_kernel,
        out_shape=jax.ShapeDtypeStruct((HEAD + 2 * HALF, HALF), bf16),
        in_specs=[VMEM] * 3,
        out_specs=VMEM,
        compiler_params=pltpu.CompilerParams(vmem_limit_bytes=4 * MIB),
    )(head, own, sib)


def weight_kernel(meta, grad_pre, feats, neigh, mine, other, source, sums, sems):
    loads = [pltpu.make_async_copy(v, source.at[j], sems.at[j]) for j, v in enumerate((feats, neigh))]
    for load in loads:
        load.start()
    core = meta[0]
    low, high = grad_pre[:, :HALF], grad_pre[:, HALF:]
    for load in loads:
        load.wait()
    stores = []
    for j, (out, from_low) in enumerate(((other, core == 1), (mine, core == 0))):
        part = jnp.where(from_low, low, high)
        bias = jnp.sum(part.astype(f32), axis=0, keepdims=True)
        for g in range(NY):
            cols = source[g // 2, :, (g % 2) * HALF : (g % 2 + 1) * HALF]
            sums[j, g, :, :HALF] = tile_product(cols, part)
            sums[j, g, :, HALF:] = jnp.zeros((HALF, BLK), f32)
            if g == 0:
                sums[j, g, 0:1, HALF:] = bias[:, :BLK]
                sums[j, g, 1:2, HALF:] = bias[:, BLK:]
        stores.append(pltpu.make_async_copy(sums.at[j], out, sems.at[2 + j]))
        stores[-1].start()
    for store in stores:
        store.wait()


def weight_terms(meta, feats, neigh, grad_pre):
    shape = (NY, HALF, HALF + BLK)
    return pl.pallas_call(
        weight_kernel,
        out_shape=[jax.ShapeDtypeStruct(shape, f32)] * 2,
        in_specs=[SMEM, VMEM, HBM, HBM],
        out_specs=[HBM] * 2,
        scratch_shapes=[
            pltpu.VMEM((2, *feats.shape), bf16),
            pltpu.VMEM((2, *shape), f32),
            pltpu.SemaphoreType.DMA((4,)),
        ],
        compiler_params=pltpu.CompilerParams(vmem_limit_bytes=8 * MIB),
    )(meta, grad_pre, feats, neigh)


def agg_kernel(meta, pre_act, cotan, w_neigh, grad_pre, agg_own, agg_other):
    grad = jnp.where(pre_act[...] > 0, cotan[...], jnp.zeros_like(cotan))
    grad_pre[...] = grad
    for out, half in ((agg_other, 1 - meta[0]), (agg_own, meta[0])):
        weight = w_neigh[pl.ds(pl.multiple_of(half * HALF, HALF), HALF), :]
        product = lax.dot_general(grad, weight, (((1,), (1,)), ((), ())), preferred_element_type=f32)
        out[...] = product.astype(bf16)


def agg_terms(meta, pre_act, cotan, w_neigh):
    half = jax.ShapeDtypeStruct((HALF, HALF), bf16)
    return pl.pallas_call(
        agg_kernel,
        out_shape=[jax.ShapeDtypeStruct(pre_act.shape, bf16), half, half],
        in_specs=[SMEM] + [VMEM] * 3,
        out_specs=[VMEM] * 3,
        compiler_params=pltpu.CompilerParams(vmem_limit_bytes=6 * MIB),
    )(meta, pre_act, cotan, w_neigh)


def join_kernel(head, own, sib, out):
    out[:HEAD] = head[...]
    out[HEAD : HEAD + HALF] = own[...]
    out[HEAD + HALF :] = sib[...]


def join_chunk(head, own, sib):
    return pl.pallas_call(
        join_kernel,
        out_shape=jax.ShapeDtypeStruct((HEAD + 2 * HALF, HALF), bf16),
        in_specs=[VMEM] * 3,
        out_specs=VMEM,
        compiler_params=pltpu.CompilerParams(vmem_limit_bytes=4 * MIB),
    )(head, own, sib)


def weight_kernel(meta, feats, neigh, grad_pre, mine, other):
    core = meta[0]
    low, high = grad_pre[:, :HALF], grad_pre[:, HALF:]
    for out, from_low in ((mine, core == 0), (other, core == 1)):
        part = jnp.where(from_low, low, high)
        bias = jnp.sum(part.astype(f32), axis=0, keepdims=True)
        for g in range(NY):
            source = feats if g < 2 else neigh
            cols = source[:, (g % 2) * HALF : (g % 2 + 1) * HALF]
            out[g, :, :HALF] = tile_product(cols, part)
            out[g, :, HALF:] = jnp.zeros((HALF, BLK), f32)
            if g == 0:
                out[g, 0:1, HALF:] = bias[:, :BLK]
                out[g, 1:2, HALF:] = bias[:, BLK:]


def weight_terms(meta, feats, neigh, grad_pre):
    return pl.pallas_call(
        weight_kernel,
        out_shape=[jax.ShapeDtypeStruct((NY, HALF, HALF + BLK), f32)] * 2,
        in_specs=[SMEM] + [VMEM] * 3,
        out_specs=[VMEM] * 2,
        compiler_params=pltpu.CompilerParams(vmem_limit_bytes=10 * MIB),
    )(meta, feats, neigh, grad_pre)


def scalars(kernel, sizes, *args):
    return pl.pallas_call(
        kernel,
        out_shape=[jax.ShapeDtypeStruct((n,), i32) for n in sizes],
        in_specs=[SMEM] * len(args),
        out_specs=[SMEM] * len(sizes),
        compiler_params=pltpu.CompilerParams(vmem_limit_bytes=3 * MIB),
    )(*args)


def add(*terms):
    total = terms[0].astype(f32)
    for term in terms[1:]:
        total = total + term.astype(f32)
    return total


def add_head(value, head):
    n = head.shape[0]
    return jnp.concatenate([add(value[:n], head).astype(bf16), value[n:].astype(bf16)])


def add_tail(value, tail):
    n = value.shape[0] - tail.shape[0]
    return jnp.concatenate([value[:n].astype(bf16), add(value[n:], tail).astype(bf16)])


def return_sums(first, sums_of, weights, join_weights):
    a2h, a2t, b4h, b4t, y2h, y2t = first
    w = next(weights)
    b4h, b4t, a2h, a2t, y2h, y2t, (a1, a3, b3, b5, y1, y3, b2, b6) = sums_of(1, (b4h, b4t, a2h, a2t, y2h, y2t))
    up, down = shift(b4h, "z", 1), shift(b4t, "z", -1)
    ax_p, ax_m = shift(a2h, "x", 1), shift(a2t, "x", -1)
    y_p = shift(y2h, "group", 1)

    up, down, ax_p, ax_m, y_p, y2t, a1, a3, b3, b5, w = bar((up, down, ax_p, ax_m, y_p, y2t, a1, a3, b3, b5, w))
    up, down = add_head(b3, up), add_tail(b5, down)
    up, down, ax_p, ax_m, y2t, w = bar((up, down, ax_p, ax_m, y2t, w))
    w = weights.send(w)
    up, down = shift(up, "z", 1), shift(down, "z", -1)
    ax_p, ax_m = shift(add_head(a1, ax_p), "x", 1), shift(add_tail(a3, ax_m), "x", -1)
    y_m = shift(y2t, "group", -1)

    up, down, y_p, y_m, (a0, b0, b1, b7) = sums_of(2, (up, down, y_p, y_m))
    up, down = add(b2, up).astype(bf16), add(b6, down).astype(bf16)
    up, down = shift(up, "z", 1), shift(down, "z", -1)
    y_p = shift(add_head(y1, y_p), "group", 1)

    def part_a(dz):
        rows = slice(2 * dz, 2 * dz + 2)
        return add(a0[rows], ax_p[rows], ax_m[rows])

    def part_b(dx):
        rows = slice(2 * dx, 2 * dx + 2)
        cross = slice(8 + 2 * dx, 10 + 2 * dx)
        sums = add(b0[rows], up[rows], down[rows], y_p[cross], y_m[cross])
        return jnp.concatenate([sums, add(y_p[rows], y_m[rows])])

    up, down, ax_p, ax_m, y_m, a0, b1, b7 = bar((up, down, ax_p, ax_m, y_m, a0, b1, b7))
    far = part_a(4).astype(bf16)
    up, down = add(b1, up).astype(bf16), add(b7, down).astype(bf16)
    far, up, down, y_m = bar((far, up, down, y_m))
    az_p, az_m = shift(far[:1], "z", 1), shift(far[1:], "z", -1)
    up, down = shift(up, "z", 1), shift(down, "z", -1)
    az_p, az_m, y_m = bar((az_p, az_m, y_m))
    y_m = shift(add_tail(y3, y_m), "group", -1)
    az_p, az_m, up, down, w = bar((az_p, az_m, up, down, w))
    w = weights.send(w)
    az_p, az_m = add_head(part_a(3), az_p), add_tail(part_a(5), az_m)
    az_p, az_m = shift(az_p, "z", 1), shift(az_m, "z", -1)
    az_p, az_m = add(part_a(2), az_p).astype(bf16), add(part_a(6), az_m).astype(bf16)
    far = part_b(2).astype(bf16)
    az_p, az_m, far = bar((az_p, az_m, far))
    bx_p, bx_m = shift(far[:2], "x", 1), shift(far[2:], "x", -1)
    az_p, az_m = shift(az_p, "z", 1), shift(az_m, "z", -1)
    bx_p, bx_m = add_head(part_b(1), bx_p), add_tail(part_b(3), bx_m)
    az_p, az_m = add(part_a(1), az_p).astype(bf16), add(part_a(7), az_m).astype(bf16)
    az_p, az_m, bx_p, bx_m, w = bar((az_p, az_m, bx_p, bx_m, w))
    w_sib = shift(w, "core", 1)
    bx_p, bx_m = shift(bx_p, "x", 1), shift(bx_m, "x", -1)
    az_p, az_m = shift(az_p, "z", 1), shift(az_m, "z", -1)
    joined = join_weights(w, w_sib)
    az_p, az_m, bx_p, bx_m, *joined = bar((az_p, az_m, bx_p, bx_m, *joined))
    sum_b = add(part_b(0), bx_p, bx_m)
    return add(part_a(0), az_p, az_m, sum_b[2:]), sum_b[:2], joined


def body(
    feats,
    neigh,
    pre_act,
    cotan,
    w_self,
    w_neigh,
    send_list,
    send_live,
    cross_list,
    cross_live,
    home_tiles,
    home_target,
    home_source,
    far_tiles,
    far_target,
    far_source,
    far_count,
):
    y, z, x, core = (lax.axis_index(name) for name in AXES)
    meta = jnp.stack([core, z, x, y]).astype(i32)
    first_core = core == 0
    cols = (((1,), (1,)), ((), ()))
    ints = jnp.concatenate(
        [
            (send_live * 2 + send_list).reshape(-1),
            (cross_live * 2 + cross_list).reshape(-1),
            home_target[0, 0],
            home_source[0, 0],
            far_target[0, 0],
            far_source[0, 0],
            far_count[0],
            jnp.zeros((INTS - FC - 1,), i32),
        ]
    )
    row = jnp.stack([ints, shift(ints, "x", -1), shift(ints, "x", 2), shift(ints, "x", 1)])
    row = jnp.stack([row, shift(row, "core", 1)], axis=1)
    words = row[:, :, :CROSS].reshape(2, HALF).astype(bf16)
    cross_words = jnp.pad(row[:, :, CROSS:HT].reshape(1, BLK // 2).astype(bf16), ((0, 0), (0, HALF - BLK // 2)))
    row = row.reshape(-1)

    def join(mine, other):
        low, high = jnp.where(first_core, mine, other), jnp.where(first_core, other, mine)
        return jnp.concatenate([low, high], axis=-1)

    grad_pre = jnp.where(pre_act > 0, cotan, jnp.zeros_like(cotan))
    wn_mine = lax.dynamic_slice_in_dim(w_neigh, core * HALF, HALF)
    wn_other = lax.dynamic_slice_in_dim(w_neigh, (1 - core) * HALF, HALF)
    agg_other = lax.dot_general(grad_pre, wn_other, cols, preferred_element_type=f32).astype(bf16)
    agg_sib = shift(agg_other, "core", 1)
    agg_own = lax.dot_general(grad_pre, wn_mine, cols, preferred_element_type=f32).astype(bf16)
    head = jnp.concatenate([words, cross_words, jnp.zeros((HEAD - 3, HALF), bf16)])
    chunk = join_chunk(head, agg_own, agg_sib)

    far_own, home_own = far_tiles[0, 0], home_tiles[0, 0]
    mine, other = weight_terms(meta, feats, neigh, grad_pre)

    far_sib, home_sib = shift(far_own, "core", 1), shift(home_own, "core", 1)
    chunk, far_sib, home_sib, mine, other = bar((chunk, far_sib, home_sib, mine, other))
    up1, dn1 = shift(chunk, "z", 1), shift(chunk, "z", -1)
    own3, own1 = shift(far_own, "x", 1), shift(far_own, "x", -1)
    other = shift(other, "core", 1)
    store = deposit(None, chunk0=chunk, tiles0=far_own, tiles1=far_sib, tiles8=home_own, tiles9=home_sib)
    up1, dn1, own1, own3, chunk, row, mine, other, far_sib, store = bar(
        (up1, dn1, own1, own3, chunk, row, mine, other, far_sib, store)
    )
    store = deposit(store, chunk7=up1, chunk1=dn1, tiles2=own1, tiles6=own3)
    weights = (mine + other).reshape(4 * HALF, HALF + BLK)
    weights = lax.psum_scatter(weights, "group", scatter_dimension=0, tiled=True)
    up2, dn2 = shift(up1, "z", 1), shift(dn1, "z", -1)
    sib3, sib1 = shift(far_sib, "x", 1), shift(far_sib, "x", -1)
    y1 = shift(chunk, "group", 1)
    (picked,) = scalars(pick_kernel, (PICKED,), meta, row)
    up2, dn2, sib1, sib3, own3, y1, chunk, picked, store = bar((up2, dn2, sib1, sib3, own3, y1, chunk, picked, store))
    store = deposit(store, chunk6=up2, chunk2=dn2, tiles3=sib1, tiles7=sib3, chunk8=y1)
    up3, dn3 = shift(up2, "z", 1), shift(dn2, "z", -1)
    own2, sib2 = shift(own3, "x", 1), shift(sib1, "x", -1)
    y3 = shift(chunk, "group", 3)
    up3, dn3, own2, sib2, y3, chunk, weights, store = bar((up3, dn3, own2, sib2, y3, chunk, weights, store))
    store = deposit(store, chunk5=up3, chunk3=dn3, tiles4=own2, tiles5=sib2, chunk10=y3)
    weights = lax.psum_scatter(weights, "z", scatter_dimension=0, tiled=True)
    middle = HEAD + 2 * BLK
    up4, dn4 = shift(up3[:middle], "z", 1), shift(dn3[middle:], "z", -1)
    y2 = shift(chunk, "group", 2)
    up4, dn4, y2, store = bar((up4, dn4, y2, store))
    store = deposit(store, chunk4=up4, tail4=dn4, chunk9=y2)
    todo = list_tiles(meta, row, picked, store)

    def weight_stages(w):
        w = yield w
        w = jnp.pad(w, ((0, 16), (0, 0)))
        w = yield lax.all_gather(w, ("group", "x"), axis=0)
        w = jnp.sum(w.reshape(NY, NX, 48, HALF + BLK)[:, :, :32], axis=1)
        yield lax.all_gather(w, "z", axis=0)

    def sums_of(group, arrived):
        *arrived, now = bar((*arrived, todo))
        return *arrived, tile_sums(group, now, store)

    (first,) = sums_of(0, ())
    def rows_of(value):
        return value.transpose(1, 0, 2, 3).reshape(4 * HALF, HALF + BLK)

    def join_weights(mine, other):
        mine, other = rows_of(mine), rows_of(other)
        sums = join(mine[:, :HALF], other[:, :HALF])
        return sums[:512], sums[512:], join(mine[:2, HALF:].reshape(-1), other[:2, HALF:].reshape(-1))

    sum_a, sum_b, joined = return_sums(first, sums_of, weight_stages(weights), join_weights)
    self_grad = lax.dot_general(grad_pre, w_self, cols, preferred_element_type=f32)
    other = shift(sum_b, "core", 1)
    grad_input = self_grad + join(sum_a.reshape(2 * BLK, HALF), other.reshape(2 * BLK, HALF))
    return grad_input.astype(bf16), *joined


def solution(mesh):
    fine = Mesh(mesh.devices.reshape(NY, NZ, NX, 2), AXES)
    rows = P(AXES, None)
    part = lambda extra: P("group", DOM, *([None] * extra))
    return jax.shard_map(
        body,
        mesh=fine,
        in_specs=(rows,) * 4
        + (P(), P())
        + (part(1), part(1), part(2), part(2), part(3), part(1), part(1), part(3), part(1), part(1), part(0)),
        out_specs=(rows, P(), P(), P()),
        check_vma=False,
    )
```
